128 devices in a mesh: fsdp: 4 (over x), ctx: 4 (over y_lo, core), tp: 8 (over y_hi, z).
Axes of the slice: x: 4, y: 4 (y_hi: 2, y_lo: 2; y = y_hi * 2 + y_lo), z: 4, core: 2. Of those that a mesh axis runs over, the one named last changes fastest.
Arguments:
- tokens: bfloat16 [8, 1024, 2048], P('fsdp', 'ctx'), may hold values from -6 to 6
- block_order: int32 [8], replicated, may hold values from 0 to 7, each once
- cotangent: bfloat16 [8, 1024, 2048], P('fsdp', 'ctx'), may hold values from -6 to 6
- qkv_weight: bfloat16 [2, 2048, 6144], P(None, ('fsdp', 'ctx'), 'tp'), may hold values from -0.125 to 0.125
- qkv_bias: bfloat16 [2, 6144], P(None, 'tp'), may hold values from -1.1953125 to 1.1953125
- dense_weight: bfloat16 [2, 2048, 2048], P(None, ('fsdp', 'ctx'), 'tp'), may hold values from -0.75 to 0.75
- up_weight: bfloat16 [2, 2048, 8192], P(None, ('fsdp', 'ctx'), 'tp'), may hold values from -0.125 to 0.125
- up_bias: bfloat16 [2, 8192], P(None, 'tp'), may hold values from -1.1953125 to 1.1953125
- down_weight: bfloat16 [2, 2048, 8192], P(None, ('fsdp', 'ctx'), 'tp'), may hold values from -0.0625 to 0.0625
- norm_gains: bfloat16 [2, 2, 2048], replicated, may hold values from 0.5 to 1.5
- norm_shifts: bfloat16 [2, 2, 2048], replicated, may hold values from -1.1953125 to 1.1953125
- out_bias: bfloat16 [2, 2048], replicated, may hold values from -1.1953125 to 1.1953125
Outputs:
- activations: float32 [8, 1024, 2048], P('fsdp', 'ctx')
- input_grad: float32 [8, 1024, 2048], P('fsdp', 'ctx')
- qkv_weight_grad: float32 [2, 2048, 6144], P(None, ('fsdp', 'ctx'), 'tp')
- qkv_bias_grad: float32 [2, 6144], P(None, 'tp')
- dense_weight_grad: float32 [2, 2048, 2048], P(None, ('fsdp', 'ctx'), 'tp')
- up_weight_grad: float32 [2, 2048, 8192], P(None, ('fsdp', 'ctx'), 'tp')
- up_bias_grad: float32 [2, 8192], P(None, 'tp')
- down_weight_grad: float32 [2, 2048, 8192], P(None, ('fsdp', 'ctx'), 'tp')
- norm_gains_grad: float32 [2, 2, 2048], replicated
- norm_shifts_grad: float32 [2, 2, 2048], replicated
- out_bias_grad: float32 [2, 2048], replicated
The draws below stay inside these ranges and needn't reach their ends.
Inputs may be any that keep to these rules, and one draw needn't show every extreme that they name: Each of 0 to 2 * 4 - 1 appears once; block slot j of a sequence (rows j * 128 to j * 128 + 127) holds positions block_order[j] * 128 onward, for every sequence.
All inputs are finite; a program needn't handle non-finite values.
Results may differ from the reference program's by a relative error of at most 0.023.
Values may be sent and summed in bfloat16 or wider, within the bound.
No kernel may reach another device: no remote copies, remote signals or barrier semaphores. Data moves between devices by JAX's collectives and lax.ppermute only.
A program may use at most 192 MiB of HBM per device.

```python
import math
from functools import partial
import jax
import jax.numpy as jnp
from jax import lax

D = 2048
HEADS = 8
HD = 256
ROT = 64
FF = 8192
LAYERS = 2
LEN = 1024
BATCH = 8
BLOCK = 128
N_CTX = 4


def shard_levels(stream_key, shape, pieces, smallest, largest):
    def one(dim, shards_of):
        steps = jax.random.uniform(jax.random.fold_in(jax.random.fold_in(stream_key, 6), dim), (shards_of,), jnp.float32, smallest / len(pieces), largest / len(pieces))
        return jnp.repeat(jnp.exp(steps), shape[dim] // shards_of).reshape((-1,) + (1,) * (len(shape) - dim - 1))

    gain = one(*pieces[0])
    for cut in pieces[1:]:
        gain = gain * one(*cut)
    return gain


def scatter_about(key, extent, deviation, reach, pieces=(), held_as=jnp.bfloat16):
    drawn = jax.random.normal(key, extent, jnp.float32) * deviation
    if len(pieces) > 0:
        drawn = shard_levels(key, extent, pieces, -0.22, 0.18) * drawn
    return jnp.clip(drawn, min=-reach, max=reach).astype(held_as)


def setup_inputs(seed: int = 0) -> dict:
    key_of = jax.random.split(jax.random.key(seed), 13)
    tokens = scatter_about(key_of[0], (BATCH, LEN, D), 1.0, 6.0, ((0, 4), (1, 4)))
    block_order = jax.random.permutation(key_of[1], 2 * N_CTX).astype(jnp.int32)
    cotangent = scatter_about(key_of[2], (BATCH, LEN, D), 1.0, 6.0, ((0, 4), (1, 4)))
    qkv_weight = scatter_about(key_of[3], (LAYERS, D, 3 * D), D ** -0.5, 0.125, ((1, 16), (2, 8)))
    qkv_bias = scatter_about(key_of[4], (LAYERS, 3 * D), 0.2, 1.1953125, ((1, 8),))
    dense_weight = scatter_about(key_of[5], (LAYERS, D, D), (D // 32) ** -0.5, 0.75, ((1, 16), (2, 8)))
    up_weight = scatter_about(key_of[6], (LAYERS, D, FF), D ** -0.5, 0.125, ((1, 16), (2, 8)))
    up_bias = scatter_about(key_of[7], (LAYERS, FF), 0.2, 1.1953125, ((1, 8),))
    down_weight = scatter_about(key_of[8], (LAYERS, D, FF), FF ** -0.5, 0.0625, ((1, 16), (2, 8)))
    norm_gains = jnp.clip(1.0 + 0.1 * jax.random.normal(key_of[9], (LAYERS, 2, D), jnp.float32), 0.5, 1.5).astype(jnp.bfloat16)
    norm_shifts = scatter_about(key_of[10], (LAYERS, 2, D), 0.2, 1.1953125)
    out_bias = scatter_about(key_of[11], (LAYERS, D), 0.2, 1.1953125)
    return dict(tokens=tokens, block_order=block_order, cotangent=cotangent, qkv_weight=qkv_weight, qkv_bias=qkv_bias, dense_weight=dense_weight, up_weight=up_weight, up_bias=up_bias, down_weight=down_weight, norm_gains=norm_gains, norm_shifts=norm_shifts, out_bias=out_bias)


@jax.custom_vjp
def low(v):
    return lax.optimization_barrier(v.astype(jnp.bfloat16)).astype(jnp.float32)

@jax.custom_vjp
def low_back(v):
    return v

def low_keep(v):
    return (low(v), None)

def low_pass(kept, grad):
    return (grad,)

def back_keep(v):
    return (v, None)

def back_low(kept, grad):
    return (low(grad),)
low.defvjp(low_keep, low_pass)
low_back.defvjp(back_keep, back_low)
EPSILON = 1e-05
HIGHEST = lax.Precision.HIGHEST

def rotary_tables(positions):
    half_width = ROT // 2
    inverse = 10000.0 ** (-(jnp.arange(half_width, dtype=jnp.float32) * 2.0) / ROT)
    angles = positions.astype(jnp.float32)[:, None] * inverse[None, :]
    return (jnp.cos(angles), jnp.sin(angles))

def rotate(rows_in, cosine, sine_table):
    half_width = ROT // 2
    lead_part = rows_in[..., :half_width]
    pair_part = rows_in[..., half_width:ROT]
    return jnp.concatenate([lead_part * cosine - pair_part * sine_table, pair_part * cosine + lead_part * sine_table, rows_in[..., ROT:]], axis=-1)

def layer_norm(stream, gain_row, shift_row):
    center = stream - lax.optimization_barrier(jnp.mean(stream, axis=-1, keepdims=True))
    spread = lax.optimization_barrier(jnp.mean(center * center, axis=-1, keepdims=True))
    return center * lax.rsqrt(spread + EPSILON) * gain_row + shift_row

def attend(packed, cosine, sine_table, allowed):
    queries = low(rotate(packed[:, :, 0], cosine[:, None, :], sine_table[:, None, :]))
    key_rows = low(rotate(packed[:, :, 1], cosine[:, None, :], sine_table[:, None, :]))
    value_rows = low(packed[:, :, 2])
    scores = low_back(jnp.einsum('qhd,khd->hqk', queries, key_rows, precision=HIGHEST) * HD ** (-0.5))
    masked = jnp.where(allowed[None], scores, -1e+30)
    exponent = jnp.exp(masked - lax.optimization_barrier(jnp.max(masked, axis=-1, keepdims=True)))
    probability = exponent / lax.optimization_barrier(jnp.sum(exponent, axis=-1, keepdims=True))
    mixed_heads = jnp.einsum('hqk,khd->qhd', low(probability), value_rows, precision=HIGHEST)
    return low(low_back(mixed_heads)).reshape(mixed_heads.shape[0], HEADS * HD)

def block_layer(stream, weights, cosine, sine_table, allowed):
    qkv_weight, qkv_bias, dense_weight, up_weight, up_bias, down_weight, norm_gains, norm_shifts, out_bias = weights
    normed_attn = low(layer_norm(stream, norm_gains[0], norm_shifts[0]))
    normed_mlp = low(layer_norm(stream, norm_gains[1], norm_shifts[1]))
    packed = low_back(jnp.einsum('bld,de->ble', normed_attn, qkv_weight, precision=HIGHEST) + qkv_bias)
    packed = packed.reshape(packed.shape[0], packed.shape[1], HEADS, 3, HD)
    attend_one = jax.checkpoint(partial(attend, cosine=cosine, sine_table=sine_table, allowed=allowed))
    mixed_heads = lax.map(attend_one, packed)
    attn_out = jnp.einsum('ble,de->bld', mixed_heads, dense_weight, precision=HIGHEST)
    hidden = low_back(jnp.einsum('bld,df->blf', normed_mlp, up_weight, precision=HIGHEST) + up_bias)
    active = low(jax.nn.gelu(hidden, approximate=False))
    mlp_out = jnp.einsum('blf,df->bld', active, down_weight, precision=HIGHEST)
    return stream + low_back(attn_out + mlp_out) + out_bias

def reference(tokens, block_order, cotangent, qkv_weight, qkv_bias, dense_weight, up_weight, up_bias, down_weight, norm_gains, norm_shifts, out_bias):
    slot_index = jnp.arange(LEN, dtype=jnp.int32)
    positions = block_order[slot_index // BLOCK] * BLOCK + slot_index % BLOCK
    cosine, sine_table = rotary_tables(positions)
    allowed = positions[None, :] <= positions[:, None]
    params = tuple((array.astype(jnp.float32) for array in (qkv_weight, qkv_bias, dense_weight, up_weight, up_bias, down_weight, norm_gains, norm_shifts, out_bias)))

    def forward(stream, weights):
        for index_layer in range(LAYERS):
            stream = block_layer(stream, tuple((array[index_layer] for array in weights)), cosine, sine_table, allowed)
        return stream
    group_size = math.gcd(BATCH, max(1, 4096 // LEN))
    inputs = tokens.astype(jnp.float32).reshape(BATCH // group_size, group_size, LEN, D)
    cotangents = cotangent.astype(jnp.float32).reshape(BATCH // group_size, group_size, LEN, D)

    def advance(totals, batch_pair):
        outputs, pullback = jax.vjp(forward, batch_pair[0], params)
        grad_stream, grad_params = pullback(batch_pair[1])
        return (tuple((total + grad for total, grad in zip(totals, grad_params))), (outputs, grad_stream))
    zeros = tuple((jnp.zeros_like(array) for array in params))
    totals, (outputs, grad_streams) = lax.scan(advance, zeros, (inputs, cotangents))
    return (outputs.reshape(BATCH, LEN, D), grad_streams.reshape(BATCH, LEN, D), totals[0], totals[1], totals[2], totals[3], totals[4], totals[5], totals[6], totals[7], totals[8])
```

```python
import jax
import jax.numpy as jnp
from jax import lax
from jax.experimental import pallas as pl
from jax.experimental.pallas import tpu as pltpu
from jax.sharding import PartitionSpec as P

HD = 256
ROT = 64
LAYERS = 2
EPSILON = 1e-05
LANES = 128
TILE = 256
CHUNK = 32
QKV, DENSE, UP, DOWN = 0, 3, 4, 8
F32 = jnp.float32
BF16 = jnp.bfloat16
VMEM_LIMIT = 18 * 1024 * 1024
COST = 0.1


def swap_core(value):
    return lax.ppermute(value, "ctx", [(i, i ^ 1) for i in range(4)])


def swap_y(value):
    return lax.ppermute(value, "ctx", [(i, i ^ 2) for i in range(4)])


def swap_x(value, k):
    return lax.ppermute(value, "fsdp", [(i, i ^ k) for i in range(4)])


def swap_tp(value, k):
    return lax.ppermute(value, "tp", [(i, i ^ k) for i in range(8)])


def from_z(value, k):
    return lax.ppermute(value, "tp", [((i & 4) + (i + k) % 4, i) for i in range(8)])


def to_z(value, k):
    return lax.ppermute(value, "tp", [(i, (i & 4) + (i + k) % 4) for i in range(8)])


def gather_weights(shard):
    return lax.all_gather(shard, ("fsdp", "ctx"), axis=1, tiled=True)


def total_of(parts):
    total = parts[0].astype(F32)
    for a in parts[1:]:
        total = total + a.astype(F32)
    return total.astype(BF16)


def add(a, b):
    return total_of((a, b))


def together(*values):
    return lax.optimization_barrier(values)


def tp_1(pieces):
    return pieces[0], [to_z(pieces[k], k) for k in (1, 3, 2)]


def tp_2(own, got):
    total = total_of((own, *got))
    return total, swap_tp(total, 4)


def tp_3(total, far):
    total = add(total, far)
    return total, [from_z(total, k) for k in (1, 3, 2)]


def tp_pieces(total, got):
    return (total, got[0], got[2], got[1])


def call(body, grid, ins, in_specs, outs, out_specs, scratch=(), prefetch=0, flops=0):
    nbytes = sum(a.size * a.dtype.itemsize for a in outs)
    nbytes += sum(min(a.size * a.dtype.itemsize, 1 << 22) for a in ins)
    return pl.pallas_call(
        body,
        grid_spec=pltpu.PrefetchScalarGridSpec(
            num_scalar_prefetch=prefetch,
            grid=grid,
            in_specs=in_specs,
            out_specs=out_specs,
            scratch_shapes=scratch,
        ),
        out_shape=outs,
        compiler_params=pltpu.CompilerParams(vmem_limit_bytes=VMEM_LIMIT),
        cost_estimate=pl.CostEstimate(
            flops=int(flops * COST), bytes_accessed=int(nbytes * COST), transcendentals=0
        ),
    )(*ins)


def call_once(body, ins, outs, scratch=(), prefetch=0, hbm=(), out_hbm=False, flops=0):
    ins = tuple(
        pltpu.with_memory_space_constraint(a, pltpu.HBM) if i in hbm else a
        for i, a in enumerate(ins)
    )
    specs = [
        pl.BlockSpec(memory_space=pltpu.HBM) if i in hbm else whole(a)
        for i, a in enumerate(ins)
        if i >= prefetch
    ]
    out_specs = [pl.BlockSpec(memory_space=pltpu.HBM) if out_hbm else whole(a) for a in outs]
    return call(body, (1,), ins, specs, outs, out_specs, scratch, prefetch, flops)


def shape(dims, dtype):
    return jax.ShapeDtypeStruct(dims, dtype)


def whole(a):
    return pl.BlockSpec(a.shape, lambda *_: (0,) * len(a.shape))


def dot_nn(a, b):
    return lax.dot_general(a, b, (((1,), (0,)), ((), ())), preferred_element_type=F32)


def dot_nt(a, b):
    return lax.dot_general(a, b, (((1,), (1,)), ((), ())), preferred_element_type=F32)


def dot_tn(a, b):
    return lax.dot_general(a, b, (((0,), (0,)), ((), ())), preferred_element_type=F32)


def fold_rows(a):
    return jnp.sum(a.reshape(a.shape[0] // 8, 8, a.shape[1]), axis=0)


def sum_rows(a):
    return jnp.sum(a, axis=0, keepdims=True)


def span(j, size):
    return pl.ds(pl.multiple_of(j * size, size), size)


def start(copies):
    for copy in copies:
        copy.start()


def wait(copies):
    for copy in copies:
        copy.wait()


def load_panels(w_ref, first, scratch, sems, at=0):
    return [
        pltpu.make_async_copy(w_ref.at[first + i], scratch.at[at + i], sems.at[at + i])
        for i in range(scratch.shape[0] - at)
    ]


def panels_scratch(n, width):
    return [pltpu.VMEM((n, width, TILE), BF16), pltpu.SemaphoreType.DMA((n,))]


class Tiles:
    def __init__(self, w_ref, runs, scratch, sems):
        self.w_ref, self.runs, self.scratch, self.sems = w_ref, runs, scratch, sems

    def copies(self, j):
        at = 0
        for i, (first, n) in enumerate(self.runs):
            yield pltpu.make_async_copy(
                self.w_ref.at[first : first + n, span(j, TILE), :],
                self.scratch.at[j, at : at + n],
                self.sems.at[i, j],
            )
            at += n

    def start(self):
        def step(j, carry):
            start(self.copies(j))
            return carry

        lax.fori_loop(0, self.scratch.shape[0], step, 0)

    def get(self, j):
        wait(self.copies(j))
        n = self.scratch.shape[1]
        return [self.scratch[j, i] for i in range(n)]


def tiles_scratch(runs, width):
    n = sum(size for _, size in runs)
    return [
        pltpu.VMEM((width // TILE, n, TILE, TILE), BF16),
        pltpu.SemaphoreType.DMA((len(runs), width // TILE)),
    ]


def row_copies(source, row_ref, target, sems, back=False):
    per = source.shape[1] // CHUNK

    def copy(k):
        far = source.at[k // per, span(row_ref[k], CHUNK)]
        own = target.at[span(k, CHUNK)]
        ends = (own, far) if back else (far, own)
        return pltpu.make_async_copy(*ends, sems.at[k])

    return copy


def for_chunks(n, step, carry=0):
    return lax.fori_loop(0, n, step, carry)


class Rows:
    def __init__(self, refs, scratch, sems):
        self.scratch, self.sems = scratch, sems
        chunks = scratch.shape[0] // CHUNK
        if len(refs) == 1:
            self.parts = [(refs[0], 0, 0, chunks)]
            return
        n = chunks // (2 * len(refs))
        self.parts = [
            (ref, s * n, s * (chunks // 2) + i * n, n) for s in range(2) for i, ref in enumerate(refs)
        ]

    def copy(self, part, i):
        ref, first, base, _ = part
        return pltpu.make_async_copy(
            ref.at[span(first + i, CHUNK)],
            self.scratch.at[span(base + i, CHUNK)],
            self.sems.at[base + i],
        )


def start_rows(*rows):
    order = [(p[2] + i, r, p, i) for r in rows for p in r.parts for i in range(p[3])]
    for _, r, part, i in sorted(order, key=lambda entry: entry[0]):
        r.copy(part, i).start()


def for_rows(pieces, others, fn, carry=0):
    for part in pieces.parts:

        def step(i, carry, part=part):
            pieces.copy(part, i).wait()
            for other in others:
                other.copy(other.parts[0], part[2] + i).wait()
            at = span(part[2] + i, CHUNK)
            return fn(part[2] + i, pieces.scratch[at, :].astype(F32), carry)

        carry = lax.fori_loop(0, part[3], step, carry)
    return carry


def rows_scratch(rows, width, n=1):
    one = [pltpu.VMEM((rows, width), BF16), pltpu.SemaphoreType.DMA((rows // CHUNK,))]
    return one * n


def piece_shapes(rows, width):
    return [shape((rows // 4, width), BF16)] * 4


def put_pieces(at, y, refs):
    half = y.shape[0] // 2
    n = half // len(refs)
    for i, ref in enumerate(refs):
        for s in range(2):
            rows = slice(s * half + i * n, s * half + (i + 1) * n)
            ref[s * n : (s + 1) * n, at] = y[rows].astype(BF16)


def put_norms(at, x, vec_ref, layer, stat_ref, na_ref, nm_ref):
    mean = jnp.mean(x, axis=1, keepdims=True)
    center = x - mean
    r = lax.rsqrt(jnp.mean(center * center, axis=1, keepdims=True) + EPSILON)
    u = center * r
    lane = lax.broadcasted_iota(jnp.int32, (x.shape[0], LANES), 1)
    stat_ref[at, :] = jnp.where(lane < LANES // 2, mean, r)
    na_ref[at, :] = (u * vec_ref[layer, 0:1] + vec_ref[layer, 2:3]).astype(BF16)
    nm_ref[at, :] = (u * vec_ref[layer, 1:2] + vec_ref[layer, 3:4]).astype(BF16)


def unit_of(x, stats):
    return (x.astype(F32) - stats[:, 0:1]) * stats[:, LANES // 2 : LANES // 2 + 1]


def put_qkv(na_ref, loads, w_ref, b_ref, t_ref, q_ref, kv_ref):
    for j in range(3):
        loads[j].wait()
        y = dot_nn(na_ref[...], w_ref[j]) + b_ref[:, j * HD : (j + 1) * HD]
        if j == 0:
            q_ref[...] = turn(y, t_ref, 1.0).astype(BF16)
        elif j == 1:
            kv_ref[:, :HD] = turn(y, t_ref, 1.0).astype(BF16)
        else:
            kv_ref[:, HD:] = y.astype(BF16)


def in_outs(rows, width):
    return [
        shape((rows, width), BF16),
        shape((rows, LANES), F32),
        shape((rows, width), BF16),
        shape((rows, width), BF16),
        shape((rows, HD), BF16),
        shape((rows, 2 * HD), BF16),
    ]


def first_in(tokens, row_at, vec, w, bias, tables):
    width = tokens.shape[2]
    rows = tokens.shape[0] * tokens.shape[1]

    def body(
        row_ref,
        tok_ref,
        vec_ref,
        w_ref,
        b_ref,
        t_ref,
        x_ref,
        stat_ref,
        na_ref,
        nm_ref,
        q_ref,
        kv_ref,
        panels,
        sems,
        row_sems,
    ):
        news = row_copies(tok_ref, row_ref, x_ref, row_sems)
        for k in range(rows // CHUNK):
            news(k).start()
        loads = load_panels(w_ref, QKV, panels, sems)
        start(loads)

        def step(i, carry):
            news(i).wait()
            at = span(i, CHUNK)
            put_norms(at, x_ref[at, :].astype(F32), vec_ref, 0, stat_ref, na_ref, nm_ref)
            return carry

        for_chunks(rows // CHUNK, step)
        put_qkv(na_ref, loads, panels, b_ref, t_ref, q_ref, kv_ref)

    return call_once(
        body,
        (row_at, tokens, vec, w, bias, tables),
        in_outs(rows, width),
        panels_scratch(3, width) + [pltpu.SemaphoreType.DMA((rows // CHUNK,))],
        prefetch=1,
        hbm=(1, 3),
        flops=2 * rows * width * 3 * HD,
    )


def next_in(x, pieces, layer, vec, w, bias, tables):
    rows, width = x.shape

    def body(x_ref, *rest):
        refs = rest[:4]
        vec_ref, w_ref, b_ref, t_ref, new_ref, stat_ref, na_ref, nm_ref = rest[4:12]
        q_ref, kv_ref, panels, sems, xs, x_sems, ps, p_sems = rest[12:]
        xs, ps = Rows([x_ref], xs, x_sems), Rows(refs, ps, p_sems)
        start_rows(xs, ps)
        loads = load_panels(w_ref, QKV, panels, sems)
        start(loads)

        def step(i, branch, carry):
            at = span(i, CHUNK)
            new = xs.scratch[at, :].astype(F32) + branch + vec_ref[layer - 1, 4:5]
            new_ref[at, :] = new.astype(BF16)
            put_norms(at, new, vec_ref, layer, stat_ref, na_ref, nm_ref)
            return carry

        for_rows(ps, [xs], step)
        put_qkv(na_ref, loads, panels, b_ref, t_ref, q_ref, kv_ref)

    return call_once(
        body,
        (x, *pieces, vec, w, bias, tables),
        in_outs(rows, width),
        panels_scratch(3, width) + rows_scratch(rows, width, 2),
        hbm=(0, 1, 2, 3, 4, 6),
        flops=2 * rows * width * 3 * HD,
    )


def gelu_parts(h):
    e = jnp.exp(-0.5 * h * h)
    t = 1.0 / (1.0 + (0.3275911 * 0.5**0.5) * jnp.abs(h))
    tail = 1.061405429 * t - 1.453152027
    tail = tail * t + 1.421413741
    tail = tail * t - 0.284496736
    tail = (tail * t + 0.254829592) * t * (0.5 * e)
    return jnp.where(h >= 0, 1.0 - tail, tail), e * 0.3989422804014327


def project_up(nm, w, bias):
    rows, width = nm.shape
    hidden = bias.shape[1]

    def body(n_ref, w_ref, b_ref, act_ref, slope_ref, panels, sems):
        loads = load_panels(w_ref, UP, panels, sems)
        start(loads)
        for j in range(hidden // TILE):
            at = slice(j * TILE, (j + 1) * TILE)
            loads[j].wait()
            h = dot_nn(n_ref[...], panels[j]) + b_ref[:, at]
            cdf, density = gelu_parts(h)
            act_ref[:, at] = (h * cdf).astype(BF16)
            slope_ref[:, at] = (cdf + h * density).astype(BF16)

    return call_once(
        body,
        (nm, w, bias),
        [shape((rows, hidden), BF16), shape((rows, hidden), BF16)],
        panels_scratch(hidden // TILE, width),
        hbm=(1,),
        flops=2 * rows * width * hidden,
    )


def weights_of(q, kvs, qpos, kpos):
    scores = [dot_nt(q, kv[:, :HD]) * HD**-0.5 for kv in kvs]
    scores = jnp.concatenate(scores, axis=1)
    scores = jnp.where(kpos <= qpos, scores, -1e30)
    e = jnp.exp(scores - jnp.max(scores, axis=1, keepdims=True))
    return e / jnp.sum(e, axis=1, keepdims=True)


def attend_out(q, kvs, qpos, kpos, active, w):
    rows, hidden = active.shape
    width = w.shape[1]
    seqs = kpos.shape[0]
    per = rows // seqs
    runs = [(DENSE, 1), (DOWN, hidden // TILE)]

    def body(q_ref, k0, k1, k2, k3, qp_ref, kp_ref, act_ref, w_ref, mixed_ref, *rest):
        refs = rest[:4]
        wide, sems, left = rest[4:]
        tiles = Tiles(w_ref, runs, wide, sems)
        tiles.start()
        for s in range(seqs):
            at = slice(s * per, (s + 1) * per)
            kvs = [ref[at] for ref in (k0, k1, k2, k3)]
            p = weights_of(q_ref[at], kvs, qp_ref[at], kp_ref[s : s + 1]).astype(BF16)
            mixed = sum(dot_nn(p[:, i * per : (i + 1) * per], kvs[i][:, HD:]) for i in range(4))
            mixed_ref[at] = mixed.astype(BF16)
        left[:, :HD] = mixed_ref[...]
        left[:, HD:] = act_ref[...]

        def step(j, carry):
            y = dot_nt(left[...], jnp.concatenate(tiles.get(j), axis=1))
            put_pieces(span(j, TILE), y, refs)
            return carry

        lax.fori_loop(0, width // TILE, step, 0)

    out = call_once(
        body,
        (q, *kvs, qpos, kpos, active, w),
        [shape((rows, HD), BF16)] + piece_shapes(rows, width),
        tiles_scratch(runs, width) + [pltpu.VMEM((rows, HD + hidden), BF16)],
        hbm=(8,),
        flops=16 * rows * per * HD + 2 * rows * width * (HD + hidden),
    )
    return out[0], out[1:]


def put_back_out(gb_ref, loads, panels, slope_ref, gm_ref, gh_ref, part_ref):
    for j in range(panels.shape[0]):
        loads[j].wait()
        y = dot_nn(gb_ref[...], panels[j])
        if j == 0:
            gm_ref[...] = y.astype(BF16)
        else:
            at = slice((j - 1) * TILE, j * TILE)
            gh = (y * slope_ref[:, at].astype(F32)).astype(BF16)
            gh_ref[:, at] = gh
            part_ref[6:7, at] = sum_rows(gh.astype(F32))


def load_back_out(w_ref, panels, sems):
    first = pltpu.make_async_copy(w_ref.at[DENSE], panels.at[0], sems.at[0])
    return [first] + load_panels(w_ref, DOWN, panels, sems, at=1)


def back_out_shapes(rows, width, hidden):
    return [
        shape((rows, width), BF16),
        shape((rows, HD), BF16),
        shape((rows, hidden), BF16),
        shape((8, width), F32),
    ]


def last_back_out(cotangent, row_at, w, slope):
    width = cotangent.shape[2]
    rows, hidden = slope.shape
    n = 1 + hidden // TILE

    def body(
        row_ref, cot_ref, w_ref, slope_ref, gb_ref, gm_ref, gh_ref, part_ref, panels, sems, row_sems
    ):
        news = row_copies(cot_ref, row_ref, gb_ref, row_sems)
        for k in range(rows // CHUNK):
            news(k).start()
        loads = load_back_out(w_ref, panels, sems)
        start(loads)
        part_ref[...] = jnp.zeros_like(part_ref)

        def step(i, total):
            news(i).wait()
            return total + fold_rows(gb_ref[span(i, CHUNK), :].astype(F32))

        total = for_chunks(rows // CHUNK, step, jnp.zeros((8, width), F32))
        part_ref[4:5, :] = sum_rows(total)
        put_back_out(gb_ref, loads, panels, slope_ref, gm_ref, gh_ref, part_ref)

    return call_once(
        body,
        (row_at, cotangent, w, slope),
        back_out_shapes(rows, width, hidden),
        panels_scratch(n, width) + [pltpu.SemaphoreType.DMA((rows // CHUNK,))],
        prefetch=1,
        hbm=(1, 2),
        flops=2 * rows * width * n * TILE,
    )


def grad_in(g, x, stats, total):
    u = unit_of(x, stats)
    back = total - jnp.mean(total, axis=1, keepdims=True)
    back = back - u * jnp.mean(total * u, axis=1, keepdims=True)
    return g.astype(F32) + stats[:, LANES // 2 : LANES // 2 + 1] * back


def next_back_out(g, x, stats, pieces, w, slope):
    rows, width = g.shape
    hidden = slope.shape[1]
    n = 1 + hidden // TILE

    def body(g_ref, x_ref, stat_ref, *rest):
        refs = rest[:4]
        w_ref, slope_ref, gb_ref, gm_ref, gh_ref, part_ref, panels, sems = rest[4:12]
        gs, xs, ps = (
            Rows(r, rest[12 + 2 * i], rest[13 + 2 * i])
            for i, r in enumerate(([g_ref], [x_ref], refs))
        )
        start_rows(gs, xs, ps)
        loads = load_back_out(w_ref, panels, sems)
        start(loads)
        part_ref[...] = jnp.zeros_like(part_ref)

        def step(i, branch, total):
            at = span(i, CHUNK)
            new = grad_in(gs.scratch[at, :], xs.scratch[at, :], stat_ref[at, :], branch)
            gb_ref[at, :] = new.astype(BF16)
            return total + fold_rows(new)

        total = for_rows(ps, [gs, xs], step, jnp.zeros((8, width), F32))
        part_ref[4:5, :] = sum_rows(total)
        put_back_out(gb_ref, loads, panels, slope_ref, gm_ref, gh_ref, part_ref)

    return call_once(
        body,
        (g, x, stats, *pieces, w, slope),
        back_out_shapes(rows, width, hidden),
        panels_scratch(n, width) + rows_scratch(rows, width, 3),
        hbm=(0, 1, 3, 4, 5, 6, 7),
        flops=2 * rows * width * n * TILE,
    )


def attend_back(q, kvs, gm, qpos, kpos):
    rows = q.shape[0]
    seqs = kpos.shape[0]
    per = rows // seqs

    def body(q_ref, k0, k1, k2, k3, gm_ref, qp_ref, kp_ref, dq_ref, own_ref, y_ref, send_ref):
        part = [slice(i * per, (i + 1) * per) for i in range(4)]
        for s in range(seqs):
            at = part[s]
            kvs = [ref[at] for ref in (k0, k1, k2, k3)]
            q = q_ref[at]
            gm = gm_ref[at]
            p = weights_of(q, kvs, qp_ref[at], kp_ref[s : s + 1])
            dp = jnp.concatenate([dot_nt(gm, kv[:, HD:]) for kv in kvs], axis=1)
            ds = (p * (dp - jnp.sum(p * dp, axis=1, keepdims=True))).astype(BF16)
            p = p.astype(BF16)
            dq = sum(dot_nn(ds[:, part[i]], kvs[i][:, :HD]) for i in range(4))
            dq_ref[at] = dq * HD**-0.5
            late = slice(rows + s * per, rows + (s + 1) * per)
            places = (own_ref.at[at], send_ref.at[at], y_ref.at[at], send_ref.at[late])
            for i, ref in enumerate(places):
                ref[:, :HD] = (dot_tn(ds[:, part[i]], q) * HD**-0.5).astype(ref.dtype)
                ref[:, HD:] = dot_tn(p[:, part[i]], gm).astype(ref.dtype)

    return call_once(
        body,
        (q, *kvs, gm, qpos, kpos),
        [
            shape((rows, HD), F32),
            shape((rows, 2 * HD), F32),
            shape((rows, 2 * HD), F32),
            shape((2 * rows, 2 * HD), BF16),
        ],
        flops=40 * rows * per * HD,
    )


def back_in(dq, own, from_core, from_y, tables, gh, w, x, stats, vec, layer, part):
    rows, hidden = gh.shape
    width = w.shape[1]
    runs = [(QKV, 3), (UP, hidden // TILE)]

    def body(
        dq_ref,
        own_ref,
        core_ref,
        y_ref,
        t_ref,
        gh_ref,
        w_ref,
        x_ref,
        stat_ref,
        vec_ref,
        part_ref,
        gp_ref,
        *rest,
    ):
        refs = rest[:4]
        sum_ref, wide, sems, xs, x_sems = rest[4:]
        tiles = Tiles(w_ref, runs, wide, sems)

        def x_copy(j):
            at = span(j, TILE)
            return pltpu.make_async_copy(x_ref.at[:, at], xs.at[j], x_sems.at[j])

        def begin(j, carry):
            start(tiles.copies(j))
            x_copy(j).start()
            return carry

        lax.fori_loop(0, width // TILE, begin, 0)
        both = own_ref[...] + core_ref[:rows].astype(F32) + y_ref[...].astype(F32)
        parts = (turn(dq_ref[...], t_ref, -1.0), turn(both[:, :HD], t_ref, -1.0), both[:, HD:])
        sum_ref[...] = part_ref[...]
        for i, a in enumerate(parts):
            a = a.astype(BF16)
            at = slice(i * HD, (i + 1) * HD)
            gp_ref[:, at] = a
            sum_ref[5:6, at] = sum_rows(a.astype(F32))

        def step(j, carry):
            at = span(j, TILE)
            w = tiles.get(j)
            gna = dot_nt(gp_ref[...], jnp.concatenate(w[:3], axis=1))
            gnm = dot_nt(gh_ref[...], jnp.concatenate(w[3:], axis=1))
            x_copy(j).wait()
            u = unit_of(xs[j], stat_ref[...])
            y = gna * vec_ref[layer, 0:1, at] + gnm * vec_ref[layer, 1:2, at]
            put_pieces(at, y, refs)
            for i, a in enumerate((gna * u, gnm * u, gna, gnm)):
                sum_ref[i : i + 1, at] = sum_rows(a)
            return carry

        lax.fori_loop(0, width // TILE, step, 0)

    out = call_once(
        body,
        (dq, own, from_core, from_y, tables, gh, w, x, stats, vec, part),
        [shape((rows, 3 * HD), BF16)] + piece_shapes(rows, width) + [shape((8, width), F32)],
        tiles_scratch(runs, width)
        + [pltpu.VMEM((width // TILE, rows, TILE), BF16), pltpu.SemaphoreType.DMA((width // TILE,))],
        hbm=(6, 7),
        flops=2 * rows * width * (3 * HD + hidden),
    )
    return out[0], out[1:5], out[5]


def put_rows(like, row_at, rows_in, pieces, others, value):
    seqs, per, width = like.shape
    rows = seqs * per
    n = len(rows_in)

    def body(row_ref, *rest):
        refs = rest[: n + 4 + len(others)]
        out_ref, own, sems = rest[len(refs) : len(refs) + 3]
        rest = rest[len(refs) + 3 :]
        loads = [Rows([refs[i]], rest[2 * i], rest[2 * i + 1]) for i in range(n)]
        ps = Rows(refs[n : n + 4], rest[2 * n], rest[2 * n + 1])
        start_rows(*loads, ps)
        copies = row_copies(out_ref, row_ref, own, sems, back=True)

        def step(i, branch, carry):
            at = span(i, CHUNK)
            chunks = [load.scratch[at, :] for load in loads]
            own[at, :] = value(chunks, branch, at, refs[n + 4 :])
            copies(i).start()
            return carry

        for_rows(ps, loads, step)

        def finish(i, carry):
            copies(i).wait()
            return carry

        for_chunks(rows // CHUNK, finish)

    return call_once(
        body,
        (row_at, *rows_in, *pieces, *others),
        [shape((seqs, per, width), F32)],
        [pltpu.VMEM((rows, width), F32), pltpu.SemaphoreType.DMA((rows // CHUNK,))]
        + rows_scratch(rows, width, n + 1),
        prefetch=1,
        hbm=tuple(range(1, n + 5)),
        out_hbm=True,
    )[0]


def last_stream(like, row_at, x, pieces, vec, layer):
    def value(chunks, branch, at, others):
        return chunks[0].astype(F32) + branch + others[0][layer, 4:5]

    return put_rows(like, row_at, (x,), pieces, (vec,), value)


def last_grad(like, row_at, g, x, stats, pieces):
    def value(chunks, branch, at, others):
        return grad_in(chunks[0], chunks[1], others[0][at, :], branch)

    return put_rows(like, row_at, (g, x), pieces, (stats,), value)


def pack_panels(layer, *parts):
    depth = parts[0].shape[1]
    panels = [(i, c) for i, a in enumerate(parts) for c in range(a.shape[2] // TILE)]

    def body(*refs):
        out_ref, sems = refs[-2:]
        copies = [
            pltpu.make_async_copy(
                refs[i].at[layer, :, c * TILE : (c + 1) * TILE], out_ref.at[p], sems.at[p]
            )
            for p, (i, c) in enumerate(panels)
        ]
        start(copies)
        wait(copies)

    return call_once(
        body,
        parts,
        [shape((len(panels), depth, TILE), BF16)],
        [pltpu.SemaphoreType.DMA((len(panels),))],
        hbm=(0, 1, 2, 3),
    )[0]


def turn(x, tables, sign):
    head = x[:, :LANES]
    half = ROT // 2
    up = pltpu.roll(head, LANES - half, 1)
    down = pltpu.roll(head, half, 1)
    head = head * tables[0] + sign * (down * tables[2] - up * tables[1])
    return jnp.concatenate([head, x[:, LANES:]], axis=1)


def weight_grad(x, ys, blocks, got=None):
    rows, width = x.shape
    cols = [a.shape[1] for a in ys]
    total = sum(cols)
    size = width // 16

    def body(block_ref, x0_ref, x1_ref, *rest):
        y_refs = rest[: len(ys)]
        left = jnp.concatenate([x0_ref[...], x1_ref[...]], axis=1)
        at = 0
        for ref, n in zip(y_refs, cols):
            y = dot_tn(left, ref[...])
            if got is not None:
                y = y + rest[len(ys)][:, at : at + n].astype(F32)
            rest[-1][:, at : at + n] = y.astype(BF16)
            at += n

    ins = (blocks, x, x, *ys)
    specs = [
        pl.BlockSpec((rows, size), lambda j, block: (0, block[2 * j])),
        pl.BlockSpec((rows, size), lambda j, block: (0, block[2 * j + 1])),
    ]
    specs += [whole(a) for a in ys]
    if got is not None:
        ins += (got,)
        specs += [pl.BlockSpec((2 * size, total), lambda j, *_: (j, 0))]
    return call(
        body,
        (4,),
        ins,
        specs,
        [shape((width // 2, total), BF16)],
        [pl.BlockSpec((2 * size, total), lambda j, *_: (j, 0))],
        prefetch=1,
        flops=2 * rows * (width // 2) * total,
    )[0]


def scatter_weight_grad(value):
    return lax.psum_scatter(value, "fsdp", scatter_dimension=0, tiled=True)


def swap_half(value):
    return swap_y(value[value.shape[0] // 2 :])


def finish_weight_grads(layers, cols):
    flat = [a for layer in layers for a in layer]
    depth = layers[0][0].shape[0] // 2
    outs = [shape((len(layers), depth, n), F32) for n in cols]

    def body(*refs):
        qkv_ref, dense_ref, up_ref, down_ref = refs[len(flat) :]
        for l in range(len(layers)):
            ins = refs[6 * l : 6 * l + 6]
            out, up, qkv = (
                ins[i][:depth].astype(F32) + ins[3 + i][...].astype(F32) for i in range(3)
            )
            qkv_ref[l] = qkv
            dense_ref[l] = out[:, :HD]
            up_ref[l] = up
            down_ref[l] = out[:, HD:]

    return call_once(body, flat, outs)


def body(
    tokens,
    block_order,
    cotangent,
    qkv_weight,
    qkv_bias,
    dense_weight,
    up_weight,
    up_bias,
    down_weight,
    norm_gains,
    norm_shifts,
    out_bias,
):
    seqs, per, width = tokens.shape
    block = 128
    c, t = lax.axis_index("ctx"), lax.axis_index("tp")

    b = jnp.arange(8, dtype=jnp.int32)
    near = (b // 2) * 4 + (c ^ (2 * (b % 2)))
    far = near ^ 1
    row_at = jnp.tile(2 * ((t + b // 2) % 4) + b % 2, seqs)

    row = row_at[:, None] * CHUNK + jnp.arange(CHUNK, dtype=jnp.int32)[None, :]
    row = row.reshape(seqs, per)
    slots = jnp.arange(block_order.shape[0], dtype=jnp.int32)

    def positions(owner):
        slot = 2 * owner + row // block
        here = slot[:, :, None] == slots
        return jnp.sum(jnp.where(here, block_order, 0), axis=2) * block + row % block

    qpos = positions(c).reshape(seqs * per, 1)
    kpos = jnp.concatenate([positions(c ^ i) for i in range(4)], axis=1)
    inverse = 10000.0 ** (-(jnp.arange(ROT // 2, dtype=F32) * 2.0) / ROT)
    angles = qpos.astype(F32) * inverse[None, :]
    cosine, sine = jnp.cos(angles), jnp.sin(angles)
    none = jnp.zeros_like(sine)
    rest = jnp.zeros((seqs * per, LANES - ROT), F32)
    tables = jnp.stack(
        [
            jnp.concatenate([cosine, cosine, rest + 1.0], axis=1),
            jnp.concatenate([sine, none, rest], axis=1),
            jnp.concatenate([none, sine, rest], axis=1),
        ]
    )

    vec = jnp.concatenate(
        [
            norm_gains,
            norm_shifts,
            out_bias[:, None],
            jnp.zeros((LAYERS, 3, width), BF16),
        ],
        axis=1,
    ).astype(F32)
    weights = (qkv_weight, dense_weight, up_weight, down_weight)
    qkv_b = qkv_bias.astype(F32)
    up_b = up_bias.astype(F32)

    kept = []
    w = sums = None
    for l in range(LAYERS):
        shard = pack_panels(l, *weights)
        if w is not None:
            shard, _ = together(shard, w)
        w = gather_weights(shard)
        if l == 0:
            new = first_in(tokens, row_at, vec, w, qkv_b[:1], tables)
        else:
            new = next_in(kept[-1][1], sums, l, vec, w, qkv_b[l : l + 1], tables)
        x, stats, na, nm, q, kv = new
        kv_y, kv_core = swap_y(kv), swap_core(kv)
        active, slope = project_up(nm, w, up_b[l : l + 1])
        kv_y, active = together(kv_y, active)
        kvs = [kv, kv_core, kv_y, swap_core(kv_y)]
        mixed, pieces = attend_out(q, kvs, qpos, kpos, active, w)
        held, moving = tp_1(pieces)
        if l < LAYERS - 1:
            held, moving = tp_2(held, moving)
            sums = tp_pieces(*tp_3(held, moving))
        kept.append((w, x, stats, na, nm, q, kvs, mixed, active, slope, pieces))

    late, late_moving = held, moving
    small = [None] * LAYERS
    scattered = [None] * LAYERS
    g = activations = None
    for l in reversed(range(LAYERS)):
        last = l == LAYERS - 1
        w, x, stats, na, nm, q, kvs, mixed, active, slope, pieces = kept[l]
        if last:
            slope, _ = together(slope, pieces)
            g, gm, gh, part = last_back_out(cotangent, row_at, w, slope)
            late_moving, gm = together(late_moving, gm)
            late, late_moving = tp_2(late, late_moving)
            q, late = together(q, late)
        else:
            after = kept[l + 1]
            g, gm, gh, part = next_back_out(g, after[1], after[2], sums, w, slope)
            sums_3, gm = together(scattered[l + 1][2], gm)
            scattered[l + 1] = (*scattered[l + 1][:2], sums_3)
        dq, own, to_y, send = attend_back(q, kvs, gm, qpos, kpos)
        from_core = swap_core(send)
        to_y = add(to_y, from_core[seqs * per :])
        from_y = swap_y(to_y)
        g_in, to_y = together(g, to_y)
        out_far = weight_grad(g_in, (mixed, active), far)
        if last:
            late_moving, out_far = together(late_moving, out_far)
            late, late_moving = tp_3(late, late_moving)
            nm, late = together(nm, late)
        out_got = swap_core(out_far)
        nm, _ = together(nm, out_far)
        up_far = weight_grad(nm, (gh,), far)
        out_got, up_far = together(out_got, up_far)
        out_near = weight_grad(g_in, (mixed, active), near, out_got)
        out_sum = scatter_weight_grad(out_near)
        up_got, out_near = together(swap_core(up_far), out_near)
        up_near = weight_grad(nm, (gh,), near, up_got)
        up_sum = scatter_weight_grad(up_near)
        from_y, up_near = together(from_y, up_near)
        if last:
            late_moving, from_y = together(late_moving, from_y)
        gp, pieces, small[l] = back_in(
            dq, own, from_core, from_y, tables, gh, w, x, stats, vec, l, part
        )
        held, moving = tp_1(pieces)
        qkv_far = weight_grad(na, (gp,), far)
        if last:
            out_sum, moving, qkv_far = together(out_sum, moving, qkv_far)
        else:
            moving, qkv_far = together(moving, qkv_far)
        held, moving = tp_2(held, moving)
        qkv_near = weight_grad(na, (gp,), near, swap_core(qkv_far))
        qkv_sum = scatter_weight_grad(qkv_near)
        if last:
            moving, qkv_near = together(moving, qkv_near)
            held, moving = tp_3(held, moving)
            up_sum, held = together(up_sum, held)
            activations = last_stream(tokens, row_at, x, tp_pieces(late, late_moving), vec, l)
            moving, activations = together(moving, activations)
        else:
            total = jnp.stack(small)
            total = total + swap_core(total)
            total = total + swap_y(total)
            after_halves = [swap_half(a) for a in scattered[l + 1]]
            moving, qkv_near, total, out_sum = together(moving, qkv_near, total, out_sum)
            held, moving = tp_3(held, moving)
            total = total + swap_x(total, 1)
            total = total + swap_x(total, 2)
            out_half = swap_half(out_sum)
            moving, total, after_halves = together(moving, total, after_halves)
        sums = tp_pieces(held, moving)
        scattered[l] = (out_sum, up_sum, qkv_sum)
    halves = [out_half] + [swap_half(a) for a in scattered[0][1:]]
    wide = total[:, :4]
    for k in (4, 1, 2):
        wide = wide + swap_tp(wide, k)
    input_grad = last_grad(tokens, row_at, g, kept[0][1], kept[0][2], sums)
    qkv_grad, dense_grad, up_grad, down_grad = finish_weight_grads(
        [(*scattered[0], *halves), (*scattered[1], *after_halves)],
        [a.shape[2] for a in weights],
    )
    return (
        activations,
        input_grad,
        qkv_grad,
        total[:, 5, : qkv_bias.shape[1]],
        dense_grad,
        up_grad,
        total[:, 6, : up_bias.shape[1]],
        down_grad,
        wide[:, 0:2],
        wide[:, 2:4],
        total[:, 4],
    )


def solution(mesh):
    weight = P(None, ("fsdp", "ctx"), "tp")
    stream = P("fsdp", "ctx", None)
    bias = P(None, "tp")
    return jax.shard_map(
        body,
        mesh=mesh,
        in_specs=(
            stream,
            P(),
            stream,
            weight,
            bias,
            weight,
            weight,
            bias,
            weight,
            P(),
            P(),
            P(),
        ),
        out_specs=(
            stream,
            stream,
            weight,
            bias,
            weight,
            weight,
            bias,
            weight,
            P(),
            P(),
            P(),
        ),
        check_vma=False,
    )
```

```python
import jax
import jax.numpy as jnp
from jax import lax
from jax.experimental import pallas as pl
from jax.experimental.pallas import tpu as pltpu
from jax.sharding import PartitionSpec as P

HD = 256
ROT = 64
LAYERS = 2
EPSILON = 1e-05
LANES = 128
TILE = 256
CHUNK = 32
ALL_PANELS = (0, 3, 4, 8)
IN_PANELS, OUT_PANELS = (0, 3), (0, 1)
F32 = jnp.float32
BF16 = jnp.bfloat16
VMEM_LIMIT = 24 * 1024 * 1024


def swap_core(value):
    return lax.ppermute(value, "ctx", [(i, i ^ 1) for i in range(4)])


def swap_y(value):
    return lax.ppermute(value, "ctx", [(i, i ^ 2) for i in range(4)])


def from_x(value, k):
    return lax.ppermute(value, "fsdp", [((i + k) % 4, i) for i in range(4)])


def swap_both(value):
    return lax.ppermute(value, "ctx", [(i, i ^ 3) for i in range(4)])


def swap_tp(value, k):
    return lax.ppermute(value, "tp", [(i, i ^ k) for i in range(8)])


def from_z(value, k):
    return lax.ppermute(value, "tp", [((i & 4) + (i + k) % 4, i) for i in range(8)])


def to_z(value, k):
    return lax.ppermute(value, "tp", [(i, (i & 4) + (i + k) % 4) for i in range(8)])


def gather_weights(shard):
    return lax.all_gather(shard, ("fsdp", "ctx"), axis=1, tiled=True)


def together(*values):
    return lax.optimization_barrier(values)


def tp_1(pieces):
    firsts = [to_z(pieces[k], k) for k in (1, 3, 2)]
    return (pieces[0], pieces[4]), (firsts, swap_tp(pieces[5], 4))


def tp_2(kept, arrived):
    (own, near), (firsts, far) = kept, arrived
    first = add_up(own, *firsts)
    parts = add_split(near, far)
    seconds = [to_z(parts[k], k) for k in (1, 3, 2)]
    return (first, parts[0]), (swap_tp(first, 4), seconds)


def tp_3_sums(kept, arrived):
    (first, own), (other, seconds) = kept, arrived
    second = add_up(own, *seconds)
    return add_up(first, other), second


def tp_3(kept, arrived):
    first, second = tp_3_sums(kept, arrived)
    seconds = [from_z(second, k) for k in (1, 3, 2)]
    firsts = [from_z(first, k) for k in (1, 3, 2)]
    return (first, second), (firsts, seconds)


def tp_4(second, seconds):
    near = stack_up(second, seconds[0], seconds[2], seconds[1])
    return near, swap_tp(near, 4)


def tp_pieces(first, firsts, near, far):
    return (first, firsts[0], firsts[2], firsts[1], near, far)


def around(value, move):
    return [move(value, k) for k in (1, 2, 3)]


def around_ctx(value):
    return [swap_y(value), swap_core(value), swap_both(value)]


def pair_up(value, got):
    return (value + got[1]) + (got[0] + got[2])


def call(body, grid, ins, in_specs, outs, out_specs, scratch=(), prefetch=0, flops=0):
    nbytes = sum(a.size * a.dtype.itemsize for a in outs)
    nbytes += sum(min(a.size * a.dtype.itemsize, 1 << 22) for a in ins)
    return pl.pallas_call(
        body,
        grid_spec=pltpu.PrefetchScalarGridSpec(
            num_scalar_prefetch=prefetch,
            grid=grid,
            in_specs=in_specs,
            out_specs=out_specs,
            scratch_shapes=scratch,
        ),
        out_shape=outs,
        compiler_params=pltpu.CompilerParams(vmem_limit_bytes=VMEM_LIMIT),
        cost_estimate=pl.CostEstimate(
            flops=int(flops), bytes_accessed=int(nbytes), transcendentals=0
        ),
    )(*ins)


def call_once(body, ins, outs, scratch=(), prefetch=0, hbm=(), out_hbm=False, flops=0):
    ins = tuple(
        pltpu.with_memory_space_constraint(a, pltpu.HBM) if i in hbm else a
        for i, a in enumerate(ins)
    )
    specs = [
        pl.BlockSpec(memory_space=pltpu.HBM) if i in hbm else whole(a)
        for i, a in enumerate(ins)
        if i >= prefetch
    ]
    out_specs = [pl.BlockSpec(memory_space=pltpu.HBM) if out_hbm else whole(a) for a in outs]
    return call(body, (1,), ins, specs, outs, out_specs, scratch, prefetch, flops)


def pinned(*arrays):
    return tuple(pltpu.with_memory_space_constraint(a, pltpu.HBM) for a in arrays)


def shape(dims, dtype):
    return jax.ShapeDtypeStruct(dims, dtype)


def whole(a):
    return pl.BlockSpec(a.shape, lambda *_: (0,) * len(a.shape))


def dot_nn(a, b):
    return lax.dot_general(a, b, (((1,), (0,)), ((), ())), preferred_element_type=F32)


def dot_nt(a, b):
    return lax.dot_general(a, b, (((1,), (1,)), ((), ())), preferred_element_type=F32)


def dot_tn(a, b):
    return lax.dot_general(a, b, (((0,), (0,)), ((), ())), preferred_element_type=F32)


def fold_rows(a):
    return jnp.sum(a.reshape(a.shape[0] // 8, 8, a.shape[1]), axis=0)


def sum_rows(a):
    return jnp.sum(a, axis=0, keepdims=True)


def span(j, size):
    return pl.ds(pl.multiple_of(j * size, size), size)


def start(copies):
    for copy in copies:
        copy.start()


def wait(copies):
    for copy in copies:
        copy.wait()


def load_panels(w_ref, first, scratch, sems, at=0):
    return [
        pltpu.make_async_copy(w_ref.at[first + i], scratch.at[at + i], sems.at[at + i])
        for i in range(scratch.shape[0] - at)
    ]


def panels_scratch(n, width):
    return [pltpu.VMEM((n, width, TILE), BF16), pltpu.SemaphoreType.DMA((n,))]


class Tiles:
    def __init__(self, w_ref, runs, scratch, sems):
        self.w_ref, self.runs, self.scratch, self.sems = w_ref, runs, scratch, sems

    def copies(self, j):
        at = 0
        for i, (first, n) in enumerate(self.runs):
            yield pltpu.make_async_copy(
                self.w_ref.at[first : first + n, span(j, TILE), :],
                self.scratch.at[j, at : at + n],
                self.sems.at[i, j],
            )
            at += n

    def start(self):
        def step(j, carry):
            start(self.copies(j))
            return carry

        lax.fori_loop(0, self.scratch.shape[0], step, 0)

    def get(self, j):
        wait(self.copies(j))
        n = self.scratch.shape[1]
        return [self.scratch[j, i] for i in range(n)]


def tiles_scratch(runs, width):
    n = sum(size for _, size in runs)
    return [
        pltpu.VMEM((width // TILE, n, TILE, TILE), BF16),
        pltpu.SemaphoreType.DMA((len(runs), width // TILE)),
    ]


def row_copies(source, row_ref, target, sems, back=False):
    per = source.shape[1] // CHUNK

    def copy(k):
        far = source.at[k // per, span(row_ref[k], CHUNK)]
        own = target.at[span(k, CHUNK)]
        ends = (own, far) if back else (far, own)
        return pltpu.make_async_copy(*ends, sems.at[k])

    return copy


def for_chunks(n, step, carry=0):
    return lax.fori_loop(0, n, step, carry)


class Rows:
    def __init__(self, refs, scratch, sems):
        self.scratch, self.sems = scratch, sems
        self.parts, base = [], 0
        for ref in refs:
            self.parts.append((ref, base, ref.shape[0] // CHUNK))
            base += ref.shape[0] // CHUNK

    def copy(self, part, i):
        ref, base, _ = part
        return pltpu.make_async_copy(
            ref.at[span(i, CHUNK)], self.scratch.at[span(base + i, CHUNK)], self.sems.at[base + i]
        )


def start_rows(*rows):
    order = [(base + i, r, (ref, base, n), i) for r in rows for ref, base, n in r.parts for i in range(n)]
    for _, r, part, i in sorted(order, key=lambda entry: entry[0]):
        r.copy(part, i).start()


def for_rows(pieces, others, fn, carry=0):
    for part in pieces.parts:

        def step(i, carry, part=part):
            pieces.copy(part, i).wait()
            for other in others:
                other.copy(other.parts[0], part[1] + i).wait()
            at = span(part[1] + i, CHUNK)
            return fn(part[1] + i, pieces.scratch[at, :].astype(F32), carry)

        carry = lax.fori_loop(0, part[2], step, carry)
    return carry


def rows_scratch(rows, width, n=1):
    one = [pltpu.VMEM((rows, width), BF16), pltpu.SemaphoreType.DMA((rows // CHUNK,))]
    return one * n


def piece_shapes(rows, width):
    return [shape((rows // 8, width), BF16)] * 4 + [shape((rows // 4, width), BF16)] * 2


def put_pieces(at, y, refs):
    base = 0
    for ref in refs:
        ref[:, at] = y[base : base + ref.shape[0]].astype(BF16)
        base += ref.shape[0]


def put_norms(at, x, vec_ref, layer, stat_ref, na_ref, nm_ref):
    mean = jnp.mean(x, axis=1, keepdims=True)
    center = x - mean
    r = lax.rsqrt(jnp.mean(center * center, axis=1, keepdims=True) + EPSILON)
    u = center * r
    lane = lax.broadcasted_iota(jnp.int32, (x.shape[0], LANES), 1)
    stat_ref[at, :] = jnp.where(lane < LANES // 2, mean, r)
    na_ref[at, :] = (u * vec_ref[layer, 0:1] + vec_ref[layer, 2:3]).astype(BF16)
    nm_ref[at, :] = (u * vec_ref[layer, 1:2] + vec_ref[layer, 3:4]).astype(BF16)


def unit_of(x, stats):
    return (x.astype(F32) - stats[:, 0:1]) * stats[:, LANES // 2 : LANES // 2 + 1]


def put_qkv(na_ref, loads, w_ref, b_ref, t_ref, q_ref, kv_ref):
    for j in range(3):
        loads[j].wait()
        y = dot_nn(na_ref[...], w_ref[j]) + b_ref[:, j * HD : (j + 1) * HD]
        if j == 0:
            q_ref[...] = turn(y, t_ref, 1.0).astype(BF16)
        elif j == 1:
            kv_ref[:, :HD] = turn(y, t_ref, 1.0).astype(BF16)
        else:
            kv_ref[:, HD:] = y.astype(BF16)


def in_outs(rows, width):
    return [
        shape((rows, width), BF16),
        shape((rows, LANES), F32),
        shape((rows, width), BF16),
        shape((rows, width), BF16),
        shape((rows, HD), BF16),
        shape((rows, 2 * HD), BF16),
    ]


def first_in(tokens, row_at, vec, w, bias, tables):
    width = tokens.shape[2]
    rows = tokens.shape[0] * tokens.shape[1]

    def body(
        row_ref,
        tok_ref,
        vec_ref,
        w_ref,
        b_ref,
        t_ref,
        x_ref,
        stat_ref,
        na_ref,
        nm_ref,
        q_ref,
        kv_ref,
        panels,
        sems,
        row_sems,
    ):
        news = row_copies(tok_ref, row_ref, x_ref, row_sems)
        for k in range(rows // CHUNK):
            news(k).start()
        loads = load_panels(w_ref, w[1], panels, sems)
        start(loads)

        def step(i, carry):
            news(i).wait()
            at = span(i, CHUNK)
            put_norms(at, x_ref[at, :].astype(F32), vec_ref, 0, stat_ref, na_ref, nm_ref)
            return carry

        for_chunks(rows // CHUNK, step)
        put_qkv(na_ref, loads, panels, b_ref, t_ref, q_ref, kv_ref)

    return call_once(
        body,
        (row_at, tokens, vec, w[0], bias, tables),
        in_outs(rows, width),
        panels_scratch(3, width) + [pltpu.SemaphoreType.DMA((rows // CHUNK,))],
        prefetch=1,
        hbm=(1, 3),
        flops=2 * rows * width * 3 * HD,
    )


def next_in(x, pieces, layer, vec, w, bias, tables):
    rows, width = x.shape

    def body(x_ref, *rest):
        refs = rest[:6]
        vec_ref, w_ref, b_ref, t_ref, new_ref, stat_ref, na_ref, nm_ref = rest[6:14]
        q_ref, kv_ref, panels, sems, xs, x_sems, ps, p_sems = rest[14:]
        xs, ps = Rows([x_ref], xs, x_sems), Rows(refs, ps, p_sems)
        start_rows(xs, ps)
        loads = load_panels(w_ref, w[1], panels, sems)
        start(loads)

        def step(i, branch, carry):
            at = span(i, CHUNK)
            new = xs.scratch[at, :].astype(F32) + branch + vec_ref[layer - 1, 4:5]
            new_ref[at, :] = new.astype(BF16)
            put_norms(at, new, vec_ref, layer, stat_ref, na_ref, nm_ref)
            return carry

        for_rows(ps, [xs], step)
        put_qkv(na_ref, loads, panels, b_ref, t_ref, q_ref, kv_ref)

    return call_once(
        body,
        (x, *pieces, vec, w[0], bias, tables),
        in_outs(rows, width),
        panels_scratch(3, width) + rows_scratch(rows, width, 2),
        hbm=(0, 1, 2, 3, 4, 5, 6, 8),
        flops=2 * rows * width * 3 * HD,
    )


def gelu_parts(h):
    e = jnp.exp(-0.5 * h * h)
    t = 1.0 / (1.0 + (0.3275911 * 0.5**0.5) * jnp.abs(h))
    tail = 1.061405429 * t - 1.453152027
    tail = tail * t + 1.421413741
    tail = tail * t - 0.284496736
    tail = (tail * t + 0.254829592) * t * (0.5 * e)
    return jnp.where(h >= 0, 1.0 - tail, tail), e * 0.3989422804014327


def project_up(nm, w, bias):
    rows, width = nm.shape
    hidden = bias.shape[1]

    def body(n_ref, w_ref, b_ref, act_ref, slope_ref, panels, sems):
        loads = load_panels(w_ref, w[2], panels, sems)
        start(loads)
        for j in range(hidden // TILE):
            at = slice(j * TILE, (j + 1) * TILE)
            loads[j].wait()
            h = dot_nn(n_ref[...], panels[j]) + b_ref[:, at]
            cdf, density = gelu_parts(h)
            act_ref[:, at] = (h * cdf).astype(BF16)
            slope_ref[:, at] = (cdf + h * density).astype(BF16)

    return call_once(
        body,
        (nm, w[0], bias),
        [shape((rows, hidden), BF16), shape((rows, hidden), BF16)],
        panels_scratch(hidden // TILE, width),
        hbm=(1,),
        flops=2 * rows * width * hidden,
    )


def weights_of(q, kvs, qpos, kpos):
    scores = [dot_nt(q, kv[:, :HD]) * HD**-0.5 for kv in kvs]
    scores = jnp.concatenate(scores, axis=1)
    scores = jnp.where(kpos <= qpos, scores, -1e30)
    e = jnp.exp(scores - jnp.max(scores, axis=1, keepdims=True))
    return e / jnp.sum(e, axis=1, keepdims=True)


def attend_out(q, kvs, qpos, kpos, active, w):
    rows, hidden = active.shape
    width = w[0].shape[1]
    seqs = kpos.shape[0]
    per = rows // seqs
    runs = [(w[1], 1), (w[2], hidden // TILE)]

    def body(q_ref, k0, k1, k2, k3, qp_ref, kp_ref, act_ref, w_ref, mixed_ref, *rest):
        refs = rest[:6]
        wide, sems, left = rest[6:]
        tiles = Tiles(w_ref, runs, wide, sems)
        tiles.start()
        for s in range(seqs):
            at = slice(s * per, (s + 1) * per)
            kvs = [ref[at] for ref in (k0, k1, k2, k3)]
            p = weights_of(q_ref[at], kvs, qp_ref[at], kp_ref[s : s + 1]).astype(BF16)
            mixed = sum(dot_nn(p[:, i * per : (i + 1) * per], kvs[i][:, HD:]) for i in range(4))
            mixed_ref[at] = mixed.astype(BF16)
        left[:, :HD] = mixed_ref[...]
        left[:, HD:] = act_ref[...]

        def step(j, carry):
            y = dot_nt(left[...], jnp.concatenate(tiles.get(j), axis=1))
            put_pieces(span(j, TILE), y, refs)
            return carry

        lax.fori_loop(0, width // TILE, step, 0)

    out = call_once(
        body,
        (q, *kvs, qpos, kpos, active, w[0]),
        [shape((rows, HD), BF16)] + piece_shapes(rows, width),
        tiles_scratch(runs, width) + [pltpu.VMEM((rows, HD + hidden), BF16)],
        hbm=(8,),
        flops=16 * rows * per * HD + 2 * rows * width * (HD + hidden),
    )
    return out[0], out[1:]


def put_back_out(gb_ref, loads, panels, slope_ref, gm_ref, gh_ref, part_ref):
    for j in range(panels.shape[0]):
        loads[j].wait()
        y = dot_nn(gb_ref[...], panels[j])
        if j == 0:
            gm_ref[...] = y.astype(BF16)
        else:
            at = slice((j - 1) * TILE, j * TILE)
            gh = (y * slope_ref[:, at].astype(F32)).astype(BF16)
            gh_ref[:, at] = gh
            part_ref[6:7, at] = sum_rows(gh.astype(F32))


def load_back_out(w_ref, w, panels, sems):
    first = pltpu.make_async_copy(w_ref.at[w[1]], panels.at[0], sems.at[0])
    return [first] + load_panels(w_ref, w[2], panels, sems, at=1)


def back_out_shapes(rows, width, hidden):
    return [
        shape((rows, width), BF16),
        shape((rows, HD), BF16),
        shape((rows, hidden), BF16),
        shape((8, width), F32),
    ]


def last_back_out(cotangent, row_at, w, slope):
    width = cotangent.shape[2]
    rows, hidden = slope.shape
    n = 1 + hidden // TILE

    def body(
        row_ref, cot_ref, w_ref, slope_ref, gb_ref, gm_ref, gh_ref, part_ref, panels, sems, row_sems
    ):
        news = row_copies(cot_ref, row_ref, gb_ref, row_sems)
        for k in range(rows // CHUNK):
            news(k).start()
        loads = load_back_out(w_ref, w, panels, sems)
        start(loads)
        part_ref[...] = jnp.zeros_like(part_ref)

        def step(i, total):
            news(i).wait()
            return total + fold_rows(gb_ref[span(i, CHUNK), :].astype(F32))

        total = for_chunks(rows // CHUNK, step, jnp.zeros((8, width), F32))
        part_ref[4:5, :] = sum_rows(total)
        put_back_out(gb_ref, loads, panels, slope_ref, gm_ref, gh_ref, part_ref)

    return call_once(
        body,
        (row_at, cotangent, w[0], *pinned(slope)),
        back_out_shapes(rows, width, hidden),
        panels_scratch(n, width) + [pltpu.SemaphoreType.DMA((rows // CHUNK,))],
        prefetch=1,
        hbm=(1, 2),
        flops=2 * rows * width * n * TILE,
    )


def grad_in(g, x, stats, total):
    u = unit_of(x, stats)
    back = total - jnp.mean(total, axis=1, keepdims=True)
    back = back - u * jnp.mean(total * u, axis=1, keepdims=True)
    return g.astype(F32) + stats[:, LANES // 2 : LANES // 2 + 1] * back


def next_back_out(g, x, stats, pieces, w, slope):
    rows, width = g.shape
    hidden = slope.shape[1]
    n = 1 + hidden // TILE

    def body(g_ref, x_ref, stat_ref, *rest):
        refs = rest[:6]
        w_ref, slope_ref, gb_ref, gm_ref, gh_ref, part_ref, panels, sems = rest[6:14]
        gs, xs, ps = (
            Rows(r, rest[14 + 2 * i], rest[15 + 2 * i])
            for i, r in enumerate(([g_ref], [x_ref], refs))
        )
        start_rows(gs, xs, ps)
        loads = load_back_out(w_ref, w, panels, sems)
        start(loads)
        part_ref[...] = jnp.zeros_like(part_ref)

        def step(i, branch, total):
            at = span(i, CHUNK)
            new = grad_in(gs.scratch[at, :], xs.scratch[at, :], stat_ref[at, :], branch)
            gb_ref[at, :] = new.astype(BF16)
            return total + fold_rows(new)

        total = for_rows(ps, [gs, xs], step, jnp.zeros((8, width), F32))
        part_ref[4:5, :] = sum_rows(total)
        put_back_out(gb_ref, loads, panels, slope_ref, gm_ref, gh_ref, part_ref)

    return call_once(
        body,
        (g, x, stats, *pieces, w[0], *pinned(slope)),
        back_out_shapes(rows, width, hidden),
        panels_scratch(n, width) + rows_scratch(rows, width, 3),
        hbm=(0, 1, 3, 4, 5, 6, 7, 8, 9),
        flops=2 * rows * width * n * TILE,
    )


def attend_back(q, kvs, gm, qpos, kpos):
    rows = q.shape[0]
    seqs = kpos.shape[0]
    per = rows // seqs

    def body(q_ref, k0, k1, k2, k3, gm_ref, qp_ref, kp_ref, dq_ref, own_ref, y_ref, send_ref):
        part = [slice(i * per, (i + 1) * per) for i in range(4)]
        for s in range(seqs):
            at = part[s]
            kvs = [ref[at] for ref in (k0, k1, k2, k3)]
            q = q_ref[at]
            gm = gm_ref[at]
            p = weights_of(q, kvs, qp_ref[at], kp_ref[s : s + 1])
            dp = jnp.concatenate([dot_nt(gm, kv[:, HD:]) for kv in kvs], axis=1)
            ds = (p * (dp - jnp.sum(p * dp, axis=1, keepdims=True))).astype(BF16)
            p = p.astype(BF16)
            dq = sum(dot_nn(ds[:, part[i]], kvs[i][:, :HD]) for i in range(4))
            dq_ref[at] = dq * HD**-0.5
            late = slice(rows + s * per, rows + (s + 1) * per)
            places = (own_ref.at[at], send_ref.at[at], y_ref.at[at], send_ref.at[late])
            for i, ref in enumerate(places):
                ref[:, :HD] = (dot_tn(ds[:, part[i]], q) * HD**-0.5).astype(ref.dtype)
                ref[:, HD:] = dot_tn(p[:, part[i]], gm).astype(ref.dtype)

    return call_once(
        body,
        (q, *pinned(*kvs), gm, qpos, kpos),
        [
            shape((rows, HD), F32),
            shape((rows, 2 * HD), F32),
            shape((rows, 2 * HD), F32),
            shape((2 * rows, 2 * HD), BF16),
        ],
        flops=40 * rows * per * HD,
    )


def back_in(dq, own, from_core, from_y, tables, gh, w, x, stats, vec, layer, part):
    rows, hidden = gh.shape
    width = w[0].shape[1]
    runs = [(w[1], 3), (w[2], hidden // TILE)]

    def body(
        dq_ref,
        own_ref,
        core_ref,
        y_ref,
        t_ref,
        gh_ref,
        w_ref,
        x_ref,
        stat_ref,
        vec_ref,
        part_ref,
        gp_ref,
        *rest,
    ):
        refs = rest[:6]
        sum_ref, wide, sems, xs, x_sems = rest[6:]
        tiles = Tiles(w_ref, runs, wide, sems)

        def x_copy(j):
            at = span(j, TILE)
            return pltpu.make_async_copy(x_ref.at[:, at], xs.at[j], x_sems.at[j])

        def begin(j, carry):
            start(tiles.copies(j))
            x_copy(j).start()
            return carry

        lax.fori_loop(0, width // TILE, begin, 0)
        both = own_ref[...] + core_ref[:rows].astype(F32) + y_ref[...].astype(F32)
        parts = (turn(dq_ref[...], t_ref, -1.0), turn(both[:, :HD], t_ref, -1.0), both[:, HD:])
        sum_ref[...] = part_ref[...]
        for i, a in enumerate(parts):
            a = a.astype(BF16)
            at = slice(i * HD, (i + 1) * HD)
            gp_ref[:, at] = a
            sum_ref[5:6, at] = sum_rows(a.astype(F32))

        def step(j, carry):
            at = span(j, TILE)
            w_tile = tiles.get(j)
            gna = dot_nt(gp_ref[...], jnp.concatenate(w_tile[:3], axis=1))
            gnm = dot_nt(gh_ref[...], jnp.concatenate(w_tile[3:], axis=1))
            x_copy(j).wait()
            u = unit_of(xs[j], stat_ref[...])
            y = gna * vec_ref[layer, 0:1, at] + gnm * vec_ref[layer, 1:2, at]
            put_pieces(at, y, refs)
            for i, a in enumerate((gna * u, gnm * u, gna, gnm)):
                sum_ref[i : i + 1, at] = sum_rows(a)
            return carry

        lax.fori_loop(0, width // TILE, step, 0)

    out = call_once(
        body,
        (*pinned(dq, own, from_core), from_y, tables, *pinned(gh), w[0], x, stats, vec, part),
        [shape((rows, 3 * HD), BF16)] + piece_shapes(rows, width) + [shape((8, width), F32)],
        tiles_scratch(runs, width)
        + [pltpu.VMEM((width // TILE, rows, TILE), BF16), pltpu.SemaphoreType.DMA((width // TILE,))],
        hbm=(6, 7),
        flops=2 * rows * width * (3 * HD + hidden),
    )
    return out[0], out[1:7], out[7]


def put_rows(like, row_at, rows_in, pieces, others, value):
    seqs, per, width = like.shape
    rows = seqs * per
    n = len(rows_in)

    def body(row_ref, *rest):
        refs = rest[: n + 6 + len(others)]
        out_ref, own, sems = rest[len(refs) : len(refs) + 3]
        rest = rest[len(refs) + 3 :]
        loads = [Rows([refs[i]], rest[2 * i], rest[2 * i + 1]) for i in range(n)]
        ps = Rows(refs[n : n + 6], rest[2 * n], rest[2 * n + 1])
        start_rows(*loads, ps)
        copies = row_copies(out_ref, row_ref, own, sems, back=True)

        def step(i, branch, carry):
            at = span(i, CHUNK)
            chunks = [load.scratch[at, :] for load in loads]
            own[at, :] = value(chunks, branch, at, refs[n + 6 :])
            copies(i).start()
            return carry

        for_rows(ps, loads, step)

        def finish(i, carry):
            copies(i).wait()
            return carry

        for_chunks(rows // CHUNK, finish)

    return call_once(
        body,
        (row_at, *rows_in, *pieces, *others),
        [shape((seqs, per, width), F32)],
        [pltpu.VMEM((rows, width), F32), pltpu.SemaphoreType.DMA((rows // CHUNK,))]
        + rows_scratch(rows, width, n + 1),
        prefetch=1,
        hbm=tuple(range(1, n + 7)),
        out_hbm=True,
    )[0]


def last_stream(like, row_at, x, pieces, vec, layer):
    def value(chunks, branch, at, others):
        return chunks[0].astype(F32) + branch + others[0][layer, 4:5]

    return put_rows(like, row_at, (x,), pieces, (vec,), value)


def last_grad(like, row_at, g, x, stats, pieces):
    def value(chunks, branch, at, others):
        return grad_in(chunks[0], chunks[1], others[0][at, :], branch)

    return put_rows(like, row_at, (g, x), pieces, (stats,), value)


def pack_panels(layer, *parts):
    depth = parts[0].shape[1]
    panels = [(i, c) for i, a in enumerate(parts) for c in range(a.shape[2] // TILE)]

    def body(*refs):
        out_ref, sems = refs[-2:]
        copies = [
            pltpu.make_async_copy(
                refs[i].at[layer, :, c * TILE : (c + 1) * TILE], out_ref.at[p], sems.at[p]
            )
            for p, (i, c) in enumerate(panels)
        ]
        start(copies)
        wait(copies)

    return call_once(
        body,
        parts,
        [shape((len(panels), depth, TILE), BF16)],
        [pltpu.SemaphoreType.DMA((len(panels),))],
        hbm=tuple(range(len(parts))),
    )[0]


def turn(x, tables, sign):
    head = x[:, :LANES]
    half = ROT // 2
    up = pltpu.roll(head, LANES - half, 1)
    down = pltpu.roll(head, half, 1)
    head = head * tables[0] + sign * (down * tables[2] - up * tables[1])
    return jnp.concatenate([head, x[:, LANES:]], axis=1)


def add_up(*parts):
    def body(*refs):
        total = refs[0][...].astype(F32)
        for ref in refs[1:-1]:
            total = total + ref[...].astype(F32)
        refs[-1][...] = total.astype(BF16)

    return call_once(body, pinned(*parts), [shape(parts[0].shape, BF16)])[0]


def add_split(a, b):
    rows, width = a.shape
    n = rows // 4

    def body(a_ref, b_ref, *outs):
        for i, ref in enumerate(outs):
            at = slice(i * n, (i + 1) * n)
            ref[...] = (a_ref[at].astype(F32) + b_ref[at].astype(F32)).astype(BF16)

    return call_once(body, pinned(a, b), [shape((n, width), BF16)] * 4)


def stack_up(*parts):
    n, width = parts[0].shape

    def body(*refs):
        for i, ref in enumerate(refs[:-1]):
            refs[-1][i * n : (i + 1) * n] = ref[...]

    return call_once(body, pinned(*parts), [shape((n * len(parts), width), BF16)])[0]


def add_late(a, b):
    rows = a.shape[0]

    def body(a_ref, b_ref, out_ref):
        out_ref[...] = (a_ref[...] + b_ref[...].astype(F32)).astype(BF16)

    return call(
        body,
        (1,),
        (a, b),
        [whole(a), pl.BlockSpec((rows, b.shape[1]), lambda *_: (b.shape[0] // rows - 1, 0))],
        [shape(a.shape, BF16)],
        [whole(a)],
    )[0]


def weight_grad(x, ys, blocks, got=None):
    rows, width = x.shape
    cols = [a.shape[1] for a in ys]
    total = sum(cols)
    size = width // 16
    tiles = blocks.shape[0] // 2

    def body(block_ref, x_ref, *rest):
        y_refs = rest[: len(ys)]
        out_ref, xs, sems = rest[-3:]
        j = pl.program_id(0)

        def copy(i):
            at = pl.multiple_of(block_ref[i] * size, size)
            return pltpu.make_async_copy(x_ref.at[:, pl.ds(at, size)], xs.at[i], sems.at[i])

        @pl.when(j == 0)
        def _():
            for i in range(2 * tiles):
                copy(i).start()

        copy(2 * j).wait()
        copy(2 * j + 1).wait()
        left = jnp.concatenate([xs[2 * j], xs[2 * j + 1]], axis=1)
        at = 0
        for ref, n in zip(y_refs, cols):
            y = dot_tn(left, ref[...])
            if got is not None:
                y = y + rest[len(ys)][:, at : at + n].astype(F32)
            out_ref[:, at : at + n] = y.astype(BF16)
            at += n

    ins = (blocks, *pinned(x), *ys)
    specs = [pl.BlockSpec(memory_space=pltpu.HBM)] + [whole(a) for a in ys]
    if got is not None:
        ins += (got,)
        specs += [pl.BlockSpec((2 * size, total), lambda j, *_: (j, 0))]
    return call(
        body,
        (tiles,),
        ins,
        specs,
        [shape((width // 2, total), BF16)],
        [pl.BlockSpec((2 * size, total), lambda j, *_: (j, 0))],
        scratch=[pltpu.VMEM((2 * tiles, rows, size), BF16), pltpu.SemaphoreType.DMA((2 * tiles,))],
        prefetch=1,
        flops=2 * rows * (width // 2) * total,
    )[0]


def scatter_weight_grad(value):
    return lax.psum_scatter(value, "fsdp", scatter_dimension=0, tiled=True)


def swap_half(value):
    return swap_y(value[value.shape[0] // 2 :])


def finish_weight_grads(layers, cols):
    flat = [a for layer in layers for a in layer]
    depth = layers[0][0].shape[0] // 2
    outs = [shape((len(layers), depth, n), F32) for n in cols]

    def body(*refs):
        qkv_ref, dense_ref, up_ref, down_ref = refs[len(flat) :]
        for l in range(len(layers)):
            ins = refs[6 * l : 6 * l + 6]
            out, up, qkv = (
                ins[i][:depth].astype(F32) + ins[3 + i][...].astype(F32) for i in range(3)
            )
            qkv_ref[l] = qkv
            dense_ref[l] = out[:, :HD]
            up_ref[l] = up
            down_ref[l] = out[:, HD:]

    return call_once(body, pinned(*flat), outs)


def body(
    tokens,
    block_order,
    cotangent,
    qkv_weight,
    qkv_bias,
    dense_weight,
    up_weight,
    up_bias,
    down_weight,
    norm_gains,
    norm_shifts,
    out_bias,
):
    seqs, per, width = tokens.shape
    block = 128
    c, t = lax.axis_index("ctx"), lax.axis_index("tp")
    y_hi, z = t // 4, t % 4

    b = jnp.arange(8, dtype=jnp.int32)
    near = (b // 2) * 4 + (c ^ (2 * (b % 2)))
    far = near ^ 1
    row_at = jnp.concatenate(
        [2 * ((z + b // 2) % 4) + b % 2, (y_hi ^ (b // 4)) * 4 + (z + b) % 4]
    )

    row = row_at[:, None] * CHUNK + jnp.arange(CHUNK, dtype=jnp.int32)[None, :]
    row = row.reshape(seqs, per)
    slots = jnp.arange(block_order.shape[0], dtype=jnp.int32)

    def positions(owner):
        slot = 2 * owner + row // block
        here = slot[:, :, None] == slots
        return jnp.sum(jnp.where(here, block_order, 0), axis=2) * block + row % block

    qpos = positions(c).reshape(seqs * per, 1)
    kpos = jnp.concatenate([positions(c ^ i) for i in range(4)], axis=1)
    inverse = 10000.0 ** (-(jnp.arange(ROT // 2, dtype=F32) * 2.0) / ROT)
    angles = qpos.astype(F32) * inverse[None, :]
    cosine, sine = jnp.cos(angles), jnp.sin(angles)
    none = jnp.zeros_like(sine)
    rest = jnp.zeros((seqs * per, LANES - ROT), F32)
    tables = jnp.stack(
        [
            jnp.concatenate([cosine, cosine, rest + 1.0], axis=1),
            jnp.concatenate([sine, none, rest], axis=1),
            jnp.concatenate([none, sine, rest], axis=1),
        ]
    )

    vec = jnp.concatenate(
        [
            norm_gains,
            norm_shifts,
            out_bias[:, None],
            jnp.zeros((LAYERS, 3, width), BF16),
        ],
        axis=1,
    ).astype(F32)
    weights = (qkv_weight, dense_weight, up_weight, down_weight)
    qkv_b = qkv_bias.astype(F32)
    up_b = up_bias.astype(F32)

    kept = []
    rows = seqs * per
    w_all = gather_weights(pack_panels(0, *weights))
    w_all, vec, tables, qpos, kpos, near, far = together(w_all, vec, tables, qpos, kpos, near, far)
    w_in, w_out = (w_all, ALL_PANELS[0], ALL_PANELS[2]), (w_all, ALL_PANELS[1], ALL_PANELS[3])
    sums = None
    for l in range(LAYERS):
        bias = qkv_b[l : l + 1]
        if l == 0:
            new = first_in(tokens, row_at, vec, w_in, bias, tables)
        else:
            new = next_in(kept[-1][2], sums, l, vec, w_in, bias, tables)
        x, stats, na, nm, q, kv = new
        kv_y, kv_core = swap_y(kv), swap_core(kv)
        active, slope = project_up(nm, w_in, up_b[l : l + 1])
        kv_y, active = together(kv_y, active)
        kvs = [kv, kv_core, kv_y, swap_core(kv_y)]
        mixed, terms = attend_out(q, kvs, qpos, kpos, active, w_out)
        held, moving = tp_1(terms)
        kept.append((w_in, w_out, x, stats, na, nm, q, kvs, mixed, active, slope, terms))
        if l < LAYERS - 1:
            shard, _ = together(pack_panels(l + 1, qkv_weight, up_weight), kv_y)
            w_in = (gather_weights(shard), *IN_PANELS)
            held, moving = tp_2(held, together(*moving))
            shard, moving = together(pack_panels(l + 1, dense_weight, down_weight), moving)
            (first, second), (firsts, seconds) = tp_3(held, moving)
            seconds, first = together(seconds, first)
            sums = tp_pieces(first, firsts, *tp_4(second, seconds))
            w_out = (gather_weights(shard), *OUT_PANELS)

    late, late_moving = held, moving
    small = [None] * LAYERS
    scattered = [None] * LAYERS
    g = None
    for l in reversed(range(LAYERS)):
        last = l == LAYERS - 1
        w_in, w_out, x, stats, na, nm, q, kvs, mixed, active, slope, terms = kept[l]
        if last:
            slope, _ = together(slope, terms)
            g, gm, gh, part = last_back_out(cotangent, row_at, w_out, slope)
            late_moving, gm = together(late_moving, gm)
            late, late_moving = tp_2(late, late_moving)
        else:
            after = kept[l + 1]
            g, gm, gh, part = next_back_out(g, after[2], after[3], sums, w_out, slope)
        dq, own, to_y, send = attend_back(q, kvs, gm, qpos, kpos)
        from_core = swap_core(send)
        out_far = weight_grad(g, pinned(mixed, active), far)
        if last:
            late_moving, out_far = together(late_moving, out_far)
        else:
            late_first, late_second = tp_3_sums(late, late_moving)
            late_seconds = [from_z(late_second, k) for k in (1, 3, 2)]
            late_seconds, out_far = together(late_seconds, out_far)
            late_near, late_far = tp_4(late_second, late_seconds)
            late_firsts = [from_z(late_first, k) for k in (1, 3, 2)]
        from_core, out_far = together(from_core, out_far)
        from_y = swap_y(add_late(to_y, from_core))
        out_got = swap_core(out_far)
        up_far = weight_grad(nm, pinned(gh), far)
        out_got, up_far = together(out_got, up_far)
        out_near = weight_grad(g, pinned(mixed, active), near, out_got)
        up_got, out_near = together(swap_core(up_far), out_near)
        up_near = weight_grad(nm, pinned(gh), near, up_got)
        if last:
            from_y, out_near, up_near = together(from_y, out_near, up_near)
        else:
            from_y, out_near, up_near, qkv_after = together(
                from_y, out_near, up_near, scattered[l + 1][2]
            )
            scattered[l + 1] = (*scattered[l + 1][:2], qkv_after)
        out_sum = scatter_weight_grad(out_near)
        gp, terms, small[l] = back_in(
            dq, own, from_core, from_y, tables, gh, w_in, x, stats, vec, l, part
        )
        if not last:
            late_firsts, late_far, gp = together(late_firsts, late_far, gp)
        held, moving = tp_1(terms)
        up_sum = scatter_weight_grad(up_near)
        qkv_far = weight_grad(na, (gp,), far)
        moving, qkv_far, out_sum = together(moving, qkv_far, out_sum)
        held, moving = tp_2(held, moving)
        qkv_got = swap_core(qkv_far)
        if last:
            moving, qkv_got = together(moving, qkv_got)
        else:
            total = jnp.stack(small)
            parts = around_ctx(total)
            moving, qkv_got, parts = together(moving, qkv_got, parts)
        first, second = tp_3_sums(held, moving)
        second, first, qkv_got = together(second, first, qkv_got)
        seconds = [from_z(second, k) for k in (1, 3, 2)]
        firsts = [from_z(first, k) for k in (1, 3, 2)]
        qkv_near = weight_grad(na, (gp,), near, qkv_got)
        qkv_sum = scatter_weight_grad(qkv_near)
        if last:
            seconds, qkv_near, up_sum = together(seconds, qkv_near, up_sum)
            sums = tp_pieces(first, firsts, *tp_4(second, seconds))
        else:
            total = pair_up(total, parts)
            parts = around(total, from_x)
            seconds, qkv_near, parts = together(seconds, qkv_near, parts)
            sum_near, sum_far = tp_4(second, seconds)
            total = pair_up(total, parts)
            wide = total[:, :4]
            parts = around(wide, from_z)
            late_pieces = tp_pieces(late_first, late_firsts, late_near, late_far)
            activations = last_stream(tokens, row_at, kept[-1][2], late_pieces, vec, LAYERS - 1)
            sum_far, firsts, parts, activations = together(sum_far, firsts, parts, activations)
            wide = pair_up(wide, parts)
            wide = wide + swap_tp(wide, 4)
            sums = tp_pieces(first, firsts, sum_near, sum_far)
        scattered[l] = (out_sum, up_sum, qkv_sum)
    halves = [[swap_half(a) for a in layer] for layer in scattered]
    input_grad = last_grad(tokens, row_at, g, kept[0][2], kept[0][3], sums)
    input_grad, halves = together(input_grad, halves)
    qkv_grad, dense_grad, up_grad, down_grad = finish_weight_grads(
        [(*scattered[l], *halves[l]) for l in range(LAYERS)],
        [a.shape[2] for a in weights],
    )
    return (
        activations,
        input_grad,
        qkv_grad,
        total[:, 5, : qkv_bias.shape[1]],
        dense_grad,
        up_grad,
        total[:, 6, : up_bias.shape[1]],
        down_grad,
        wide[:, 0:2],
        wide[:, 2:4],
        total[:, 4],
    )


def solution(mesh):
    weight = P(None, ("fsdp", "ctx"), "tp")
    stream = P("fsdp", "ctx", None)
    bias = P(None, "tp")
    return jax.shard_map(
        body,
        mesh=mesh,
        in_specs=(
            stream,
            P(),
            stream,
            weight,
            bias,
            weight,
            weight,
            bias,
            weight,
            P(),
            P(),
            P(),
        ),
        out_specs=(
            stream,
            stream,
            weight,
            bias,
            weight,
            weight,
            bias,
            weight,
            P(),
            P(),
            P(),
        ),
        check_vma=False,
    )
```

```python
import jax
import jax.numpy as jnp
from jax import lax
from jax.experimental import pallas as pl
from jax.experimental.pallas import tpu as pltpu
from jax.sharding import PartitionSpec as P

HD = 256
ROT = 64
LAYERS = 2
EPSILON = 1e-05
LANES = 128
TILE = 256
CHUNK = 32
IN_PANELS, OUT_PANELS = (0, 3), (0, 1)
F32 = jnp.float32
BF16 = jnp.bfloat16
VMEM_LIMIT = 24 * 1024 * 1024


def swap_core(value):
    return lax.ppermute(value, "ctx", [(i, i ^ 1) for i in range(4)])


def swap_y(value):
    return lax.ppermute(value, "ctx", [(i, i ^ 2) for i in range(4)])


def from_x(value, k):
    return lax.ppermute(value, "fsdp", [((i + k) % 4, i) for i in range(4)])


def swap_both(value):
    return lax.ppermute(value, "ctx", [(i, i ^ 3) for i in range(4)])


def swap_tp(value, k):
    return lax.ppermute(value, "tp", [(i, i ^ k) for i in range(8)])


def from_z(value, k):
    return lax.ppermute(value, "tp", [((i & 4) + (i + k) % 4, i) for i in range(8)])


def to_z(value, k):
    return lax.ppermute(value, "tp", [(i, (i & 4) + (i + k) % 4) for i in range(8)])


def gather_weights(shard):
    return lax.all_gather(shard, ("fsdp", "ctx"), axis=1, tiled=True)


def together(*values):
    return lax.optimization_barrier(values)


def tp_1(pieces):
    firsts = [to_z(pieces[k], k) for k in (1, 3, 2)]
    return (pieces[0], pieces[4]), (firsts, swap_tp(pieces[5], 4))


def tp_2(kept, arrived):
    (own, near), (firsts, far) = kept, arrived
    first = add_up(own, *firsts)
    parts = add_split(near, far)
    seconds = [to_z(parts[k], k) for k in (1, 3, 2)]
    return (first, parts[0]), (swap_tp(first, 4), seconds)


def tp_3_sums(kept, arrived):
    (first, own), (other, seconds) = kept, arrived
    second = add_up(own, *seconds)
    return add_up(first, other), second


def tp_3(kept, arrived):
    first, second = tp_3_sums(kept, arrived)
    seconds = [from_z(second, k) for k in (1, 3, 2)]
    firsts = [from_z(first, k) for k in (1, 3, 2)]
    return (first, second), (firsts, seconds)


def tp_4(second, seconds):
    near = stack_up(second, seconds[0], seconds[2], seconds[1])
    return near, swap_tp(near, 4)


def tp_pieces(first, firsts, near, far):
    return (first, firsts[0], firsts[2], firsts[1], near, far)


def around(value, move):
    return [move(value, k) for k in (1, 2, 3)]


def around_ctx(value):
    return [swap_y(value), swap_core(value), swap_both(value)]


def pair_up(value, got):
    return (value + got[1]) + (got[0] + got[2])


def call(body, grid, ins, in_specs, outs, out_specs, scratch=(), prefetch=0, flops=0):
    nbytes = sum(a.size * a.dtype.itemsize for a in outs)
    nbytes += sum(min(a.size * a.dtype.itemsize, 1 << 22) for a in ins)
    return pl.pallas_call(
        body,
        grid_spec=pltpu.PrefetchScalarGridSpec(
            num_scalar_prefetch=prefetch,
            grid=grid,
            in_specs=in_specs,
            out_specs=out_specs,
            scratch_shapes=scratch,
        ),
        out_shape=outs,
        compiler_params=pltpu.CompilerParams(vmem_limit_bytes=VMEM_LIMIT),
        cost_estimate=pl.CostEstimate(
            flops=int(flops), bytes_accessed=int(nbytes), transcendentals=0
        ),
    )(*ins)


def call_once(body, ins, outs, scratch=(), prefetch=0, hbm=(), out_hbm=False, flops=0):
    ins = tuple(
        pltpu.with_memory_space_constraint(a, pltpu.HBM) if i in hbm else a
        for i, a in enumerate(ins)
    )
    specs = [
        pl.BlockSpec(memory_space=pltpu.HBM) if i in hbm else whole(a)
        for i, a in enumerate(ins)
        if i >= prefetch
    ]
    out_specs = [pl.BlockSpec(memory_space=pltpu.HBM) if out_hbm else whole(a) for a in outs]
    return call(body, (1,), ins, specs, outs, out_specs, scratch, prefetch, flops)


def pinned(*arrays):
    return tuple(pltpu.with_memory_space_constraint(a, pltpu.HBM) for a in arrays)


def shape(dims, dtype):
    return jax.ShapeDtypeStruct(dims, dtype)


def whole(a):
    return pl.BlockSpec(a.shape, lambda *_: (0,) * len(a.shape))


def dot_nn(a, b):
    return lax.dot_general(a, b, (((1,), (0,)), ((), ())), preferred_element_type=F32)


def dot_nt(a, b):
    return lax.dot_general(a, b, (((1,), (1,)), ((), ())), preferred_element_type=F32)


def dot_tn(a, b):
    return lax.dot_general(a, b, (((0,), (0,)), ((), ())), preferred_element_type=F32)


def fold_rows(a):
    return jnp.sum(a.reshape(a.shape[0] // 8, 8, a.shape[1]), axis=0)


def sum_rows(a):
    return jnp.sum(a, axis=0, keepdims=True)


def span(j, size):
    return pl.ds(pl.multiple_of(j * size, size), size)


def start(copies):
    for copy in copies:
        copy.start()


def wait(copies):
    for copy in copies:
        copy.wait()


def load_panels(w_ref, first, scratch, sems, at=0):
    return [
        pltpu.make_async_copy(w_ref.at[first + i], scratch.at[at + i], sems.at[at + i])
        for i in range(scratch.shape[0] - at)
    ]


def panels_scratch(n, width):
    return [pltpu.VMEM((n, width, TILE), BF16), pltpu.SemaphoreType.DMA((n,))]


class Tiles:
    def __init__(self, w_ref, runs, scratch, sems):
        self.w_ref, self.runs, self.scratch, self.sems = w_ref, runs, scratch, sems

    def copies(self, j):
        at = 0
        for i, (first, n) in enumerate(self.runs):
            yield pltpu.make_async_copy(
                self.w_ref.at[first : first + n, span(j, TILE), :],
                self.scratch.at[j, at : at + n],
                self.sems.at[i, j],
            )
            at += n

    def start(self):
        def step(j, carry):
            start(self.copies(j))
            return carry

        lax.fori_loop(0, self.scratch.shape[0], step, 0)

    def get(self, j):
        wait(self.copies(j))
        n = self.scratch.shape[1]
        return [self.scratch[j, i] for i in range(n)]


def tiles_scratch(runs, width):
    n = sum(size for _, size in runs)
    return [
        pltpu.VMEM((width // TILE, n, TILE, TILE), BF16),
        pltpu.SemaphoreType.DMA((len(runs), width // TILE)),
    ]


def row_copies(source, row_ref, target, sems, back=False):
    per = source.shape[1] // CHUNK

    def copy(k):
        far = source.at[k // per, span(row_ref[k], CHUNK)]
        own = target.at[span(k, CHUNK)]
        ends = (own, far) if back else (far, own)
        return pltpu.make_async_copy(*ends, sems.at[k])

    return copy


def for_chunks(n, step, carry=0):
    return lax.fori_loop(0, n, step, carry)


class Rows:
    def __init__(self, refs, scratch, sems):
        self.scratch, self.sems = scratch, sems
        self.parts, base = [], 0
        for ref in refs:
            self.parts.append((ref, base, ref.shape[0] // CHUNK))
            base += ref.shape[0] // CHUNK

    def copy(self, part, i):
        ref, base, _ = part
        return pltpu.make_async_copy(
            ref.at[span(i, CHUNK)], self.scratch.at[span(base + i, CHUNK)], self.sems.at[base + i]
        )


def start_rows(*rows):
    order = [(base + i, r, (ref, base, n), i) for r in rows for ref, base, n in r.parts for i in range(n)]
    for _, r, part, i in sorted(order, key=lambda entry: entry[0]):
        r.copy(part, i).start()


def for_rows(pieces, others, fn, carry=0):
    for part in pieces.parts:

        def step(i, carry, part=part):
            pieces.copy(part, i).wait()
            for other in others:
                other.copy(other.parts[0], part[1] + i).wait()
            at = span(part[1] + i, CHUNK)
            return fn(part[1] + i, pieces.scratch[at, :].astype(F32), carry)

        carry = lax.fori_loop(0, part[2], step, carry)
    return carry


def rows_scratch(rows, width, n=1):
    one = [pltpu.VMEM((rows, width), BF16), pltpu.SemaphoreType.DMA((rows // CHUNK,))]
    return one * n


def piece_shapes(rows, width):
    return [shape((rows // 8, width), BF16)] * 4 + [shape((rows // 4, width), BF16)] * 2


def put_pieces(at, y, refs):
    base = 0
    for ref in refs:
        ref[:, at] = y[base : base + ref.shape[0]].astype(BF16)
        base += ref.shape[0]


def put_norms(at, x, vec_ref, layer, stat_ref, na_ref, nm_ref):
    mean = jnp.mean(x, axis=1, keepdims=True)
    center = x - mean
    r = lax.rsqrt(jnp.mean(center * center, axis=1, keepdims=True) + EPSILON)
    u = center * r
    lane = lax.broadcasted_iota(jnp.int32, (x.shape[0], LANES), 1)
    stat_ref[at, :] = jnp.where(lane < LANES // 2, mean, r)
    na_ref[at, :] = (u * vec_ref[layer, 0:1] + vec_ref[layer, 2:3]).astype(BF16)
    nm_ref[at, :] = (u * vec_ref[layer, 1:2] + vec_ref[layer, 3:4]).astype(BF16)


def unit_of(x, stats):
    return (x.astype(F32) - stats[:, 0:1]) * stats[:, LANES // 2 : LANES // 2 + 1]


def put_qkv(na_ref, loads, w_ref, b_ref, t_ref, q_ref, kv_ref):
    for j in range(3):
        loads[j].wait()
        y = dot_nn(na_ref[...], w_ref[j]) + b_ref[:, j * HD : (j + 1) * HD]
        if j == 0:
            q_ref[...] = turn(y, t_ref, 1.0).astype(BF16)
        elif j == 1:
            kv_ref[:, :HD] = turn(y, t_ref, 1.0).astype(BF16)
        else:
            kv_ref[:, HD:] = y.astype(BF16)


def in_outs(rows, width):
    return [
        shape((rows, width), BF16),
        shape((rows, LANES), F32),
        shape((rows, width), BF16),
        shape((rows, width), BF16),
        shape((rows, HD), BF16),
        shape((rows, 2 * HD), BF16),
    ]


def first_in(tokens, row_at, vec, w, bias, tables):
    width = tokens.shape[2]
    rows = tokens.shape[0] * tokens.shape[1]

    def body(
        row_ref,
        tok_ref,
        vec_ref,
        w_ref,
        b_ref,
        t_ref,
        x_ref,
        stat_ref,
        na_ref,
        nm_ref,
        q_ref,
        kv_ref,
        panels,
        sems,
        row_sems,
    ):
        news = row_copies(tok_ref, row_ref, x_ref, row_sems)
        for k in range(rows // CHUNK):
            news(k).start()
        loads = load_panels(w_ref, w[1], panels, sems)
        start(loads)

        def step(i, carry):
            news(i).wait()
            at = span(i, CHUNK)
            put_norms(at, x_ref[at, :].astype(F32), vec_ref, 0, stat_ref, na_ref, nm_ref)
            return carry

        for_chunks(rows // CHUNK, step)
        put_qkv(na_ref, loads, panels, b_ref, t_ref, q_ref, kv_ref)

    return call_once(
        body,
        (row_at, tokens, vec, w[0], bias, tables),
        in_outs(rows, width),
        panels_scratch(3, width) + [pltpu.SemaphoreType.DMA((rows // CHUNK,))],
        prefetch=1,
        hbm=(1, 3),
        flops=2 * rows * width * 3 * HD,
    )


def next_in(x, pieces, layer, vec, w, bias, tables):
    rows, width = x.shape

    def body(x_ref, *rest):
        refs = rest[:6]
        vec_ref, w_ref, b_ref, t_ref, new_ref, stat_ref, na_ref, nm_ref = rest[6:14]
        q_ref, kv_ref, panels, sems, xs, x_sems, ps, p_sems = rest[14:]
        xs, ps = Rows([x_ref], xs, x_sems), Rows(refs, ps, p_sems)
        start_rows(xs, ps)
        loads = load_panels(w_ref, w[1], panels, sems)
        start(loads)

        def step(i, branch, carry):
            at = span(i, CHUNK)
            new = xs.scratch[at, :].astype(F32) + branch + vec_ref[layer - 1, 4:5]
            new_ref[at, :] = new.astype(BF16)
            put_norms(at, new, vec_ref, layer, stat_ref, na_ref, nm_ref)
            return carry

        for_rows(ps, [xs], step)
        put_qkv(na_ref, loads, panels, b_ref, t_ref, q_ref, kv_ref)

    return call_once(
        body,
        (x, *pieces, vec, w[0], bias, tables),
        in_outs(rows, width),
        panels_scratch(3, width) + rows_scratch(rows, width, 2),
        hbm=(0, 1, 2, 3, 4, 5, 6, 8),
        flops=2 * rows * width * 3 * HD,
    )


def gelu_parts(h):
    e = jnp.exp(-0.5 * h * h)
    t = 1.0 / (1.0 + (0.3275911 * 0.5**0.5) * jnp.abs(h))
    tail = 1.061405429 * t - 1.453152027
    tail = tail * t + 1.421413741
    tail = tail * t - 0.284496736
    tail = (tail * t + 0.254829592) * t * (0.5 * e)
    return jnp.where(h >= 0, 1.0 - tail, tail), e * 0.3989422804014327


def project_up(nm, w, bias):
    rows, width = nm.shape
    hidden = bias.shape[1]

    def body(n_ref, w_ref, b_ref, act_ref, slope_ref, panels, sems):
        loads = load_panels(w_ref, w[2], panels, sems)
        start(loads)
        for j in range(hidden // TILE):
            at = slice(j * TILE, (j + 1) * TILE)
            loads[j].wait()
            h = dot_nn(n_ref[...], panels[j]) + b_ref[:, at]
            cdf, density = gelu_parts(h)
            act_ref[:, at] = (h * cdf).astype(BF16)
            slope_ref[:, at] = (cdf + h * density).astype(BF16)

    return call_once(
        body,
        (nm, w[0], bias),
        [shape((rows, hidden), BF16), shape((rows, hidden), BF16)],
        panels_scratch(hidden // TILE, width),
        hbm=(1,),
        flops=2 * rows * width * hidden,
    )


def weights_of(q, kvs, qpos, kpos):
    scores = [dot_nt(q, kv[:, :HD]) * HD**-0.5 for kv in kvs]
    scores = jnp.concatenate(scores, axis=1)
    scores = jnp.where(kpos <= qpos, scores, -1e30)
    e = jnp.exp(scores - jnp.max(scores, axis=1, keepdims=True))
    return e / jnp.sum(e, axis=1, keepdims=True)


def attend_out(q, kvs, qpos, kpos, active, w):
    rows, hidden = active.shape
    width = w[0].shape[1]
    seqs = kpos.shape[0]
    per = rows // seqs
    runs = [(w[1], 1), (w[2], hidden // TILE)]

    def body(q_ref, k0, k1, k2, k3, qp_ref, kp_ref, act_ref, w_ref, mixed_ref, *rest):
        refs = rest[:6]
        wide, sems, left = rest[6:]
        tiles = Tiles(w_ref, runs, wide, sems)
        tiles.start()
        for s in range(seqs):
            at = slice(s * per, (s + 1) * per)
            kvs = [ref[at] for ref in (k0, k1, k2, k3)]
            p = weights_of(q_ref[at], kvs, qp_ref[at], kp_ref[s : s + 1]).astype(BF16)
            mixed = sum(dot_nn(p[:, i * per : (i + 1) * per], kvs[i][:, HD:]) for i in range(4))
            mixed_ref[at] = mixed.astype(BF16)
        left[:, :HD] = mixed_ref[...]
        left[:, HD:] = act_ref[...]

        def step(j, carry):
            y = dot_nt(left[...], jnp.concatenate(tiles.get(j), axis=1))
            put_pieces(span(j, TILE), y, refs)
            return carry

        lax.fori_loop(0, width // TILE, step, 0)

    out = call_once(
        body,
        (q, *kvs, qpos, kpos, active, w[0]),
        [shape((rows, HD), BF16)] + piece_shapes(rows, width),
        tiles_scratch(runs, width) + [pltpu.VMEM((rows, HD + hidden), BF16)],
        hbm=(8,),
        flops=16 * rows * per * HD + 2 * rows * width * (HD + hidden),
    )
    return out[0], out[1:]


def put_back_out(gb_ref, loads, panels, slope_ref, gm_ref, gh_ref, part_ref):
    for j in range(panels.shape[0]):
        loads[j].wait()
        y = dot_nn(gb_ref[...], panels[j])
        if j == 0:
            gm_ref[...] = y.astype(BF16)
        else:
            at = slice((j - 1) * TILE, j * TILE)
            gh = (y * slope_ref[:, at].astype(F32)).astype(BF16)
            gh_ref[:, at] = gh
            part_ref[6:7, at] = sum_rows(gh.astype(F32))


def load_back_out(w_ref, w, panels, sems):
    first = pltpu.make_async_copy(w_ref.at[w[1]], panels.at[0], sems.at[0])
    return [first] + load_panels(w_ref, w[2], panels, sems, at=1)


def back_out_shapes(rows, width, hidden):
    return [
        shape((rows, width), BF16),
        shape((rows, HD), BF16),
        shape((rows, hidden), BF16),
        shape((8, width), F32),
    ]


def last_back_out(cotangent, row_at, w, slope):
    width = cotangent.shape[2]
    rows, hidden = slope.shape
    n = 1 + hidden // TILE

    def body(
        row_ref, cot_ref, w_ref, slope_ref, gb_ref, gm_ref, gh_ref, part_ref, panels, sems, row_sems
    ):
        news = row_copies(cot_ref, row_ref, gb_ref, row_sems)
        for k in range(rows // CHUNK):
            news(k).start()
        loads = load_back_out(w_ref, w, panels, sems)
        start(loads)
        part_ref[...] = jnp.zeros_like(part_ref)

        def step(i, total):
            news(i).wait()
            return total + fold_rows(gb_ref[span(i, CHUNK), :].astype(F32))

        total = for_chunks(rows // CHUNK, step, jnp.zeros((8, width), F32))
        part_ref[4:5, :] = sum_rows(total)
        put_back_out(gb_ref, loads, panels, slope_ref, gm_ref, gh_ref, part_ref)

    return call_once(
        body,
        (row_at, cotangent, w[0], *pinned(slope)),
        back_out_shapes(rows, width, hidden),
        panels_scratch(n, width) + [pltpu.SemaphoreType.DMA((rows // CHUNK,))],
        prefetch=1,
        hbm=(1, 2),
        flops=2 * rows * width * n * TILE,
    )


def grad_in(g, x, stats, total):
    u = unit_of(x, stats)
    back = total - jnp.mean(total, axis=1, keepdims=True)
    back = back - u * jnp.mean(total * u, axis=1, keepdims=True)
    return g.astype(F32) + stats[:, LANES // 2 : LANES // 2 + 1] * back


def next_back_out(g, x, stats, pieces, w, slope):
    rows, width = g.shape
    hidden = slope.shape[1]
    n = 1 + hidden // TILE

    def body(g_ref, x_ref, stat_ref, *rest):
        refs = rest[:6]
        w_ref, slope_ref, gb_ref, gm_ref, gh_ref, part_ref, panels, sems = rest[6:14]
        gs, xs, ps = (
            Rows(r, rest[14 + 2 * i], rest[15 + 2 * i])
            for i, r in enumerate(([g_ref], [x_ref], refs))
        )
        start_rows(gs, xs, ps)
        loads = load_back_out(w_ref, w, panels, sems)
        start(loads)
        part_ref[...] = jnp.zeros_like(part_ref)

        def step(i, branch, total):
            at = span(i, CHUNK)
            new = grad_in(gs.scratch[at, :], xs.scratch[at, :], stat_ref[at, :], branch)
            gb_ref[at, :] = new.astype(BF16)
            return total + fold_rows(new)

        total = for_rows(ps, [gs, xs], step, jnp.zeros((8, width), F32))
        part_ref[4:5, :] = sum_rows(total)
        put_back_out(gb_ref, loads, panels, slope_ref, gm_ref, gh_ref, part_ref)

    return call_once(
        body,
        (g, x, stats, *pieces, w[0], *pinned(slope)),
        back_out_shapes(rows, width, hidden),
        panels_scratch(n, width) + rows_scratch(rows, width, 3),
        hbm=(0, 1, 3, 4, 5, 6, 7, 8, 9),
        flops=2 * rows * width * n * TILE,
    )


def attend_back(q, kvs, gm, qpos, kpos):
    rows = q.shape[0]
    seqs = kpos.shape[0]
    per = rows // seqs

    def body(q_ref, k0, k1, k2, k3, gm_ref, qp_ref, kp_ref, dq_ref, own_ref, y_ref, send_ref):
        part = [slice(i * per, (i + 1) * per) for i in range(4)]
        for s in range(seqs):
            at = part[s]
            kvs = [ref[at] for ref in (k0, k1, k2, k3)]
            q = q_ref[at]
            gm = gm_ref[at]
            p = weights_of(q, kvs, qp_ref[at], kp_ref[s : s + 1])
            dp = jnp.concatenate([dot_nt(gm, kv[:, HD:]) for kv in kvs], axis=1)
            ds = (p * (dp - jnp.sum(p * dp, axis=1, keepdims=True))).astype(BF16)
            p = p.astype(BF16)
            dq = sum(dot_nn(ds[:, part[i]], kvs[i][:, :HD]) for i in range(4))
            dq_ref[at] = dq * HD**-0.5
            late = slice(rows + s * per, rows + (s + 1) * per)
            places = (own_ref.at[at], send_ref.at[at], y_ref.at[at], send_ref.at[late])
            for i, ref in enumerate(places):
                ref[:, :HD] = (dot_tn(ds[:, part[i]], q) * HD**-0.5).astype(ref.dtype)
                ref[:, HD:] = dot_tn(p[:, part[i]], gm).astype(ref.dtype)

    return call_once(
        body,
        (q, *pinned(*kvs), gm, qpos, kpos),
        [
            shape((rows, HD), F32),
            shape((rows, 2 * HD), F32),
            shape((rows, 2 * HD), F32),
            shape((2 * rows, 2 * HD), BF16),
        ],
        flops=40 * rows * per * HD,
    )


def back_in(dq, own, from_core, from_y, tables, gh, w, x, stats, vec, layer, part):
    rows, hidden = gh.shape
    width = w[0].shape[1]
    runs = [(w[1], 3), (w[2], hidden // TILE)]

    def body(
        dq_ref,
        own_ref,
        core_ref,
        y_ref,
        t_ref,
        gh_ref,
        w_ref,
        x_ref,
        stat_ref,
        vec_ref,
        part_ref,
        gp_ref,
        *rest,
    ):
        refs = rest[:6]
        sum_ref, wide, sems, xs, x_sems = rest[6:]
        tiles = Tiles(w_ref, runs, wide, sems)

        def x_copy(j):
            at = span(j, TILE)
            return pltpu.make_async_copy(x_ref.at[:, at], xs.at[j], x_sems.at[j])

        def begin(j, carry):
            start(tiles.copies(j))
            x_copy(j).start()
            return carry

        lax.fori_loop(0, width // TILE, begin, 0)
        both = own_ref[...] + core_ref[:rows].astype(F32) + y_ref[...].astype(F32)
        parts = (turn(dq_ref[...], t_ref, -1.0), turn(both[:, :HD], t_ref, -1.0), both[:, HD:])
        sum_ref[...] = part_ref[...]
        for i, a in enumerate(parts):
            a = a.astype(BF16)
            at = slice(i * HD, (i + 1) * HD)
            gp_ref[:, at] = a
            sum_ref[5:6, at] = sum_rows(a.astype(F32))

        def step(j, carry):
            at = span(j, TILE)
            w_tile = tiles.get(j)
            gna = dot_nt(gp_ref[...], jnp.concatenate(w_tile[:3], axis=1))
            gnm = dot_nt(gh_ref[...], jnp.concatenate(w_tile[3:], axis=1))
            x_copy(j).wait()
            u = unit_of(xs[j], stat_ref[...])
            y = gna * vec_ref[layer, 0:1, at] + gnm * vec_ref[layer, 1:2, at]
            put_pieces(at, y, refs)
            for i, a in enumerate((gna * u, gnm * u, gna, gnm)):
                sum_ref[i : i + 1, at] = sum_rows(a)
            return carry

        lax.fori_loop(0, width // TILE, step, 0)

    out = call_once(
        body,
        (*pinned(dq, own, from_core), from_y, tables, *pinned(gh), w[0], x, stats, vec, part),
        [shape((rows, 3 * HD), BF16)] + piece_shapes(rows, width) + [shape((8, width), F32)],
        tiles_scratch(runs, width)
        + [pltpu.VMEM((width // TILE, rows, TILE), BF16), pltpu.SemaphoreType.DMA((width // TILE,))],
        hbm=(6, 7),
        flops=2 * rows * width * (3 * HD + hidden),
    )
    return out[0], out[1:7], out[7]


def put_rows(like, row_at, rows_in, pieces, others, value):
    seqs, per, width = like.shape
    rows = seqs * per
    n = len(rows_in)

    def body(row_ref, *rest):
        refs = rest[: n + 6 + len(others)]
        out_ref, own, sems = rest[len(refs) : len(refs) + 3]
        rest = rest[len(refs) + 3 :]
        loads = [Rows([refs[i]], rest[2 * i], rest[2 * i + 1]) for i in range(n)]
        ps = Rows(refs[n : n + 6], rest[2 * n], rest[2 * n + 1])
        start_rows(*loads, ps)
        copies = row_copies(out_ref, row_ref, own, sems, back=True)

        def step(i, branch, carry):
            at = span(i, CHUNK)
            chunks = [load.scratch[at, :] for load in loads]
            own[at, :] = value(chunks, branch, at, refs[n + 6 :])
            copies(i).start()
            return carry

        for_rows(ps, loads, step)

        def finish(i, carry):
            copies(i).wait()
            return carry

        for_chunks(rows // CHUNK, finish)

    return call_once(
        body,
        (row_at, *rows_in, *pieces, *others),
        [shape((seqs, per, width), F32)],
        [pltpu.VMEM((rows, width), F32), pltpu.SemaphoreType.DMA((rows // CHUNK,))]
        + rows_scratch(rows, width, n + 1),
        prefetch=1,
        hbm=tuple(range(1, n + 7)),
        out_hbm=True,
    )[0]


def last_stream(like, row_at, x, pieces, vec, layer):
    def value(chunks, branch, at, others):
        return chunks[0].astype(F32) + branch + others[0][layer, 4:5]

    return put_rows(like, row_at, (x,), pieces, (vec,), value)


def last_grad(like, row_at, g, x, stats, pieces):
    def value(chunks, branch, at, others):
        return grad_in(chunks[0], chunks[1], others[0][at, :], branch)

    return put_rows(like, row_at, (g, x), pieces, (stats,), value)


def pack_panels(layer, *parts):
    depth = parts[0].shape[1]
    panels = [(i, c) for i, a in enumerate(parts) for c in range(a.shape[2] // TILE)]

    def body(*refs):
        out_ref, sems = refs[-2:]
        copies = [
            pltpu.make_async_copy(
                refs[i].at[layer, :, c * TILE : (c + 1) * TILE], out_ref.at[p], sems.at[p]
            )
            for p, (i, c) in enumerate(panels)
        ]
        start(copies)
        wait(copies)

    return call_once(
        body,
        parts,
        [shape((len(panels), depth, TILE), BF16)],
        [pltpu.SemaphoreType.DMA((len(panels),))],
        hbm=tuple(range(len(parts))),
    )[0]


def turn(x, tables, sign):
    head = x[:, :LANES]
    half = ROT // 2
    up = pltpu.roll(head, LANES - half, 1)
    down = pltpu.roll(head, half, 1)
    head = head * tables[0] + sign * (down * tables[2] - up * tables[1])
    return jnp.concatenate([head, x[:, LANES:]], axis=1)


def add_up(*parts):
    def body(*refs):
        total = refs[0][...].astype(F32)
        for ref in refs[1:-1]:
            total = total + ref[...].astype(F32)
        refs[-1][...] = total.astype(BF16)

    return call_once(body, pinned(*parts), [shape(parts[0].shape, BF16)])[0]


def add_split(a, b):
    rows, width = a.shape
    n = rows // 4

    def body(a_ref, b_ref, *outs):
        for i, ref in enumerate(outs):
            at = slice(i * n, (i + 1) * n)
            ref[...] = (a_ref[at].astype(F32) + b_ref[at].astype(F32)).astype(BF16)

    return call_once(body, pinned(a, b), [shape((n, width), BF16)] * 4)


def stack_up(*parts):
    n, width = parts[0].shape

    def body(*refs):
        for i, ref in enumerate(refs[:-1]):
            refs[-1][i * n : (i + 1) * n] = ref[...]

    return call_once(body, pinned(*parts), [shape((n * len(parts), width), BF16)])[0]


def add_late(a, b):
    rows = a.shape[0]

    def body(a_ref, b_ref, out_ref):
        out_ref[...] = (a_ref[...] + b_ref[...].astype(F32)).astype(BF16)

    return call(
        body,
        (1,),
        (a, b),
        [whole(a), pl.BlockSpec((rows, b.shape[1]), lambda *_: (b.shape[0] // rows - 1, 0))],
        [shape(a.shape, BF16)],
        [whole(a)],
    )[0]


def weight_grad(x, ys, blocks, got=None):
    rows, width = x.shape
    cols = [a.shape[1] for a in ys]
    total = sum(cols)
    size = width // 16
    tiles = blocks.shape[0] // 2

    def body(block_ref, x_ref, *rest):
        y_refs = rest[: len(ys)]
        out_ref, xs, sems = rest[-3:]
        j = pl.program_id(0)

        def copy(i):
            at = pl.multiple_of(block_ref[i] * size, size)
            return pltpu.make_async_copy(x_ref.at[:, pl.ds(at, size)], xs.at[i], sems.at[i])

        @pl.when(j == 0)
        def _():
            for i in range(2 * tiles):
                copy(i).start()

        copy(2 * j).wait()
        copy(2 * j + 1).wait()
        left = jnp.concatenate([xs[2 * j], xs[2 * j + 1]], axis=1)
        at = 0
        for ref, n in zip(y_refs, cols):
            y = dot_tn(left, ref[...])
            if got is not None:
                y = y + rest[len(ys)][:, at : at + n].astype(F32)
            out_ref[:, at : at + n] = y.astype(BF16)
            at += n

    ins = (blocks, *pinned(x), *ys)
    specs = [pl.BlockSpec(memory_space=pltpu.HBM)] + [whole(a) for a in ys]
    if got is not None:
        ins += (got,)
        specs += [pl.BlockSpec((2 * size, total), lambda j, *_: (j, 0))]
    return call(
        body,
        (tiles,),
        ins,
        specs,
        [shape((width // 2, total), BF16)],
        [pl.BlockSpec((2 * size, total), lambda j, *_: (j, 0))],
        scratch=[pltpu.VMEM((2 * tiles, rows, size), BF16), pltpu.SemaphoreType.DMA((2 * tiles,))],
        prefetch=1,
        flops=2 * rows * (width // 2) * total,
    )[0]


def scatter_weight_grad(value):
    return lax.psum_scatter(value, "fsdp", scatter_dimension=0, tiled=True)


def swap_half(value):
    return swap_y(value[value.shape[0] // 2 :])


def finish_weight_grads(layers, cols):
    flat = [a for layer in layers for a in layer]
    depth = layers[0][0].shape[0] // 2
    outs = [shape((len(layers), depth, n), F32) for n in cols]

    def body(*refs):
        qkv_ref, dense_ref, up_ref, down_ref = refs[len(flat) :]
        for l in range(len(layers)):
            ins = refs[6 * l : 6 * l + 6]
            out, up, qkv = (
                ins[i][:depth].astype(F32) + ins[3 + i][...].astype(F32) for i in range(3)
            )
            qkv_ref[l] = qkv
            dense_ref[l] = out[:, :HD]
            up_ref[l] = up
            down_ref[l] = out[:, HD:]

    return call_once(body, pinned(*flat), outs)


def body(
    tokens,
    block_order,
    cotangent,
    qkv_weight,
    qkv_bias,
    dense_weight,
    up_weight,
    up_bias,
    down_weight,
    norm_gains,
    norm_shifts,
    out_bias,
):
    seqs, per, width = tokens.shape
    block = 128
    c, t = lax.axis_index("ctx"), lax.axis_index("tp")
    y_hi, z = t // 4, t % 4

    b = jnp.arange(8, dtype=jnp.int32)
    near = (b // 2) * 4 + (c ^ (2 * (b % 2)))
    far = near ^ 1
    row_at = jnp.concatenate(
        [2 * ((z + b // 2) % 4) + b % 2, (y_hi ^ (b // 4)) * 4 + (z + b) % 4]
    )

    row = row_at[:, None] * CHUNK + jnp.arange(CHUNK, dtype=jnp.int32)[None, :]
    row = row.reshape(seqs, per)
    slots = jnp.arange(block_order.shape[0], dtype=jnp.int32)

    def positions(owner):
        slot = 2 * owner + row // block
        here = slot[:, :, None] == slots
        return jnp.sum(jnp.where(here, block_order, 0), axis=2) * block + row % block

    qpos = positions(c).reshape(seqs * per, 1)
    kpos = jnp.concatenate([positions(c ^ i) for i in range(4)], axis=1)
    inverse = 10000.0 ** (-(jnp.arange(ROT // 2, dtype=F32) * 2.0) / ROT)
    angles = qpos.astype(F32) * inverse[None, :]
    cosine, sine = jnp.cos(angles), jnp.sin(angles)
    none = jnp.zeros_like(sine)
    rest = jnp.zeros((seqs * per, LANES - ROT), F32)
    tables = jnp.stack(
        [
            jnp.concatenate([cosine, cosine, rest + 1.0], axis=1),
            jnp.concatenate([sine, none, rest], axis=1),
            jnp.concatenate([none, sine, rest], axis=1),
        ]
    )

    vec = jnp.concatenate(
        [
            norm_gains,
            norm_shifts,
            out_bias[:, None],
            jnp.zeros((LAYERS, 3, width), BF16),
        ],
        axis=1,
    ).astype(F32)
    weights = (qkv_weight, dense_weight, up_weight, down_weight)
    qkv_b = qkv_bias.astype(F32)
    up_b = up_bias.astype(F32)

    kept = []
    rows = seqs * per
    ins = [pack_panels(l, qkv_weight, up_weight) for l in range(LAYERS)]
    outs = [pack_panels(l, dense_weight, down_weight) for l in range(LAYERS)]
    w = gather_weights(ins[0])
    w, ins, outs, vec, tables, qpos, kpos, near, far = together(
        w, ins[1:], outs, vec, tables, qpos, kpos, near, far
    )
    w_in, w_out = (w, *IN_PANELS), (gather_weights(outs[0]), *OUT_PANELS)
    sums = None
    for l in range(LAYERS):
        bias = qkv_b[l : l + 1]
        if l == 0:
            new = first_in(tokens, row_at, vec, w_in, bias, tables)
        else:
            new = next_in(kept[-1][2], sums, l, vec, w_in, bias, tables)
        x, stats, na, nm, q, kv = new
        kv_y, kv_core = swap_y(kv), swap_core(kv)
        active, slope = project_up(nm, w_in, up_b[l : l + 1])
        kv_y, active = together(kv_y, active)
        kvs = [kv, kv_core, kv_y, swap_core(kv_y)]
        mixed, terms = attend_out(q, kvs, qpos, kpos, active, w_out)
        held, moving = tp_1(terms)
        kept.append((w_in, w_out, x, stats, na, nm, q, kvs, mixed, active, slope, terms))
        if l < LAYERS - 1:
            shard, _, _ = together(ins[l], kv_y, w_out[0])
            w_in = (gather_weights(shard), *IN_PANELS)
            held, moving = tp_2(held, together(*moving))
            shard, moving = together(outs[l + 1], moving)
            (first, second), (firsts, seconds) = tp_3(held, moving)
            seconds, first = together(seconds, first)
            sums = tp_pieces(first, firsts, *tp_4(second, seconds))
            w_out = (gather_weights(shard), *OUT_PANELS)

    late, late_moving = held, moving
    small = [None] * LAYERS
    scattered = [None] * LAYERS
    g = None
    for l in reversed(range(LAYERS)):
        last = l == LAYERS - 1
        w_in, w_out, x, stats, na, nm, q, kvs, mixed, active, slope, terms = kept[l]
        if last:
            slope, _ = together(slope, terms)
            g, gm, gh, part = last_back_out(cotangent, row_at, w_out, slope)
            late_moving, gm = together(late_moving, gm)
            late, late_moving = tp_2(late, late_moving)
        else:
            after = kept[l + 1]
            g, gm, gh, part = next_back_out(g, after[2], after[3], sums, w_out, slope)
        dq, own, to_y, send = attend_back(q, kvs, gm, qpos, kpos)
        from_core = swap_core(send)
        out_far = weight_grad(g, pinned(mixed, active), far)
        if last:
            late_moving, out_far = together(late_moving, out_far)
        else:
            late_first, late_second = tp_3_sums(late, late_moving)
            late_seconds = [from_z(late_second, k) for k in (1, 3, 2)]
            late_seconds, out_far = together(late_seconds, out_far)
            late_near, late_far = tp_4(late_second, late_seconds)
            late_firsts = [from_z(late_first, k) for k in (1, 3, 2)]
        from_core, out_far = together(from_core, out_far)
        from_y = swap_y(add_late(to_y, from_core))
        out_got = swap_core(out_far)
        up_far = weight_grad(nm, pinned(gh), far)
        out_got, up_far = together(out_got, up_far)
        out_near = weight_grad(g, pinned(mixed, active), near, out_got)
        if last:
            up_got, out_near = together(swap_core(up_far), out_near)
        else:
            out_after, up_after, qkv_after = scattered[l + 1]
            out_half = swap_half(out_after)
            up_got, out_near, out_half = together(swap_core(up_far), out_near, out_half)
            up_half = swap_half(up_after)
        up_near = weight_grad(nm, pinned(gh), near, up_got)
        if last:
            from_y, out_near, up_near = together(from_y, out_near, up_near)
        else:
            from_y, out_near, up_near, qkv_after, up_half = together(
                from_y, out_near, up_near, qkv_after, up_half
            )
        out_sum = scatter_weight_grad(out_near)
        gp, terms, small[l] = back_in(
            dq, own, from_core, from_y, tables, gh, w_in, x, stats, vec, l, part
        )
        if not last:
            late_firsts, late_far, gp = together(late_firsts, late_far, gp)
        held, moving = tp_1(terms)
        up_sum = scatter_weight_grad(up_near)
        qkv_far = weight_grad(na, (gp,), far)
        moving, qkv_far, out_sum = together(moving, qkv_far, out_sum)
        held, moving = tp_2(held, moving)
        qkv_got = swap_core(qkv_far)
        if last:
            moving, qkv_got = together(moving, qkv_got)
        else:
            total = jnp.stack(small)
            parts = around_ctx(total)
            moving, qkv_got, parts = together(moving, qkv_got, parts)
        first, second = tp_3_sums(held, moving)
        second, first, qkv_got = together(second, first, qkv_got)
        seconds = [from_z(second, k) for k in (1, 3, 2)]
        firsts = [from_z(first, k) for k in (1, 3, 2)]
        qkv_near = weight_grad(na, (gp,), near, qkv_got)
        qkv_sum = scatter_weight_grad(qkv_near)
        if last:
            seconds, qkv_near, up_sum = together(seconds, qkv_near, up_sum)
            sums = tp_pieces(first, firsts, *tp_4(second, seconds))
        else:
            total = pair_up(total, parts)
            parts = around(total, from_x)
            qkv_half, next_half = swap_half(qkv_after), swap_half(out_sum)
            seconds, qkv_near, parts, qkv_half, next_half = together(
                seconds, qkv_near, parts, qkv_half, next_half
            )
            halves = [[next_half], [out_half, up_half, qkv_half]]
            scattered[l + 1] = (out_after, up_after, qkv_after)
            sum_near, sum_far = tp_4(second, seconds)
            total = pair_up(total, parts)
            wide = total[:, :4]
            parts = around(wide, from_z)
            late_pieces = tp_pieces(late_first, late_firsts, late_near, late_far)
            activations = last_stream(tokens, row_at, kept[-1][2], late_pieces, vec, LAYERS - 1)
            sum_far, firsts, parts, activations = together(sum_far, firsts, parts, activations)
            halves[0] += [swap_half(up_sum), swap_half(qkv_sum)]
            wide = pair_up(wide, parts)
            wide = wide + swap_tp(wide, 4)
            sums = tp_pieces(first, firsts, sum_near, sum_far)
        scattered[l] = (out_sum, up_sum, qkv_sum)
    input_grad = last_grad(tokens, row_at, g, kept[0][2], kept[0][3], sums)
    input_grad, halves = together(input_grad, halves)
    qkv_grad, dense_grad, up_grad, down_grad = finish_weight_grads(
        [(*scattered[l], *halves[l]) for l in range(LAYERS)],
        [a.shape[2] for a in weights],
    )
    return (
        activations,
        input_grad,
        qkv_grad,
        total[:, 5, : qkv_bias.shape[1]],
        dense_grad,
        up_grad,
        total[:, 6, : up_bias.shape[1]],
        down_grad,
        wide[:, 0:2],
        wide[:, 2:4],
        total[:, 4],
    )


def solution(mesh):
    weight = P(None, ("fsdp", "ctx"), "tp")
    stream = P("fsdp", "ctx", None)
    bias = P(None, "tp")
    return jax.shard_map(
        body,
        mesh=mesh,
        in_specs=(
            stream,
            P(),
            stream,
            weight,
            bias,
            weight,
            weight,
            bias,
            weight,
            P(),
            P(),
            P(),
        ),
        out_specs=(
            stream,
            stream,
            weight,
            bias,
            weight,
            weight,
            bias,
            weight,
            P(),
            P(),
            P(),
        ),
        check_vma=False,
    )
```

```python
import jax
import jax.numpy as jnp
from jax import lax
from jax.experimental import pallas as pl
from jax.experimental.pallas import tpu as pltpu
from jax.sharding import PartitionSpec as P

HD = 256
ROT = 64
LAYERS = 2
EPSILON = 1e-05
LANES = 128
TILE = 256
CHUNK = 32
ALL_PANELS = (0, 3, 4, 8)
IN_PANELS, OUT_PANELS = (0, 3), (0, 1)
F32 = jnp.float32
BF16 = jnp.bfloat16
VMEM_LIMIT = 24 * 1024 * 1024


def swap_core(value):
    return lax.ppermute(value, "ctx", [(i, i ^ 1) for i in range(4)])


def swap_y(value):
    return lax.ppermute(value, "ctx", [(i, i ^ 2) for i in range(4)])


def from_x(value, k):
    return lax.ppermute(value, "fsdp", [((i + k) % 4, i) for i in range(4)])


def swap_both(value):
    return lax.ppermute(value, "ctx", [(i, i ^ 3) for i in range(4)])


def swap_tp(value, k):
    return lax.ppermute(value, "tp", [(i, i ^ k) for i in range(8)])


def from_z(value, k):
    return lax.ppermute(value, "tp", [((i & 4) + (i + k) % 4, i) for i in range(8)])


def to_z(value, k):
    return lax.ppermute(value, "tp", [(i, (i & 4) + (i + k) % 4) for i in range(8)])


def gather_weights(shard):
    return lax.all_gather(shard, ("fsdp", "ctx"), axis=1, tiled=True)


def together(*values):
    return lax.optimization_barrier(values)


def tp_1(pieces):
    firsts = [to_z(pieces[k], k) for k in (1, 3, 2)]
    return (pieces[0], pieces[4]), (firsts, swap_tp(pieces[5], 4))


def tp_2(kept, arrived):
    (own, near), (firsts, far) = kept, arrived
    first = add_up(own, *firsts)
    parts = add_split(near, far)
    seconds = [to_z(parts[k], k) for k in (1, 3, 2)]
    return (first, parts[0]), (swap_tp(first, 4), seconds)


def tp_3_sums(kept, arrived):
    (first, own), (other, seconds) = kept, arrived
    second = add_up(own, *seconds)
    return add_up(first, other), second


def tp_3(kept, arrived):
    first, second = tp_3_sums(kept, arrived)
    seconds = [from_z(second, k) for k in (1, 3, 2)]
    firsts = [from_z(first, k) for k in (1, 3, 2)]
    return (first, second), (firsts, seconds)


def tp_4(second, seconds):
    near = stack_up(second, seconds[0], seconds[2], seconds[1])
    return near, swap_tp(near, 4)


def tp_pieces(first, firsts, near, far):
    return (first, firsts[0], firsts[2], firsts[1], near, far)


def around(value, move):
    return [move(value, k) for k in (1, 2, 3)]


def around_ctx(value):
    return [swap_y(value), swap_core(value), swap_both(value)]


def pair_up(value, got):
    return (value + got[1]) + (got[0] + got[2])


def call(body, grid, ins, in_specs, outs, out_specs, scratch=(), prefetch=0, flops=0):
    nbytes = sum(a.size * a.dtype.itemsize for a in outs)
    nbytes += sum(min(a.size * a.dtype.itemsize, 1 << 22) for a in ins)
    return pl.pallas_call(
        body,
        grid_spec=pltpu.PrefetchScalarGridSpec(
            num_scalar_prefetch=prefetch,
            grid=grid,
            in_specs=in_specs,
            out_specs=out_specs,
            scratch_shapes=scratch,
        ),
        out_shape=outs,
        compiler_params=pltpu.CompilerParams(vmem_limit_bytes=VMEM_LIMIT),
        cost_estimate=pl.CostEstimate(
            flops=int(flops), bytes_accessed=int(nbytes), transcendentals=0
        ),
    )(*ins)


def call_once(body, ins, outs, scratch=(), prefetch=0, hbm=(), out_hbm=False, flops=0):
    ins = tuple(
        pltpu.with_memory_space_constraint(a, pltpu.HBM) if i in hbm else a
        for i, a in enumerate(ins)
    )
    specs = [
        pl.BlockSpec(memory_space=pltpu.HBM) if i in hbm else whole(a)
        for i, a in enumerate(ins)
        if i >= prefetch
    ]
    out_specs = [pl.BlockSpec(memory_space=pltpu.HBM) if out_hbm else whole(a) for a in outs]
    return call(body, (1,), ins, specs, outs, out_specs, scratch, prefetch, flops)


def pinned(*arrays):
    return tuple(pltpu.with_memory_space_constraint(a, pltpu.HBM) for a in arrays)


def shape(dims, dtype):
    return jax.ShapeDtypeStruct(dims, dtype)


def whole(a):
    return pl.BlockSpec(a.shape, lambda *_: (0,) * len(a.shape))


def dot_nn(a, b):
    return lax.dot_general(a, b, (((1,), (0,)), ((), ())), preferred_element_type=F32)


def dot_nt(a, b):
    return lax.dot_general(a, b, (((1,), (1,)), ((), ())), preferred_element_type=F32)


def dot_tn(a, b):
    return lax.dot_general(a, b, (((0,), (0,)), ((), ())), preferred_element_type=F32)


def fold_rows(a):
    return jnp.sum(a.reshape(a.shape[0] // 8, 8, a.shape[1]), axis=0)


def sum_rows(a):
    return jnp.sum(a, axis=0, keepdims=True)


def span(j, size):
    return pl.ds(pl.multiple_of(j * size, size), size)


def start(copies):
    for copy in copies:
        copy.start()


def wait(copies):
    for copy in copies:
        copy.wait()


def load_panels(w_ref, first, scratch, sems, at=0):
    return [
        pltpu.make_async_copy(w_ref.at[first + i], scratch.at[at + i], sems.at[at + i])
        for i in range(scratch.shape[0] - at)
    ]


def panels_scratch(n, width):
    return [pltpu.VMEM((n, width, TILE), BF16), pltpu.SemaphoreType.DMA((n,))]


class Tiles:
    def __init__(self, w_ref, runs, scratch, sems):
        self.w_ref, self.runs, self.scratch, self.sems = w_ref, runs, scratch, sems

    def copies(self, j):
        at = 0
        for i, (first, n) in enumerate(self.runs):
            yield pltpu.make_async_copy(
                self.w_ref.at[first : first + n, span(j, TILE), :],
                self.scratch.at[j, at : at + n],
                self.sems.at[i, j],
            )
            at += n

    def start(self):
        def step(j, carry):
            start(self.copies(j))
            return carry

        lax.fori_loop(0, self.scratch.shape[0], step, 0)

    def get(self, j):
        wait(self.copies(j))
        n = self.scratch.shape[1]
        return [self.scratch[j, i] for i in range(n)]


def tiles_scratch(runs, width):
    n = sum(size for _, size in runs)
    return [
        pltpu.VMEM((width // TILE, n, TILE, TILE), BF16),
        pltpu.SemaphoreType.DMA((len(runs), width // TILE)),
    ]


def row_copies(source, row_ref, target, sems, back=False):
    per = source.shape[1] // CHUNK

    def copy(k):
        far = source.at[k // per, span(row_ref[k], CHUNK)]
        own = target.at[span(k, CHUNK)]
        ends = (own, far) if back else (far, own)
        return pltpu.make_async_copy(*ends, sems.at[k])

    return copy


def for_chunks(n, step, carry=0):
    return lax.fori_loop(0, n, step, carry)


class Rows:
    def __init__(self, refs, scratch, sems):
        self.scratch, self.sems = scratch, sems
        self.parts, base = [], 0
        for ref in refs:
            self.parts.append((ref, base, ref.shape[0] // CHUNK))
            base += ref.shape[0] // CHUNK

    def copy(self, part, i):
        ref, base, _ = part
        return pltpu.make_async_copy(
            ref.at[span(i, CHUNK)], self.scratch.at[span(base + i, CHUNK)], self.sems.at[base + i]
        )


def start_rows(*rows):
    order = [(base + i, r, (ref, base, n), i) for r in rows for ref, base, n in r.parts for i in range(n)]
    for _, r, part, i in sorted(order, key=lambda entry: entry[0]):
        r.copy(part, i).start()


def for_rows(pieces, others, fn, carry=0):
    for part in pieces.parts:

        def step(i, carry, part=part):
            pieces.copy(part, i).wait()
            for other in others:
                other.copy(other.parts[0], part[1] + i).wait()
            at = span(part[1] + i, CHUNK)
            return fn(part[1] + i, pieces.scratch[at, :].astype(F32), carry)

        carry = lax.fori_loop(0, part[2], step, carry)
    return carry


def rows_scratch(rows, width, n=1):
    one = [pltpu.VMEM((rows, width), BF16), pltpu.SemaphoreType.DMA((rows // CHUNK,))]
    return one * n


def piece_shapes(rows, width):
    return [shape((rows // 8, width), BF16)] * 4 + [shape((rows // 4, width), BF16)] * 2


def put_pieces(at, y, refs):
    base = 0
    for ref in refs:
        ref[:, at] = y[base : base + ref.shape[0]].astype(BF16)
        base += ref.shape[0]


def put_norms(at, x, vec_ref, layer, stat_ref, na_ref, nm_ref):
    mean = jnp.mean(x, axis=1, keepdims=True)
    center = x - mean
    r = lax.rsqrt(jnp.mean(center * center, axis=1, keepdims=True) + EPSILON)
    u = center * r
    lane = lax.broadcasted_iota(jnp.int32, (x.shape[0], LANES), 1)
    stat_ref[at, :] = jnp.where(lane < LANES // 2, mean, r)
    na_ref[at, :] = (u * vec_ref[layer, 0:1] + vec_ref[layer, 2:3]).astype(BF16)
    nm_ref[at, :] = (u * vec_ref[layer, 1:2] + vec_ref[layer, 3:4]).astype(BF16)


def unit_of(x, stats):
    return (x.astype(F32) - stats[:, 0:1]) * stats[:, LANES // 2 : LANES // 2 + 1]


def put_qkv(na_ref, loads, w_ref, b_ref, t_ref, q_ref, kv_ref):
    for j in range(3):
        loads[j].wait()
        y = dot_nn(na_ref[...], w_ref[j]) + b_ref[:, j * HD : (j + 1) * HD]
        if j == 0:
            q_ref[...] = turn(y, t_ref, 1.0).astype(BF16)
        elif j == 1:
            kv_ref[:, :HD] = turn(y, t_ref, 1.0).astype(BF16)
        else:
            kv_ref[:, HD:] = y.astype(BF16)


def in_outs(rows, width):
    return [
        shape((rows, width), BF16),
        shape((rows, LANES), F32),
        shape((rows, width), BF16),
        shape((rows, width), BF16),
        shape((rows, HD), BF16),
        shape((rows, 2 * HD), BF16),
    ]


def first_in(tokens, row_at, vec, w, bias, tables):
    width = tokens.shape[2]
    rows = tokens.shape[0] * tokens.shape[1]

    def body(
        row_ref,
        tok_ref,
        vec_ref,
        w_ref,
        b_ref,
        t_ref,
        x_ref,
        stat_ref,
        na_ref,
        nm_ref,
        q_ref,
        kv_ref,
        panels,
        sems,
        row_sems,
    ):
        news = row_copies(tok_ref, row_ref, x_ref, row_sems)
        for k in range(rows // CHUNK):
            news(k).start()
        loads = load_panels(w_ref, w[1], panels, sems)
        start(loads)

        def step(i, carry):
            news(i).wait()
            at = span(i, CHUNK)
            put_norms(at, x_ref[at, :].astype(F32), vec_ref, 0, stat_ref, na_ref, nm_ref)
            return carry

        for_chunks(rows // CHUNK, step)
        put_qkv(na_ref, loads, panels, b_ref, t_ref, q_ref, kv_ref)

    return call_once(
        body,
        (row_at, tokens, vec, w[0], bias, tables),
        in_outs(rows, width),
        panels_scratch(3, width) + [pltpu.SemaphoreType.DMA((rows // CHUNK,))],
        prefetch=1,
        hbm=(1, 3),
        flops=2 * rows * width * 3 * HD,
    )


def next_in(x, pieces, layer, vec, w, bias, tables):
    rows, width = x.shape

    def body(x_ref, *rest):
        refs = rest[:6]
        vec_ref, w_ref, b_ref, t_ref, new_ref, stat_ref, na_ref, nm_ref = rest[6:14]
        q_ref, kv_ref, panels, sems, xs, x_sems, ps, p_sems = rest[14:]
        xs, ps = Rows([x_ref], xs, x_sems), Rows(refs, ps, p_sems)
        start_rows(xs, ps)
        loads = load_panels(w_ref, w[1], panels, sems)
        start(loads)

        def step(i, branch, carry):
            at = span(i, CHUNK)
            new = xs.scratch[at, :].astype(F32) + branch + vec_ref[layer - 1, 4:5]
            new_ref[at, :] = new.astype(BF16)
            put_norms(at, new, vec_ref, layer, stat_ref, na_ref, nm_ref)
            return carry

        for_rows(ps, [xs], step)
        put_qkv(na_ref, loads, panels, b_ref, t_ref, q_ref, kv_ref)

    return call_once(
        body,
        (x, *pieces, vec, w[0], bias, tables),
        in_outs(rows, width),
        panels_scratch(3, width) + rows_scratch(rows, width, 2),
        hbm=(0, 1, 2, 3, 4, 5, 6, 8),
        flops=2 * rows * width * 3 * HD,
    )


def gelu_parts(h):
    e = jnp.exp(-0.5 * h * h)
    t = 1.0 / (1.0 + (0.3275911 * 0.5**0.5) * jnp.abs(h))
    tail = 1.061405429 * t - 1.453152027
    tail = tail * t + 1.421413741
    tail = tail * t - 0.284496736
    tail = (tail * t + 0.254829592) * t * (0.5 * e)
    return jnp.where(h >= 0, 1.0 - tail, tail), e * 0.3989422804014327


def project_up(nm, w, bias):
    rows, width = nm.shape
    hidden = bias.shape[1]

    def body(n_ref, w_ref, b_ref, act_ref, slope_ref, panels, sems):
        loads = load_panels(w_ref, w[2], panels, sems)
        start(loads)
        for j in range(hidden // TILE):
            at = slice(j * TILE, (j + 1) * TILE)
            loads[j].wait()
            h = dot_nn(n_ref[...], panels[j]) + b_ref[:, at]
            cdf, density = gelu_parts(h)
            act_ref[:, at] = (h * cdf).astype(BF16)
            slope_ref[:, at] = (cdf + h * density).astype(BF16)

    return call_once(
        body,
        (nm, w[0], bias),
        [shape((rows, hidden), BF16), shape((rows, hidden), BF16)],
        panels_scratch(hidden // TILE, width),
        hbm=(1,),
        flops=2 * rows * width * hidden,
    )


def weights_of(q, kvs, qpos, kpos):
    scores = [dot_nt(q, kv[:, :HD]) * HD**-0.5 for kv in kvs]
    scores = jnp.concatenate(scores, axis=1)
    scores = jnp.where(kpos <= qpos, scores, -1e30)
    e = jnp.exp(scores - jnp.max(scores, axis=1, keepdims=True))
    return e / jnp.sum(e, axis=1, keepdims=True)


def attend_out(q, kvs, qpos, kpos, active, w):
    rows, hidden = active.shape
    width = w[0].shape[1]
    seqs = kpos.shape[0]
    per = rows // seqs
    runs = [(w[1], 1), (w[2], hidden // TILE)]

    def body(q_ref, k0, k1, k2, k3, qp_ref, kp_ref, act_ref, w_ref, mixed_ref, *rest):
        refs = rest[:6]
        wide, sems, left = rest[6:]
        tiles = Tiles(w_ref, runs, wide, sems)
        tiles.start()
        for s in range(seqs):
            at = slice(s * per, (s + 1) * per)
            kvs = [ref[at] for ref in (k0, k1, k2, k3)]
            p = weights_of(q_ref[at], kvs, qp_ref[at], kp_ref[s : s + 1]).astype(BF16)
            mixed = sum(dot_nn(p[:, i * per : (i + 1) * per], kvs[i][:, HD:]) for i in range(4))
            mixed_ref[at] = mixed.astype(BF16)
        left[:, :HD] = mixed_ref[...]
        left[:, HD:] = act_ref[...]

        def step(j, carry):
            y = dot_nt(left[...], jnp.concatenate(tiles.get(j), axis=1))
            put_pieces(span(j, TILE), y, refs)
            return carry

        lax.fori_loop(0, width // TILE, step, 0)

    out = call_once(
        body,
        (q, *kvs, qpos, kpos, active, w[0]),
        [shape((rows, HD), BF16)] + piece_shapes(rows, width),
        tiles_scratch(runs, width) + [pltpu.VMEM((rows, HD + hidden), BF16)],
        hbm=(8,),
        flops=16 * rows * per * HD + 2 * rows * width * (HD + hidden),
    )
    return out[0], out[1:]


def put_back_out(gb_ref, loads, panels, slope_ref, gm_ref, gh_ref, part_ref):
    for j in range(panels.shape[0]):
        loads[j].wait()
        y = dot_nn(gb_ref[...], panels[j])
        if j == 0:
            gm_ref[...] = y.astype(BF16)
        else:
            at = slice((j - 1) * TILE, j * TILE)
            gh = (y * slope_ref[:, at].astype(F32)).astype(BF16)
            gh_ref[:, at] = gh
            part_ref[6:7, at] = sum_rows(gh.astype(F32))


def load_back_out(w_ref, w, panels, sems):
    first = pltpu.make_async_copy(w_ref.at[w[1]], panels.at[0], sems.at[0])
    return [first] + load_panels(w_ref, w[2], panels, sems, at=1)


def back_out_shapes(rows, width, hidden):
    return [
        shape((rows, width), BF16),
        shape((rows, HD), BF16),
        shape((rows, hidden), BF16),
        shape((8, width), F32),
    ]


def last_back_out(cotangent, row_at, w, slope):
    width = cotangent.shape[2]
    rows, hidden = slope.shape
    n = 1 + hidden // TILE

    def body(
        row_ref, cot_ref, w_ref, slope_ref, gb_ref, gm_ref, gh_ref, part_ref, panels, sems, row_sems
    ):
        news = row_copies(cot_ref, row_ref, gb_ref, row_sems)
        for k in range(rows // CHUNK):
            news(k).start()
        loads = load_back_out(w_ref, w, panels, sems)
        start(loads)
        part_ref[...] = jnp.zeros_like(part_ref)

        def step(i, total):
            news(i).wait()
            return total + fold_rows(gb_ref[span(i, CHUNK), :].astype(F32))

        total = for_chunks(rows // CHUNK, step, jnp.zeros((8, width), F32))
        part_ref[4:5, :] = sum_rows(total)
        put_back_out(gb_ref, loads, panels, slope_ref, gm_ref, gh_ref, part_ref)

    return call_once(
        body,
        (row_at, cotangent, w[0], *pinned(slope)),
        back_out_shapes(rows, width, hidden),
        panels_scratch(n, width) + [pltpu.SemaphoreType.DMA((rows // CHUNK,))],
        prefetch=1,
        hbm=(1, 2),
        flops=2 * rows * width * n * TILE,
    )


def grad_in(g, x, stats, total):
    u = unit_of(x, stats)
    back = total - jnp.mean(total, axis=1, keepdims=True)
    back = back - u * jnp.mean(total * u, axis=1, keepdims=True)
    return g.astype(F32) + stats[:, LANES // 2 : LANES // 2 + 1] * back


def next_back_out(g, x, stats, pieces, w, slope):
    rows, width = g.shape
    hidden = slope.shape[1]
    n = 1 + hidden // TILE

    def body(g_ref, x_ref, stat_ref, *rest):
        refs = rest[:6]
        w_ref, slope_ref, gb_ref, gm_ref, gh_ref, part_ref, panels, sems = rest[6:14]
        gs, xs, ps = (
            Rows(r, rest[14 + 2 * i], rest[15 + 2 * i])
            for i, r in enumerate(([g_ref], [x_ref], refs))
        )
        start_rows(gs, xs, ps)
        loads = load_back_out(w_ref, w, panels, sems)
        start(loads)
        part_ref[...] = jnp.zeros_like(part_ref)

        def step(i, branch, total):
            at = span(i, CHUNK)
            new = grad_in(gs.scratch[at, :], xs.scratch[at, :], stat_ref[at, :], branch)
            gb_ref[at, :] = new.astype(BF16)
            return total + fold_rows(new)

        total = for_rows(ps, [gs, xs], step, jnp.zeros((8, width), F32))
        part_ref[4:5, :] = sum_rows(total)
        put_back_out(gb_ref, loads, panels, slope_ref, gm_ref, gh_ref, part_ref)

    return call_once(
        body,
        (g, x, stats, *pieces, w[0], *pinned(slope)),
        back_out_shapes(rows, width, hidden),
        panels_scratch(n, width) + rows_scratch(rows, width, 3),
        hbm=(0, 1, 3, 4, 5, 6, 7, 8, 9),
        flops=2 * rows * width * n * TILE,
    )


def attend_back(q, kvs, gm, qpos, kpos):
    rows = q.shape[0]
    seqs = kpos.shape[0]
    per = rows // seqs

    def body(q_ref, k0, k1, k2, k3, gm_ref, qp_ref, kp_ref, dq_ref, own_ref, y_ref, send_ref):
        part = [slice(i * per, (i + 1) * per) for i in range(4)]
        for s in range(seqs):
            at = part[s]
            kvs = [ref[at] for ref in (k0, k1, k2, k3)]
            q = q_ref[at]
            gm = gm_ref[at]
            p = weights_of(q, kvs, qp_ref[at], kp_ref[s : s + 1])
            dp = jnp.concatenate([dot_nt(gm, kv[:, HD:]) for kv in kvs], axis=1)
            ds = (p * (dp - jnp.sum(p * dp, axis=1, keepdims=True))).astype(BF16)
            p = p.astype(BF16)
            dq = sum(dot_nn(ds[:, part[i]], kvs[i][:, :HD]) for i in range(4))
            dq_ref[at] = dq * HD**-0.5
            late = slice(rows + s * per, rows + (s + 1) * per)
            places = (own_ref.at[at], send_ref.at[at], y_ref.at[at], send_ref.at[late])
            for i, ref in enumerate(places):
                ref[:, :HD] = (dot_tn(ds[:, part[i]], q) * HD**-0.5).astype(ref.dtype)
                ref[:, HD:] = dot_tn(p[:, part[i]], gm).astype(ref.dtype)

    return call_once(
        body,
        (q, *pinned(*kvs), gm, qpos, kpos),
        [
            shape((rows, HD), F32),
            shape((rows, 2 * HD), F32),
            shape((rows, 2 * HD), F32),
            shape((2 * rows, 2 * HD), BF16),
        ],
        flops=40 * rows * per * HD,
    )


def back_in(dq, own, from_core, from_y, tables, gh, w, x, stats, vec, layer, part):
    rows, hidden = gh.shape
    width = w[0].shape[1]
    runs = [(w[1], 3), (w[2], hidden // TILE)]

    def body(
        dq_ref,
        own_ref,
        core_ref,
        y_ref,
        t_ref,
        gh_ref,
        w_ref,
        x_ref,
        stat_ref,
        vec_ref,
        part_ref,
        gp_ref,
        *rest,
    ):
        refs = rest[:6]
        sum_ref, wide, sems, xs, x_sems = rest[6:]
        tiles = Tiles(w_ref, runs, wide, sems)

        def x_copy(j):
            at = span(j, TILE)
            return pltpu.make_async_copy(x_ref.at[:, at], xs.at[j], x_sems.at[j])

        def begin(j, carry):
            start(tiles.copies(j))
            x_copy(j).start()
            return carry

        lax.fori_loop(0, width // TILE, begin, 0)
        both = own_ref[...] + core_ref[:rows].astype(F32) + y_ref[...].astype(F32)
        parts = (turn(dq_ref[...], t_ref, -1.0), turn(both[:, :HD], t_ref, -1.0), both[:, HD:])
        sum_ref[...] = part_ref[...]
        for i, a in enumerate(parts):
            a = a.astype(BF16)
            at = slice(i * HD, (i + 1) * HD)
            gp_ref[:, at] = a
            sum_ref[5:6, at] = sum_rows(a.astype(F32))

        def step(j, carry):
            at = span(j, TILE)
            w_tile = tiles.get(j)
            gna = dot_nt(gp_ref[...], jnp.concatenate(w_tile[:3], axis=1))
            gnm = dot_nt(gh_ref[...], jnp.concatenate(w_tile[3:], axis=1))
            x_copy(j).wait()
            u = unit_of(xs[j], stat_ref[...])
            y = gna * vec_ref[layer, 0:1, at] + gnm * vec_ref[layer, 1:2, at]
            put_pieces(at, y, refs)
            for i, a in enumerate((gna * u, gnm * u, gna, gnm)):
                sum_ref[i : i + 1, at] = sum_rows(a)
            return carry

        lax.fori_loop(0, width // TILE, step, 0)

    out = call_once(
        body,
        (*pinned(dq, own, from_core), from_y, tables, *pinned(gh), w[0], x, stats, vec, part),
        [shape((rows, 3 * HD), BF16)] + piece_shapes(rows, width) + [shape((8, width), F32)],
        tiles_scratch(runs, width)
        + [pltpu.VMEM((width // TILE, rows, TILE), BF16), pltpu.SemaphoreType.DMA((width // TILE,))],
        hbm=(6, 7),
        flops=2 * rows * width * (3 * HD + hidden),
    )
    return out[0], out[1:7], out[7]


def put_rows(like, row_at, rows_in, pieces, others, value):
    seqs, per, width = like.shape
    rows = seqs * per
    n = len(rows_in)

    def body(row_ref, *rest):
        refs = rest[: n + 6 + len(others)]
        out_ref, own, sems = rest[len(refs) : len(refs) + 3]
        rest = rest[len(refs) + 3 :]
        loads = [Rows([refs[i]], rest[2 * i], rest[2 * i + 1]) for i in range(n)]
        ps = Rows(refs[n : n + 6], rest[2 * n], rest[2 * n + 1])
        start_rows(*loads, ps)
        copies = row_copies(out_ref, row_ref, own, sems, back=True)

        def step(i, branch, carry):
            at = span(i, CHUNK)
            chunks = [load.scratch[at, :] for load in loads]
            own[at, :] = value(chunks, branch, at, refs[n + 6 :])
            copies(i).start()
            return carry

        for_rows(ps, loads, step)

        def finish(i, carry):
            copies(i).wait()
            return carry

        for_chunks(rows // CHUNK, finish)

    return call_once(
        body,
        (row_at, *rows_in, *pieces, *others),
        [shape((seqs, per, width), F32)],
        [pltpu.VMEM((rows, width), F32), pltpu.SemaphoreType.DMA((rows // CHUNK,))]
        + rows_scratch(rows, width, n + 1),
        prefetch=1,
        hbm=tuple(range(1, n + 7)),
        out_hbm=True,
    )[0]


def last_stream(like, row_at, x, pieces, vec, layer):
    def value(chunks, branch, at, others):
        return chunks[0].astype(F32) + branch + others[0][layer, 4:5]

    return put_rows(like, row_at, (x,), pieces, (vec,), value)


def last_grad(like, row_at, g, x, stats, pieces):
    def value(chunks, branch, at, others):
        return grad_in(chunks[0], chunks[1], others[0][at, :], branch)

    return put_rows(like, row_at, (g, x), pieces, (stats,), value)


def pack_panels(layer, *parts):
    depth = parts[0].shape[1]
    panels = [(i, c) for i, a in enumerate(parts) for c in range(a.shape[2] // TILE)]

    def body(*refs):
        out_ref, sems = refs[-2:]
        copies = [
            pltpu.make_async_copy(
                refs[i].at[layer, :, c * TILE : (c + 1) * TILE], out_ref.at[p], sems.at[p]
            )
            for p, (i, c) in enumerate(panels)
        ]
        start(copies)
        wait(copies)

    return call_once(
        body,
        parts,
        [shape((len(panels), depth, TILE), BF16)],
        [pltpu.SemaphoreType.DMA((len(panels),))],
        hbm=tuple(range(len(parts))),
    )[0]


def turn(x, tables, sign):
    head = x[:, :LANES]
    half = ROT // 2
    up = pltpu.roll(head, LANES - half, 1)
    down = pltpu.roll(head, half, 1)
    head = head * tables[0] + sign * (down * tables[2] - up * tables[1])
    return jnp.concatenate([head, x[:, LANES:]], axis=1)


def add_up(*parts):
    def body(*refs):
        total = refs[0][...].astype(F32)
        for ref in refs[1:-1]:
            total = total + ref[...].astype(F32)
        refs[-1][...] = total.astype(BF16)

    return call_once(body, parts, [shape(parts[0].shape, BF16)])[0]


def add_split(a, b):
    rows, width = a.shape
    n = rows // 4

    def body(a_ref, b_ref, *outs):
        for i, ref in enumerate(outs):
            at = slice(i * n, (i + 1) * n)
            ref[...] = (a_ref[at].astype(F32) + b_ref[at].astype(F32)).astype(BF16)

    return call_once(body, (a, b), [shape((n, width), BF16)] * 4)


def stack_up(*parts):
    n, width = parts[0].shape

    def body(*refs):
        for i, ref in enumerate(refs[:-1]):
            refs[-1][i * n : (i + 1) * n] = ref[...]

    return call_once(body, parts, [shape((n * len(parts), width), BF16)])[0]


def add_late(a, b):
    rows = a.shape[0]

    def body(a_ref, b_ref, out_ref):
        out_ref[...] = (a_ref[...] + b_ref[...].astype(F32)).astype(BF16)

    return call(
        body,
        (1,),
        (a, b),
        [whole(a), pl.BlockSpec((rows, b.shape[1]), lambda *_: (b.shape[0] // rows - 1, 0))],
        [shape(a.shape, BF16)],
        [whole(a)],
    )[0]


def weight_grad(x, ys, blocks, got=None):
    rows, width = x.shape
    cols = [a.shape[1] for a in ys]
    total = sum(cols)
    size = width // 16
    tiles = blocks.shape[0] // 2

    def body(block_ref, x_ref, *rest):
        y_refs = rest[: len(ys)]
        out_ref, xs, sems = rest[-3:]
        j = pl.program_id(0)

        def copy(i):
            at = pl.multiple_of(block_ref[i] * size, size)
            return pltpu.make_async_copy(x_ref.at[:, pl.ds(at, size)], xs.at[i], sems.at[i])

        @pl.when(j == 0)
        def _():
            for i in range(2 * tiles):
                copy(i).start()

        copy(2 * j).wait()
        copy(2 * j + 1).wait()
        left = jnp.concatenate([xs[2 * j], xs[2 * j + 1]], axis=1)
        at = 0
        for ref, n in zip(y_refs, cols):
            y = dot_tn(left, ref[...])
            if got is not None:
                y = y + rest[len(ys)][:, at : at + n].astype(F32)
            out_ref[:, at : at + n] = y.astype(BF16)
            at += n

    ins = (blocks, *pinned(x), *ys)
    specs = [pl.BlockSpec(memory_space=pltpu.HBM)] + [whole(a) for a in ys]
    if got is not None:
        ins += (got,)
        specs += [pl.BlockSpec((2 * size, total), lambda j, *_: (j, 0))]
    return call(
        body,
        (tiles,),
        ins,
        specs,
        [shape((width // 2, total), BF16)],
        [pl.BlockSpec((2 * size, total), lambda j, *_: (j, 0))],
        scratch=[pltpu.VMEM((2 * tiles, rows, size), BF16), pltpu.SemaphoreType.DMA((2 * tiles,))],
        prefetch=1,
        flops=2 * rows * (width // 2) * total,
    )[0]


def scatter_weight_grad(value):
    return lax.psum_scatter(value, "fsdp", scatter_dimension=0, tiled=True)


def swap_half(value):
    return swap_y(value[value.shape[0] // 2 :])


def finish_weight_grads(layers, cols):
    flat = [a for layer in layers for a in layer]
    depth = layers[0][0].shape[0] // 2
    outs = [shape((len(layers), depth, n), F32) for n in cols]

    def body(*refs):
        qkv_ref, dense_ref, up_ref, down_ref = refs[len(flat) :]
        for l in range(len(layers)):
            ins = refs[6 * l : 6 * l + 6]
            out, up, qkv = (
                ins[i][:depth].astype(F32) + ins[3 + i][...].astype(F32) for i in range(3)
            )
            qkv_ref[l] = qkv
            dense_ref[l] = out[:, :HD]
            up_ref[l] = up
            down_ref[l] = out[:, HD:]

    return call_once(body, pinned(*flat), outs)


def body(
    tokens,
    block_order,
    cotangent,
    qkv_weight,
    qkv_bias,
    dense_weight,
    up_weight,
    up_bias,
    down_weight,
    norm_gains,
    norm_shifts,
    out_bias,
):
    seqs, per, width = tokens.shape
    block = 128
    c, t = lax.axis_index("ctx"), lax.axis_index("tp")
    y_hi, z = t // 4, t % 4

    b = jnp.arange(8, dtype=jnp.int32)
    near = (b // 2) * 4 + (c ^ (2 * (b % 2)))
    far = near ^ 1
    row_at = jnp.concatenate(
        [2 * ((z + b // 2) % 4) + b % 2, (y_hi ^ (b // 4)) * 4 + (z + b) % 4]
    )

    row = row_at[:, None] * CHUNK + jnp.arange(CHUNK, dtype=jnp.int32)[None, :]
    row = row.reshape(seqs, per)
    slots = jnp.arange(block_order.shape[0], dtype=jnp.int32)

    def positions(owner):
        slot = 2 * owner + row // block
        here = slot[:, :, None] == slots
        return jnp.sum(jnp.where(here, block_order, 0), axis=2) * block + row % block

    qpos = positions(c).reshape(seqs * per, 1)
    kpos = jnp.concatenate([positions(c ^ i) for i in range(4)], axis=1)
    inverse = 10000.0 ** (-(jnp.arange(ROT // 2, dtype=F32) * 2.0) / ROT)
    angles = qpos.astype(F32) * inverse[None, :]
    cosine, sine = jnp.cos(angles), jnp.sin(angles)
    none = jnp.zeros_like(sine)
    rest = jnp.zeros((seqs * per, LANES - ROT), F32)
    tables = jnp.stack(
        [
            jnp.concatenate([cosine, cosine, rest + 1.0], axis=1),
            jnp.concatenate([sine, none, rest], axis=1),
            jnp.concatenate([none, sine, rest], axis=1),
        ]
    )

    vec = jnp.concatenate(
        [
            norm_gains,
            norm_shifts,
            out_bias[:, None],
            jnp.zeros((LAYERS, 3, width), BF16),
        ],
        axis=1,
    ).astype(F32)
    weights = (qkv_weight, dense_weight, up_weight, down_weight)
    qkv_b = qkv_bias.astype(F32)
    up_b = up_bias.astype(F32)

    kept = []
    rows = seqs * per
    ins = [pack_panels(l, qkv_weight, up_weight) for l in range(1, LAYERS)]
    outs = [pack_panels(l, dense_weight, down_weight) for l in range(1, LAYERS)]
    w = gather_weights(pack_panels(0, *weights))
    w, ins, outs, vec, tables, qpos, kpos, near, far = together(
        w, ins, outs, vec, tables, qpos, kpos, near, far
    )
    w_in, w_out = (w, ALL_PANELS[0], ALL_PANELS[2]), (w, ALL_PANELS[1], ALL_PANELS[3])
    sums = None
    for l in range(LAYERS):
        bias = qkv_b[l : l + 1]
        if l == 0:
            new = first_in(tokens, row_at, vec, w_in, bias, tables)
        else:
            new = next_in(kept[-1][2], sums, l, vec, w_in, bias, tables)
        x, stats, na, nm, q, kv = new
        kv_y, kv_core = swap_y(kv), swap_core(kv)
        active, slope = project_up(nm, w_in, up_b[l : l + 1])
        kv_y, active = together(kv_y, active)
        kvs = [kv, kv_core, kv_y, swap_core(kv_y)]
        mixed, terms = attend_out(q, kvs, qpos, kpos, active, w_out)
        held, moving = tp_1(terms)
        kept.append((w_in, w_out, x, stats, na, nm, q, kvs, mixed, active, slope, terms))
        if l < LAYERS - 1:
            shard, _ = together(ins[l], kv_y)
            w_in = (gather_weights(shard), *IN_PANELS)
            held, moving = tp_2(held, together(*moving))
            shard, moving = together(outs[l], moving)
            (first, second), (firsts, seconds) = tp_3(held, moving)
            seconds, first = together(seconds, first)
            sums = tp_pieces(first, firsts, *tp_4(second, seconds))
            w_out = (gather_weights(shard), *OUT_PANELS)

    late, late_moving = held, moving
    small = [None] * LAYERS
    scattered = [None] * LAYERS
    g = None
    for l in reversed(range(LAYERS)):
        last = l == LAYERS - 1
        w_in, w_out, x, stats, na, nm, q, kvs, mixed, active, slope, terms = kept[l]
        if last:
            slope, _ = together(slope, terms)
            g, gm, gh, part = last_back_out(cotangent, row_at, w_out, slope)
            late_moving, gm = together(late_moving, gm)
            late, late_moving = tp_2(late, late_moving)
        else:
            after = kept[l + 1]
            g, gm, gh, part = next_back_out(g, after[2], after[3], sums, w_out, slope)
        dq, own, to_y, send = attend_back(q, kvs, gm, qpos, kpos)
        from_core = swap_core(send)
        out_far = weight_grad(g, pinned(mixed, active), far)
        if last:
            late_moving, out_far = together(late_moving, out_far)
        else:
            late_first, late_second = tp_3_sums(late, late_moving)
            late_seconds = [from_z(late_second, k) for k in (1, 3, 2)]
            late_seconds, out_far = together(late_seconds, out_far)
            late_near, late_far = tp_4(late_second, late_seconds)
            late_firsts = [from_z(late_first, k) for k in (1, 3, 2)]
        from_core, out_far = together(from_core, out_far)
        from_y = swap_y(add_late(to_y, from_core))
        out_got = swap_core(out_far)
        up_far = weight_grad(nm, pinned(gh), far)
        if last:
            out_got, up_far = together(out_got, up_far)
        else:
            out_got, up_far, late_far = together(out_got, up_far, late_far)
        out_near = weight_grad(g, pinned(mixed, active), near, out_got)
        up_got, out_near = together(swap_core(up_far), out_near)
        up_near = weight_grad(nm, pinned(gh), near, up_got)
        if last:
            from_y, out_near, up_near = together(from_y, out_near, up_near)
        else:
            out_after, up_after, qkv_after = scattered[l + 1]
            from_y, out_near, up_near, qkv_after = together(from_y, out_near, up_near, qkv_after)
            out_half, up_half = swap_half(out_after), swap_half(up_after)
        out_sum = scatter_weight_grad(out_near)
        gp, terms, small[l] = back_in(
            dq, own, from_core, from_y, tables, gh, w_in, x, stats, vec, l, part
        )
        if not last:
            late_firsts, out_half, up_half, gp = together(late_firsts, out_half, up_half, gp)
        held, moving = tp_1(terms)
        up_sum = scatter_weight_grad(up_near)
        qkv_far = weight_grad(na, (gp,), far)
        moving, qkv_far, out_sum = together(moving, qkv_far, out_sum)
        held, moving = tp_2(held, moving)
        qkv_got = swap_core(qkv_far)
        if last:
            moving, qkv_got = together(moving, qkv_got)
        else:
            total = jnp.stack(small)
            parts = around_ctx(total)
            moving, qkv_got, parts = together(moving, qkv_got, parts)
        first, second = tp_3_sums(held, moving)
        second, first, qkv_got = together(second, first, qkv_got)
        seconds = [from_z(second, k) for k in (1, 3, 2)]
        firsts = [from_z(first, k) for k in (1, 3, 2)]
        qkv_near = weight_grad(na, (gp,), near, qkv_got)
        qkv_sum = scatter_weight_grad(qkv_near)
        if last:
            seconds, qkv_near, up_sum = together(seconds, qkv_near, up_sum)
            sums = tp_pieces(first, firsts, *tp_4(second, seconds))
        else:
            total = pair_up(total, parts)
            parts = around(total, from_x)
            qkv_half, next_half = swap_half(qkv_after), swap_half(out_sum)
            seconds, qkv_near, parts, qkv_half, next_half = together(
                seconds, qkv_near, parts, qkv_half, next_half
            )
            halves = [[next_half], [out_half, up_half, qkv_half]]
            scattered[l + 1] = (out_after, up_after, qkv_after)
            sum_near, sum_far = tp_4(second, seconds)
            total = pair_up(total, parts)
            wide = total[:, :4]
            parts = around(wide, from_z)
            late_pieces = tp_pieces(late_first, late_firsts, late_near, late_far)
            activations = last_stream(tokens, row_at, kept[-1][2], late_pieces, vec, LAYERS - 1)
            sum_far, firsts, parts, activations = together(sum_far, firsts, parts, activations)
            halves[0] += [swap_half(up_sum), swap_half(qkv_sum)]
            wide = pair_up(wide, parts)
            wide = wide + swap_tp(wide, 4)
            sums = tp_pieces(first, firsts, sum_near, sum_far)
        scattered[l] = (out_sum, up_sum, qkv_sum)
    input_grad = last_grad(tokens, row_at, g, kept[0][2], kept[0][3], sums)
    input_grad, halves = together(input_grad, halves)
    qkv_grad, dense_grad, up_grad, down_grad = finish_weight_grads(
        [(*scattered[l], *halves[l]) for l in range(LAYERS)],
        [a.shape[2] for a in weights],
    )
    return (
        activations,
        input_grad,
        qkv_grad,
        total[:, 5, : qkv_bias.shape[1]],
        dense_grad,
        up_grad,
        total[:, 6, : up_bias.shape[1]],
        down_grad,
        wide[:, 0:2],
        wide[:, 2:4],
        total[:, 4],
    )


def solution(mesh):
    weight = P(None, ("fsdp", "ctx"), "tp")
    stream = P("fsdp", "ctx", None)
    bias = P(None, "tp")
    return jax.shard_map(
        body,
        mesh=mesh,
        in_specs=(
            stream,
            P(),
            stream,
            weight,
            bias,
            weight,
            weight,
            bias,
            weight,
            P(),
            P(),
            P(),
        ),
        out_specs=(
            stream,
            stream,
            weight,
            bias,
            weight,
            weight,
            bias,
            weight,
            P(),
            P(),
            P(),
        ),
        check_vma=False,
    )
```

```python
import jax
import jax.numpy as jnp
from jax import lax
from jax.experimental import pallas as pl
from jax.experimental.pallas import tpu as pltpu
from jax.sharding import PartitionSpec as P

HD = 256
ROT = 64
LAYERS = 2
EPSILON = 1e-05
LANES = 128
TILE = 256
CHUNK = 32
ALL_PANELS = (0, 3, 4, 8)
IN_PANELS, OUT_PANELS = (0, 3), (0, 1)
F32 = jnp.float32
BF16 = jnp.bfloat16
VMEM_LIMIT = 24 * 1024 * 1024


def swap_core(value):
    return lax.ppermute(value, "ctx", [(i, i ^ 1) for i in range(4)])


def swap_y(value):
    return lax.ppermute(value, "ctx", [(i, i ^ 2) for i in range(4)])


def from_x(value, k):
    return lax.ppermute(value, "fsdp", [((i + k) % 4, i) for i in range(4)])


def swap_both(value):
    return lax.ppermute(value, "ctx", [(i, i ^ 3) for i in range(4)])


def swap_tp(value, k):
    return lax.ppermute(value, "tp", [(i, i ^ k) for i in range(8)])


def from_z(value, k):
    return lax.ppermute(value, "tp", [((i & 4) + (i + k) % 4, i) for i in range(8)])


def to_z(value, k):
    return lax.ppermute(value, "tp", [(i, (i & 4) + (i + k) % 4) for i in range(8)])


def gather_weights(shard):
    return lax.all_gather(shard, ("fsdp", "ctx"), axis=1, tiled=True)


def together(*values):
    return lax.optimization_barrier(values)


def tp_1(pieces):
    firsts = [to_z(pieces[k], k) for k in (1, 3, 2)]
    return (pieces[0], pieces[4]), (firsts, swap_tp(pieces[5], 4))


def tp_2(kept, arrived):
    (own, near), (firsts, far) = kept, arrived
    first = add_up(own, *firsts)
    parts = add_split(near, far)
    seconds = [to_z(parts[k], k) for k in (1, 3, 2)]
    return (first, parts[0]), (swap_tp(first, 4), seconds)


def tp_3_sums(kept, arrived):
    (first, own), (other, seconds) = kept, arrived
    second = add_up(own, *seconds)
    return add_up(first, other), second


def tp_3(kept, arrived):
    first, second = tp_3_sums(kept, arrived)
    seconds = [from_z(second, k) for k in (1, 3, 2)]
    firsts = [from_z(first, k) for k in (1, 3, 2)]
    return (first, second), (firsts, seconds)


def tp_4(second, seconds):
    near = stack_up(second, seconds[0], seconds[2], seconds[1])
    return near, swap_tp(near, 4)


def tp_pieces(first, firsts, near, far):
    return (first, firsts[0], firsts[2], firsts[1], near, far)


def around(value, move):
    return [move(value, k) for k in (1, 2, 3)]


def around_ctx(value):
    return [swap_y(value), swap_core(value), swap_both(value)]


def pair_up(value, got):
    return (value + got[1]) + (got[0] + got[2])


def call(body, grid, ins, in_specs, outs, out_specs, scratch=(), prefetch=0, flops=0):
    nbytes = sum(a.size * a.dtype.itemsize for a in outs)
    nbytes += sum(min(a.size * a.dtype.itemsize, 1 << 22) for a in ins)
    return pl.pallas_call(
        body,
        grid_spec=pltpu.PrefetchScalarGridSpec(
            num_scalar_prefetch=prefetch,
            grid=grid,
            in_specs=in_specs,
            out_specs=out_specs,
            scratch_shapes=scratch,
        ),
        out_shape=outs,
        compiler_params=pltpu.CompilerParams(vmem_limit_bytes=VMEM_LIMIT),
        cost_estimate=pl.CostEstimate(
            flops=int(flops), bytes_accessed=int(nbytes), transcendentals=0
        ),
    )(*ins)


def call_once(body, ins, outs, scratch=(), prefetch=0, hbm=(), out_hbm=False, flops=0):
    ins = tuple(
        pltpu.with_memory_space_constraint(a, pltpu.HBM) if i in hbm else a
        for i, a in enumerate(ins)
    )
    specs = [
        pl.BlockSpec(memory_space=pltpu.HBM) if i in hbm else whole(a)
        for i, a in enumerate(ins)
        if i >= prefetch
    ]
    out_specs = [pl.BlockSpec(memory_space=pltpu.HBM) if out_hbm else whole(a) for a in outs]
    return call(body, (1,), ins, specs, outs, out_specs, scratch, prefetch, flops)


def pinned(*arrays):
    return tuple(pltpu.with_memory_space_constraint(a, pltpu.HBM) for a in arrays)


def shape(dims, dtype):
    return jax.ShapeDtypeStruct(dims, dtype)


def whole(a):
    return pl.BlockSpec(a.shape, lambda *_: (0,) * len(a.shape))


def dot_nn(a, b):
    return lax.dot_general(a, b, (((1,), (0,)), ((), ())), preferred_element_type=F32)


def dot_nt(a, b):
    return lax.dot_general(a, b, (((1,), (1,)), ((), ())), preferred_element_type=F32)


def dot_tn(a, b):
    return lax.dot_general(a, b, (((0,), (0,)), ((), ())), preferred_element_type=F32)


def fold_rows(a):
    return jnp.sum(a.reshape(a.shape[0] // 8, 8, a.shape[1]), axis=0)


def sum_rows(a):
    return jnp.sum(a, axis=0, keepdims=True)


def span(j, size):
    return pl.ds(pl.multiple_of(j * size, size), size)


def start(copies):
    for copy in copies:
        copy.start()


def wait(copies):
    for copy in copies:
        copy.wait()


def load_panels(w_ref, first, scratch, sems, at=0):
    return [
        pltpu.make_async_copy(w_ref.at[first + i], scratch.at[at + i], sems.at[at + i])
        for i in range(scratch.shape[0] - at)
    ]


def panels_scratch(n, width):
    return [pltpu.VMEM((n, width, TILE), BF16), pltpu.SemaphoreType.DMA((n,))]


class Tiles:
    def __init__(self, w_ref, runs, scratch, sems):
        self.w_ref, self.runs, self.scratch, self.sems = w_ref, runs, scratch, sems

    def copies(self, j):
        at = 0
        for i, (first, n) in enumerate(self.runs):
            yield pltpu.make_async_copy(
                self.w_ref.at[first : first + n, span(j, TILE), :],
                self.scratch.at[j, at : at + n],
                self.sems.at[i, j],
            )
            at += n

    def start(self):
        def step(j, carry):
            start(self.copies(j))
            return carry

        lax.fori_loop(0, self.scratch.shape[0], step, 0)

    def get(self, j):
        wait(self.copies(j))
        n = self.scratch.shape[1]
        return [self.scratch[j, i] for i in range(n)]


def tiles_scratch(runs, width):
    n = sum(size for _, size in runs)
    return [
        pltpu.VMEM((width // TILE, n, TILE, TILE), BF16),
        pltpu.SemaphoreType.DMA((len(runs), width // TILE)),
    ]


def row_copies(source, row_ref, target, sems, back=False):
    per = source.shape[1] // CHUNK

    def copy(k):
        far = source.at[k // per, span(row_ref[k], CHUNK)]
        own = target.at[span(k, CHUNK)]
        ends = (own, far) if back else (far, own)
        return pltpu.make_async_copy(*ends, sems.at[k])

    return copy


def for_chunks(n, step, carry=0):
    return lax.fori_loop(0, n, step, carry)


class Rows:
    def __init__(self, refs, scratch, sems):
        self.scratch, self.sems = scratch, sems
        self.parts, base = [], 0
        for ref in refs:
            self.parts.append((ref, base, ref.shape[0] // CHUNK))
            base += ref.shape[0] // CHUNK

    def copy(self, part, i):
        ref, base, _ = part
        return pltpu.make_async_copy(
            ref.at[span(i, CHUNK)], self.scratch.at[span(base + i, CHUNK)], self.sems.at[base + i]
        )


def start_rows(*rows):
    order = [(base + i, r, (ref, base, n), i) for r in rows for ref, base, n in r.parts for i in range(n)]
    for _, r, part, i in sorted(order, key=lambda entry: entry[0]):
        r.copy(part, i).start()


def for_rows(pieces, others, fn, carry=0):
    for part in pieces.parts:

        def step(i, carry, part=part):
            pieces.copy(part, i).wait()
            for other in others:
                other.copy(other.parts[0], part[1] + i).wait()
            at = span(part[1] + i, CHUNK)
            return fn(part[1] + i, pieces.scratch[at, :].astype(F32), carry)

        carry = lax.fori_loop(0, part[2], step, carry)
    return carry


def rows_scratch(rows, width, n=1):
    one = [pltpu.VMEM((rows, width), BF16), pltpu.SemaphoreType.DMA((rows // CHUNK,))]
    return one * n


def piece_shapes(rows, width):
    return [shape((rows // 8, width), BF16)] * 4 + [shape((rows // 4, width), BF16)] * 2


def put_pieces(at, y, refs):
    base = 0
    for ref in refs:
        ref[:, at] = y[base : base + ref.shape[0]].astype(BF16)
        base += ref.shape[0]


def put_norms(at, x, vec_ref, layer, stat_ref, na_ref, nm_ref):
    mean = jnp.mean(x, axis=1, keepdims=True)
    center = x - mean
    r = lax.rsqrt(jnp.mean(center * center, axis=1, keepdims=True) + EPSILON)
    u = center * r
    lane = lax.broadcasted_iota(jnp.int32, (x.shape[0], LANES), 1)
    stat_ref[at, :] = jnp.where(lane < LANES // 2, mean, r)
    na_ref[at, :] = (u * vec_ref[layer, 0:1] + vec_ref[layer, 2:3]).astype(BF16)
    nm_ref[at, :] = (u * vec_ref[layer, 1:2] + vec_ref[layer, 3:4]).astype(BF16)


def unit_of(x, stats):
    return (x.astype(F32) - stats[:, 0:1]) * stats[:, LANES // 2 : LANES // 2 + 1]


def put_qkv(na_ref, loads, w_ref, b_ref, t_ref, q_ref, kv_ref):
    for j in range(3):
        loads[j].wait()
        y = dot_nn(na_ref[...], w_ref[j]) + b_ref[:, j * HD : (j + 1) * HD]
        if j == 0:
            q_ref[...] = turn(y, t_ref, 1.0).astype(BF16)
        elif j == 1:
            kv_ref[:, :HD] = turn(y, t_ref, 1.0).astype(BF16)
        else:
            kv_ref[:, HD:] = y.astype(BF16)


def in_outs(rows, width):
    return [
        shape((rows, width), BF16),
        shape((rows, LANES), F32),
        shape((rows, width), BF16),
        shape((rows, width), BF16),
        shape((rows, HD), BF16),
        shape((rows, 2 * HD), BF16),
    ]


def first_in(tokens, row_at, vec, w, bias, tables):
    width = tokens.shape[2]
    rows = tokens.shape[0] * tokens.shape[1]

    def body(
        row_ref,
        tok_ref,
        vec_ref,
        w_ref,
        b_ref,
        t_ref,
        x_ref,
        stat_ref,
        na_ref,
        nm_ref,
        q_ref,
        kv_ref,
        panels,
        sems,
        row_sems,
    ):
        news = row_copies(tok_ref, row_ref, x_ref, row_sems)
        for k in range(rows // CHUNK):
            news(k).start()
        loads = load_panels(w_ref, w[1], panels, sems)
        start(loads)

        def step(i, carry):
            news(i).wait()
            at = span(i, CHUNK)
            put_norms(at, x_ref[at, :].astype(F32), vec_ref, 0, stat_ref, na_ref, nm_ref)
            return carry

        for_chunks(rows // CHUNK, step)
        put_qkv(na_ref, loads, panels, b_ref, t_ref, q_ref, kv_ref)

    return call_once(
        body,
        (row_at, tokens, vec, w[0], bias, tables),
        in_outs(rows, width),
        panels_scratch(3, width) + [pltpu.SemaphoreType.DMA((rows // CHUNK,))],
        prefetch=1,
        hbm=(1, 3),
        flops=2 * rows * width * 3 * HD,
    )


def next_in(x, pieces, layer, vec, w, bias, tables):
    rows, width = x.shape

    def body(x_ref, *rest):
        refs = rest[:6]
        vec_ref, w_ref, b_ref, t_ref, new_ref, stat_ref, na_ref, nm_ref = rest[6:14]
        q_ref, kv_ref, panels, sems, xs, x_sems, ps, p_sems = rest[14:]
        xs, ps = Rows([x_ref], xs, x_sems), Rows(refs, ps, p_sems)
        start_rows(xs, ps)
        loads = load_panels(w_ref, w[1], panels, sems)
        start(loads)

        def step(i, branch, carry):
            at = span(i, CHUNK)
            new = xs.scratch[at, :].astype(F32) + branch + vec_ref[layer - 1, 4:5]
            new_ref[at, :] = new.astype(BF16)
            put_norms(at, new, vec_ref, layer, stat_ref, na_ref, nm_ref)
            return carry

        for_rows(ps, [xs], step)
        put_qkv(na_ref, loads, panels, b_ref, t_ref, q_ref, kv_ref)

    return call_once(
        body,
        (x, *pieces, vec, w[0], bias, tables),
        in_outs(rows, width),
        panels_scratch(3, width) + rows_scratch(rows, width, 2),
        hbm=(0, 1, 2, 3, 4, 5, 6, 8),
        flops=2 * rows * width * 3 * HD,
    )


def gelu_parts(h):
    e = jnp.exp(-0.5 * h * h)
    t = 1.0 / (1.0 + (0.3275911 * 0.5**0.5) * jnp.abs(h))
    tail = 1.061405429 * t - 1.453152027
    tail = tail * t + 1.421413741
    tail = tail * t - 0.284496736
    tail = (tail * t + 0.254829592) * t * (0.5 * e)
    return jnp.where(h >= 0, 1.0 - tail, tail), e * 0.3989422804014327


def project_up(nm, w, bias):
    rows, width = nm.shape
    hidden = bias.shape[1]

    def body(n_ref, w_ref, b_ref, act_ref, slope_ref, panels, sems):
        loads = load_panels(w_ref, w[2], panels, sems)
        start(loads)
        for j in range(hidden // TILE):
            at = slice(j * TILE, (j + 1) * TILE)
            loads[j].wait()
            h = dot_nn(n_ref[...], panels[j]) + b_ref[:, at]
            cdf, density = gelu_parts(h)
            act_ref[:, at] = (h * cdf).astype(BF16)
            slope_ref[:, at] = (cdf + h * density).astype(BF16)

    return call_once(
        body,
        (nm, w[0], bias),
        [shape((rows, hidden), BF16), shape((rows, hidden), BF16)],
        panels_scratch(hidden // TILE, width),
        hbm=(1,),
        flops=2 * rows * width * hidden,
    )


def weights_of(q, kvs, qpos, kpos):
    scores = [dot_nt(q, kv[:, :HD]) * HD**-0.5 for kv in kvs]
    scores = jnp.concatenate(scores, axis=1)
    scores = jnp.where(kpos <= qpos, scores, -1e30)
    e = jnp.exp(scores - jnp.max(scores, axis=1, keepdims=True))
    return e / jnp.sum(e, axis=1, keepdims=True)


def attend_out(q, kvs, qpos, kpos, active, w):
    rows, hidden = active.shape
    width = w[0].shape[1]
    seqs = kpos.shape[0]
    per = rows // seqs
    runs = [(w[1], 1), (w[2], hidden // TILE)]

    def body(q_ref, k0, k1, k2, k3, qp_ref, kp_ref, act_ref, w_ref, mixed_ref, *rest):
        refs = rest[:6]
        wide, sems, left = rest[6:]
        tiles = Tiles(w_ref, runs, wide, sems)
        tiles.start()
        for s in range(seqs):
            at = slice(s * per, (s + 1) * per)
            kvs = [ref[at] for ref in (k0, k1, k2, k3)]
            p = weights_of(q_ref[at], kvs, qp_ref[at], kp_ref[s : s + 1]).astype(BF16)
            mixed = sum(dot_nn(p[:, i * per : (i + 1) * per], kvs[i][:, HD:]) for i in range(4))
            mixed_ref[at] = mixed.astype(BF16)
        left[:, :HD] = mixed_ref[...]
        left[:, HD:] = act_ref[...]

        def step(j, carry):
            y = dot_nt(left[...], jnp.concatenate(tiles.get(j), axis=1))
            put_pieces(span(j, TILE), y, refs)
            return carry

        lax.fori_loop(0, width // TILE, step, 0)

    out = call_once(
        body,
        (q, *kvs, qpos, kpos, active, w[0]),
        [shape((rows, HD), BF16)] + piece_shapes(rows, width),
        tiles_scratch(runs, width) + [pltpu.VMEM((rows, HD + hidden), BF16)],
        hbm=(8,),
        flops=16 * rows * per * HD + 2 * rows * width * (HD + hidden),
    )
    return out[0], out[1:]


def put_back_out(gb_ref, loads, panels, slope_ref, gm_ref, gh_ref, part_ref):
    for j in range(panels.shape[0]):
        loads[j].wait()
        y = dot_nn(gb_ref[...], panels[j])
        if j == 0:
            gm_ref[...] = y.astype(BF16)
        else:
            at = slice((j - 1) * TILE, j * TILE)
            gh = (y * slope_ref[:, at].astype(F32)).astype(BF16)
            gh_ref[:, at] = gh
            part_ref[6:7, at] = sum_rows(gh.astype(F32))


def load_back_out(w_ref, w, panels, sems):
    first = pltpu.make_async_copy(w_ref.at[w[1]], panels.at[0], sems.at[0])
    return [first] + load_panels(w_ref, w[2], panels, sems, at=1)


def back_out_shapes(rows, width, hidden):
    return [
        shape((rows, width), BF16),
        shape((rows, HD), BF16),
        shape((rows, hidden), BF16),
        shape((8, width), F32),
    ]


def last_back_out(cotangent, row_at, w, slope):
    width = cotangent.shape[2]
    rows, hidden = slope.shape
    n = 1 + hidden // TILE

    def body(
        row_ref, cot_ref, w_ref, slope_ref, gb_ref, gm_ref, gh_ref, part_ref, panels, sems, row_sems
    ):
        news = row_copies(cot_ref, row_ref, gb_ref, row_sems)
        for k in range(rows // CHUNK):
            news(k).start()
        loads = load_back_out(w_ref, w, panels, sems)
        start(loads)
        part_ref[...] = jnp.zeros_like(part_ref)

        def step(i, total):
            news(i).wait()
            return total + fold_rows(gb_ref[span(i, CHUNK), :].astype(F32))

        total = for_chunks(rows // CHUNK, step, jnp.zeros((8, width), F32))
        part_ref[4:5, :] = sum_rows(total)
        put_back_out(gb_ref, loads, panels, slope_ref, gm_ref, gh_ref, part_ref)

    return call_once(
        body,
        (row_at, cotangent, w[0], *pinned(slope)),
        back_out_shapes(rows, width, hidden),
        panels_scratch(n, width) + [pltpu.SemaphoreType.DMA((rows // CHUNK,))],
        prefetch=1,
        hbm=(1, 2),
        flops=2 * rows * width * n * TILE,
    )


def grad_in(g, x, stats, total):
    u = unit_of(x, stats)
    back = total - jnp.mean(total, axis=1, keepdims=True)
    back = back - u * jnp.mean(total * u, axis=1, keepdims=True)
    return g.astype(F32) + stats[:, LANES // 2 : LANES // 2 + 1] * back


def next_back_out(g, x, stats, pieces, w, slope):
    rows, width = g.shape
    hidden = slope.shape[1]
    n = 1 + hidden // TILE

    def body(g_ref, x_ref, stat_ref, *rest):
        refs = rest[:6]
        w_ref, slope_ref, gb_ref, gm_ref, gh_ref, part_ref, panels, sems = rest[6:14]
        gs, xs, ps = (
            Rows(r, rest[14 + 2 * i], rest[15 + 2 * i])
            for i, r in enumerate(([g_ref], [x_ref], refs))
        )
        start_rows(gs, xs, ps)
        loads = load_back_out(w_ref, w, panels, sems)
        start(loads)
        part_ref[...] = jnp.zeros_like(part_ref)

        def step(i, branch, total):
            at = span(i, CHUNK)
            new = grad_in(gs.scratch[at, :], xs.scratch[at, :], stat_ref[at, :], branch)
            gb_ref[at, :] = new.astype(BF16)
            return total + fold_rows(new)

        total = for_rows(ps, [gs, xs], step, jnp.zeros((8, width), F32))
        part_ref[4:5, :] = sum_rows(total)
        put_back_out(gb_ref, loads, panels, slope_ref, gm_ref, gh_ref, part_ref)

    return call_once(
        body,
        (g, x, stats, *pieces, w[0], *pinned(slope)),
        back_out_shapes(rows, width, hidden),
        panels_scratch(n, width) + rows_scratch(rows, width, 3),
        hbm=(0, 1, 3, 4, 5, 6, 7, 8, 9),
        flops=2 * rows * width * n * TILE,
    )


def attend_back(q, kvs, gm, qpos, kpos):
    rows = q.shape[0]
    seqs = kpos.shape[0]
    per = rows // seqs

    def body(q_ref, k0, k1, k2, k3, gm_ref, qp_ref, kp_ref, dq_ref, own_ref, y_ref, send_ref):
        part = [slice(i * per, (i + 1) * per) for i in range(4)]
        for s in range(seqs):
            at = part[s]
            kvs = [ref[at] for ref in (k0, k1, k2, k3)]
            q = q_ref[at]
            gm = gm_ref[at]
            p = weights_of(q, kvs, qp_ref[at], kp_ref[s : s + 1])
            dp = jnp.concatenate([dot_nt(gm, kv[:, HD:]) for kv in kvs], axis=1)
            ds = (p * (dp - jnp.sum(p * dp, axis=1, keepdims=True))).astype(BF16)
            p = p.astype(BF16)
            dq = sum(dot_nn(ds[:, part[i]], kvs[i][:, :HD]) for i in range(4))
            dq_ref[at] = dq * HD**-0.5
            late = slice(rows + s * per, rows + (s + 1) * per)
            places = (own_ref.at[at], send_ref.at[at], y_ref.at[at], send_ref.at[late])
            for i, ref in enumerate(places):
                ref[:, :HD] = (dot_tn(ds[:, part[i]], q) * HD**-0.5).astype(ref.dtype)
                ref[:, HD:] = dot_tn(p[:, part[i]], gm).astype(ref.dtype)

    return call_once(
        body,
        (q, *pinned(*kvs), gm, qpos, kpos),
        [
            shape((rows, HD), F32),
            shape((rows, 2 * HD), F32),
            shape((rows, 2 * HD), F32),
            shape((2 * rows, 2 * HD), BF16),
        ],
        flops=40 * rows * per * HD,
    )


def back_in(dq, own, from_core, from_y, tables, gh, w, x, stats, vec, layer, part):
    rows, hidden = gh.shape
    width = w[0].shape[1]
    runs = [(w[1], 3), (w[2], hidden // TILE)]

    def body(
        dq_ref,
        own_ref,
        core_ref,
        y_ref,
        t_ref,
        gh_ref,
        w_ref,
        x_ref,
        stat_ref,
        vec_ref,
        part_ref,
        gp_ref,
        *rest,
    ):
        refs = rest[:6]
        sum_ref, wide, sems, xs, x_sems = rest[6:]
        tiles = Tiles(w_ref, runs, wide, sems)

        def x_copy(j):
            at = span(j, TILE)
            return pltpu.make_async_copy(x_ref.at[:, at], xs.at[j], x_sems.at[j])

        def begin(j, carry):
            start(tiles.copies(j))
            x_copy(j).start()
            return carry

        lax.fori_loop(0, width // TILE, begin, 0)
        both = own_ref[...] + core_ref[:rows].astype(F32) + y_ref[...].astype(F32)
        parts = (turn(dq_ref[...], t_ref, -1.0), turn(both[:, :HD], t_ref, -1.0), both[:, HD:])
        sum_ref[...] = part_ref[...]
        for i, a in enumerate(parts):
            a = a.astype(BF16)
            at = slice(i * HD, (i + 1) * HD)
            gp_ref[:, at] = a
            sum_ref[5:6, at] = sum_rows(a.astype(F32))

        def step(j, carry):
            at = span(j, TILE)
            w_tile = tiles.get(j)
            gna = dot_nt(gp_ref[...], jnp.concatenate(w_tile[:3], axis=1))
            gnm = dot_nt(gh_ref[...], jnp.concatenate(w_tile[3:], axis=1))
            x_copy(j).wait()
            u = unit_of(xs[j], stat_ref[...])
            y = gna * vec_ref[layer, 0:1, at] + gnm * vec_ref[layer, 1:2, at]
            put_pieces(at, y, refs)
            for i, a in enumerate((gna * u, gnm * u, gna, gnm)):
                sum_ref[i : i + 1, at] = sum_rows(a)
            return carry

        lax.fori_loop(0, width // TILE, step, 0)

    out = call_once(
        body,
        (*pinned(dq, own, from_core), from_y, tables, *pinned(gh), w[0], x, stats, vec, part),
        [shape((rows, 3 * HD), BF16)] + piece_shapes(rows, width) + [shape((8, width), F32)],
        tiles_scratch(runs, width)
        + [pltpu.VMEM((width // TILE, rows, TILE), BF16), pltpu.SemaphoreType.DMA((width // TILE,))],
        hbm=(6, 7),
        flops=2 * rows * width * (3 * HD + hidden),
    )
    return out[0], out[1:7], out[7]


def put_rows(like, row_at, rows_in, pieces, others, value):
    seqs, per, width = like.shape
    rows = seqs * per
    n = len(rows_in)

    def body(row_ref, *rest):
        refs = rest[: n + 6 + len(others)]
        out_ref, own, sems = rest[len(refs) : len(refs) + 3]
        rest = rest[len(refs) + 3 :]
        loads = [Rows([refs[i]], rest[2 * i], rest[2 * i + 1]) for i in range(n)]
        ps = Rows(refs[n : n + 6], rest[2 * n], rest[2 * n + 1])
        start_rows(*loads, ps)
        copies = row_copies(out_ref, row_ref, own, sems, back=True)

        def step(i, branch, carry):
            at = span(i, CHUNK)
            chunks = [load.scratch[at, :] for load in loads]
            own[at, :] = value(chunks, branch, at, refs[n + 6 :])
            copies(i).start()
            return carry

        for_rows(ps, loads, step)

        def finish(i, carry):
            copies(i).wait()
            return carry

        for_chunks(rows // CHUNK, finish)

    return call_once(
        body,
        (row_at, *rows_in, *pieces, *others),
        [shape((seqs, per, width), F32)],
        [pltpu.VMEM((rows, width), F32), pltpu.SemaphoreType.DMA((rows // CHUNK,))]
        + rows_scratch(rows, width, n + 1),
        prefetch=1,
        hbm=tuple(range(1, n + 7)),
        out_hbm=True,
    )[0]


def last_stream(like, row_at, x, pieces, vec, layer):
    def value(chunks, branch, at, others):
        return chunks[0].astype(F32) + branch + others[0][layer, 4:5]

    return put_rows(like, row_at, (x,), pieces, (vec,), value)


def last_grad(like, row_at, g, x, stats, pieces):
    def value(chunks, branch, at, others):
        return grad_in(chunks[0], chunks[1], others[0][at, :], branch)

    return put_rows(like, row_at, (g, x), pieces, (stats,), value)


def pack_panels(layer, *parts):
    depth = parts[0].shape[1]
    panels = [(i, c) for i, a in enumerate(parts) for c in range(a.shape[2] // TILE)]

    def body(*refs):
        out_ref, sems = refs[-2:]
        copies = [
            pltpu.make_async_copy(
                refs[i].at[layer, :, c * TILE : (c + 1) * TILE], out_ref.at[p], sems.at[p]
            )
            for p, (i, c) in enumerate(panels)
        ]
        start(copies)
        wait(copies)

    return call_once(
        body,
        parts,
        [shape((len(panels), depth, TILE), BF16)],
        [pltpu.SemaphoreType.DMA((len(panels),))],
        hbm=tuple(range(len(parts))),
    )[0]


def turn(x, tables, sign):
    head = x[:, :LANES]
    half = ROT // 2
    up = pltpu.roll(head, LANES - half, 1)
    down = pltpu.roll(head, half, 1)
    head = head * tables[0] + sign * (down * tables[2] - up * tables[1])
    return jnp.concatenate([head, x[:, LANES:]], axis=1)


def add_up(*parts):
    def body(*refs):
        total = refs[0][...].astype(F32)
        for ref in refs[1:-1]:
            total = total + ref[...].astype(F32)
        refs[-1][...] = total.astype(BF16)

    return call_once(body, parts, [shape(parts[0].shape, BF16)])[0]


def add_split(a, b):
    rows, width = a.shape
    n = rows // 4

    def body(a_ref, b_ref, *outs):
        for i, ref in enumerate(outs):
            at = slice(i * n, (i + 1) * n)
            ref[...] = (a_ref[at].astype(F32) + b_ref[at].astype(F32)).astype(BF16)

    return call_once(body, (a, b), [shape((n, width), BF16)] * 4)


def stack_up(*parts):
    n, width = parts[0].shape

    def body(*refs):
        for i, ref in enumerate(refs[:-1]):
            refs[-1][i * n : (i + 1) * n] = ref[...]

    return call_once(body, parts, [shape((n * len(parts), width), BF16)])[0]


def add_late(a, b):
    rows = a.shape[0]

    def body(a_ref, b_ref, out_ref):
        out_ref[...] = (a_ref[...] + b_ref[...].astype(F32)).astype(BF16)

    return call(
        body,
        (1,),
        (a, b),
        [whole(a), pl.BlockSpec((rows, b.shape[1]), lambda *_: (b.shape[0] // rows - 1, 0))],
        [shape(a.shape, BF16)],
        [whole(a)],
    )[0]


def weight_grad(x, ys, blocks, got=None):
    rows, width = x.shape
    cols = [a.shape[1] for a in ys]
    total = sum(cols)
    size = width // 16
    tiles = blocks.shape[0] // 2

    def body(block_ref, x_ref, *rest):
        y_refs = rest[: len(ys)]
        out_ref, xs, sems = rest[-3:]
        j = pl.program_id(0)

        def copy(i):
            at = pl.multiple_of(block_ref[i] * size, size)
            return pltpu.make_async_copy(x_ref.at[:, pl.ds(at, size)], xs.at[i], sems.at[i])

        @pl.when(j == 0)
        def _():
            for i in range(2 * tiles):
                copy(i).start()

        copy(2 * j).wait()
        copy(2 * j + 1).wait()
        left = jnp.concatenate([xs[2 * j], xs[2 * j + 1]], axis=1)
        at = 0
        for ref, n in zip(y_refs, cols):
            y = dot_tn(left, ref[...])
            if got is not None:
                y = y + rest[len(ys)][:, at : at + n].astype(F32)
            out_ref[:, at : at + n] = y.astype(BF16)
            at += n

    ins = (blocks, *pinned(x), *ys)
    specs = [pl.BlockSpec(memory_space=pltpu.HBM)] + [whole(a) for a in ys]
    if got is not None:
        ins += (got,)
        specs += [pl.BlockSpec((2 * size, total), lambda j, *_: (j, 0))]
    return call(
        body,
        (tiles,),
        ins,
        specs,
        [shape((width // 2, total), BF16)],
        [pl.BlockSpec((2 * size, total), lambda j, *_: (j, 0))],
        scratch=[pltpu.VMEM((2 * tiles, rows, size), BF16), pltpu.SemaphoreType.DMA((2 * tiles,))],
        prefetch=1,
        flops=2 * rows * (width // 2) * total,
    )[0]


def scatter_weight_grad(value):
    return lax.psum_scatter(value, "fsdp", scatter_dimension=0, tiled=True)


def swap_half(value):
    return swap_y(value[value.shape[0] // 2 :])


def finish_weight_grads(layers, cols):
    flat = [a for layer in layers for a in layer]
    depth = layers[0][0].shape[0] // 2
    outs = [shape((len(layers), depth, n), F32) for n in cols]

    def body(*refs):
        qkv_ref, dense_ref, up_ref, down_ref = refs[len(flat) :]
        for l in range(len(layers)):
            ins = refs[6 * l : 6 * l + 6]
            out, up, qkv = (
                ins[i][:depth].astype(F32) + ins[3 + i][...].astype(F32) for i in range(3)
            )
            qkv_ref[l] = qkv
            dense_ref[l] = out[:, :HD]
            up_ref[l] = up
            down_ref[l] = out[:, HD:]

    return call_once(body, pinned(*flat), outs)


def body(
    tokens,
    block_order,
    cotangent,
    qkv_weight,
    qkv_bias,
    dense_weight,
    up_weight,
    up_bias,
    down_weight,
    norm_gains,
    norm_shifts,
    out_bias,
):
    seqs, per, width = tokens.shape
    block = 128
    c, t = lax.axis_index("ctx"), lax.axis_index("tp")
    y_hi, z = t // 4, t % 4

    b = jnp.arange(8, dtype=jnp.int32)
    near = (b // 2) * 4 + (c ^ (2 * (b % 2)))
    far = near ^ 1
    row_at = jnp.concatenate(
        [2 * ((z + b // 2) % 4) + b % 2, (y_hi ^ (b // 4)) * 4 + (z + b) % 4]
    )

    row = row_at[:, None] * CHUNK + jnp.arange(CHUNK, dtype=jnp.int32)[None, :]
    row = row.reshape(seqs, per)
    slots = jnp.arange(block_order.shape[0], dtype=jnp.int32)

    def positions(owner):
        slot = 2 * owner + row // block
        here = slot[:, :, None] == slots
        return jnp.sum(jnp.where(here, block_order, 0), axis=2) * block + row % block

    qpos = positions(c).reshape(seqs * per, 1)
    kpos = jnp.concatenate([positions(c ^ i) for i in range(4)], axis=1)
    inverse = 10000.0 ** (-(jnp.arange(ROT // 2, dtype=F32) * 2.0) / ROT)
    angles = qpos.astype(F32) * inverse[None, :]
    cosine, sine = jnp.cos(angles), jnp.sin(angles)
    none = jnp.zeros_like(sine)
    rest = jnp.zeros((seqs * per, LANES - ROT), F32)
    tables = jnp.stack(
        [
            jnp.concatenate([cosine, cosine, rest + 1.0], axis=1),
            jnp.concatenate([sine, none, rest], axis=1),
            jnp.concatenate([none, sine, rest], axis=1),
        ]
    )

    vec = jnp.concatenate(
        [
            norm_gains,
            norm_shifts,
            out_bias[:, None],
            jnp.zeros((LAYERS, 3, width), BF16),
        ],
        axis=1,
    ).astype(F32)
    weights = (qkv_weight, dense_weight, up_weight, down_weight)
    qkv_b = qkv_bias.astype(F32)
    up_b = up_bias.astype(F32)

    kept = []
    rows = seqs * per
    ins = [pack_panels(l, qkv_weight, up_weight) for l in range(1, LAYERS)]
    outs = [pack_panels(l, dense_weight, down_weight) for l in range(1, LAYERS)]
    w = gather_weights(pack_panels(0, *weights))
    w, ins, outs, vec, tables, qpos, kpos, near, far = together(
        w, ins, outs, vec, tables, qpos, kpos, near, far
    )
    w_in, w_out = (w, ALL_PANELS[0], ALL_PANELS[2]), (w, ALL_PANELS[1], ALL_PANELS[3])
    sums = None
    for l in range(LAYERS):
        bias = qkv_b[l : l + 1]
        if l == 0:
            new = first_in(tokens, row_at, vec, w_in, bias, tables)
        else:
            new = next_in(kept[-1][2], sums, l, vec, w_in, bias, tables)
        x, stats, na, nm, q, kv = new
        kv_y, kv_core = swap_y(kv), swap_core(kv)
        active, slope = project_up(nm, w_in, up_b[l : l + 1])
        kv_y, active = together(kv_y, active)
        kvs = [kv, kv_core, kv_y, swap_core(kv_y)]
        mixed, terms = attend_out(q, kvs, qpos, kpos, active, w_out)
        held, moving = tp_1(terms)
        kept.append((w_in, w_out, x, stats, na, nm, q, kvs, mixed, active, slope, terms))
        if l < LAYERS - 1:
            shard, _ = together(ins[l], kv_y)
            w_in = (gather_weights(shard), *IN_PANELS)
            held, moving = tp_2(held, together(*moving))
            shard, moving = together(outs[l], moving)
            (first, second), (firsts, seconds) = tp_3(held, moving)
            seconds, first = together(seconds, first)
            sums = tp_pieces(first, firsts, *tp_4(second, seconds))
            w_out = (gather_weights(shard), *OUT_PANELS)

    late, late_moving = held, moving
    small = [None] * LAYERS
    scattered = [None] * LAYERS
    g = None
    for l in reversed(range(LAYERS)):
        last = l == LAYERS - 1
        w_in, w_out, x, stats, na, nm, q, kvs, mixed, active, slope, terms = kept[l]
        if last:
            slope, _ = together(slope, terms)
            g, gm, gh, part = last_back_out(cotangent, row_at, w_out, slope)
            late_moving, gm = together(late_moving, gm)
            late, late_moving = tp_2(late, late_moving)
        else:
            after = kept[l + 1]
            g, gm, gh, part = next_back_out(g, after[2], after[3], sums, w_out, slope)
            out_after, up_after, qkv_after = scattered[l + 1]
            up_half, gm = together(swap_half(up_after), gm)
        dq, own, to_y, send = attend_back(q, kvs, gm, qpos, kpos)
        from_core = swap_core(send)
        out_far = weight_grad(g, pinned(mixed, active), far)
        if last:
            late_moving, out_far = together(late_moving, out_far)
        else:
            late_first, late_second = tp_3_sums(late, late_moving)
            late_seconds = [from_z(late_second, k) for k in (1, 3, 2)]
            late_seconds, out_far = together(late_seconds, out_far)
            late_near, late_far = tp_4(late_second, late_seconds)
            late_firsts = [from_z(late_first, k) for k in (1, 3, 2)]
        from_core, out_far = together(from_core, out_far)
        from_y = swap_y(add_late(to_y, from_core))
        out_got = swap_core(out_far)
        up_far = weight_grad(nm, pinned(gh), far)
        out_got, up_far = together(out_got, up_far)
        out_near = weight_grad(g, pinned(mixed, active), near, out_got)
        up_got, out_near = together(swap_core(up_far), out_near)
        up_near = weight_grad(nm, pinned(gh), near, up_got)
        if last:
            from_y, out_near, up_near = together(from_y, out_near, up_near)
        else:
            from_y, out_near, up_near, qkv_after = together(from_y, out_near, up_near, qkv_after)
        out_sum = scatter_weight_grad(out_near)
        gp, terms, small[l] = back_in(
            dq, own, from_core, from_y, tables, gh, w_in, x, stats, vec, l, part
        )
        if not last:
            late_firsts, late_far, gp = together(late_firsts, late_far, gp)
        held, moving = tp_1(terms)
        up_sum = scatter_weight_grad(up_near)
        qkv_far = weight_grad(na, (gp,), far)
        moving, qkv_far, out_sum = together(moving, qkv_far, out_sum)
        held, moving = tp_2(held, moving)
        qkv_got = swap_core(qkv_far)
        if last:
            moving, qkv_got = together(moving, qkv_got)
        else:
            total = jnp.stack(small)
            parts = around_ctx(total)
            moving, qkv_got, parts = together(moving, qkv_got, parts)
        first, second = tp_3_sums(held, moving)
        second, first, qkv_got = together(second, first, qkv_got)
        seconds = [from_z(second, k) for k in (1, 3, 2)]
        firsts = [from_z(first, k) for k in (1, 3, 2)]
        qkv_near = weight_grad(na, (gp,), near, qkv_got)
        qkv_sum = scatter_weight_grad(qkv_near)
        if last:
            out_half = swap_half(out_sum)
            seconds, qkv_near, up_sum, out_half = together(seconds, qkv_near, up_sum, out_half)
            sums = tp_pieces(first, firsts, *tp_4(second, seconds))
        else:
            total = pair_up(total, parts)
            parts = around(total, from_x)
            qkv_half, next_half = swap_half(qkv_after), swap_half(out_sum)
            seconds, qkv_near, parts, qkv_half, next_half = together(
                seconds, qkv_near, parts, qkv_half, next_half
            )
            halves = [[next_half], [out_half, up_half, qkv_half]]
            scattered[l + 1] = (out_after, up_after, qkv_after)
            sum_near, sum_far = tp_4(second, seconds)
            total = pair_up(total, parts)
            wide = total[:, :4]
            parts = around(wide, from_z)
            late_pieces = tp_pieces(late_first, late_firsts, late_near, late_far)
            activations = last_stream(tokens, row_at, kept[-1][2], late_pieces, vec, LAYERS - 1)
            last_halves = [swap_half(up_sum), swap_half(qkv_sum)]
            sum_far, firsts, parts, activations, last_halves = together(
                sum_far, firsts, parts, activations, last_halves
            )
            halves[0] += last_halves
            wide = pair_up(wide, parts)
            wide = wide + swap_tp(wide, 4)
            sums = tp_pieces(first, firsts, sum_near, sum_far)
        scattered[l] = (out_sum, up_sum, qkv_sum)
    input_grad = last_grad(tokens, row_at, g, kept[0][2], kept[0][3], sums)
    input_grad, halves = together(input_grad, halves)
    qkv_grad, dense_grad, up_grad, down_grad = finish_weight_grads(
        [(*scattered[l], *halves[l]) for l in range(LAYERS)],
        [a.shape[2] for a in weights],
    )
    return (
        activations,
        input_grad,
        qkv_grad,
        total[:, 5, : qkv_bias.shape[1]],
        dense_grad,
        up_grad,
        total[:, 6, : up_bias.shape[1]],
        down_grad,
        wide[:, 0:2],
        wide[:, 2:4],
        total[:, 4],
    )


def solution(mesh):
    weight = P(None, ("fsdp", "ctx"), "tp")
    stream = P("fsdp", "ctx", None)
    bias = P(None, "tp")
    return jax.shard_map(
        body,
        mesh=mesh,
        in_specs=(
            stream,
            P(),
            stream,
            weight,
            bias,
            weight,
            weight,
            bias,
            weight,
            P(),
            P(),
            P(),
        ),
        out_specs=(
            stream,
            stream,
            weight,
            bias,
            weight,
            weight,
            bias,
            weight,
            P(),
            P(),
            P(),
        ),
        check_vma=False,
    )
```
